128 devices in a mesh: section: 2 (over core), space: 64 (over z, y, x).
Axes of the slice: x: 4, y: 4, z: 4, core: 2. Of those that a mesh axis runs over, the one named last changes fastest.
Arguments:
- volume: bfloat16 [4, 32, 256, 8, 512], P(None, None, 'space'), may hold values from -6 to 6
- labels: int32 [4, 64, 2, 128], P(None, 'space'), may hold values from 0 to 3
- down_weight_two: bfloat16 [64, 32, 2, 2, 2], replicated, may hold values from -0.5 to 0.5
- w_conv_two: bfloat16 [64, 64, 3, 3, 3], replicated, may hold values from -0.21875 to 0.21875
- down_weight_three: bfloat16 [128, 64, 2, 2, 2], replicated, may hold values from -0.375 to 0.375
- w_conv_three: bfloat16 [128, 128, 3, 3, 3], replicated, may hold values from -0.15625 to 0.15625
- w_head: bfloat16 [128, 4], replicated, may hold values from -1.5 to 1.5
Outputs:
- grad_down_two: float32 [16384], P(('section', 'space'))
- grad_conv_two: float32 [110592], P(('section', 'space'))
- grad_down_three: float32 [65536], P(('section', 'space'))
- grad_conv_three: float32 [442368], P(('section', 'space'))
- grad_head: float32 [512], P(('section', 'space'))
The draws below stay inside these ranges and needn't reach their ends.
All inputs are finite; a program needn't handle non-finite values.
Results may differ from the reference program's by a relative error of at most 0.017.
Values may be sent and summed in bfloat16 or wider, within the bound.
No kernel may reach another device: no remote copies, remote signals or barrier semaphores. Data moves between devices by JAX's collectives and lax.ppermute only.
A program may use at most 320 MiB of HBM per device.

```python
import math
import jax
import jax.numpy as jnp
from jax import lax

C1 = 32
C2 = 64
C3 = 128
NCLS = 4
MB = 4
H1 = 8
W1 = 512
D1 = 256
D3 = 64
H3 = 2
W3 = 128


def place_ends(values, rng, least, largest):
    extent = values.shape
    spot = [jax.random.randint(jax.random.fold_in(rng, axis), (), 0, extent[axis]) for axis in range(len(extent))]
    values = values.at[tuple(spot)].set(least)
    longest = extent.index(max(extent))
    spot[longest] = (spot[longest] + 1) % extent[longest]
    return values.at[tuple(spot)].set(largest)


def shard_levels(rng, extent, cuts, low, high):
    gain = 1.0
    for axis_at, blocks in cuts:
        draws = jax.random.uniform(jax.random.fold_in(jax.random.fold_in(rng, 6), axis_at), (blocks,), jnp.float32, low / len(cuts), high / len(cuts))
        gain = gain * jnp.repeat(jnp.exp(draws), extent[axis_at] // blocks).reshape((-1,) + (1,) * (len(extent) - 1 - axis_at))
    return gain


def noise(own_key, shape, spread, reach, pieces=(), held_as=jnp.bfloat16):
    factor_of = shard_levels(own_key, shape, pieces, -0.22, 0.18) if pieces else 1.0
    result = jax.random.normal(own_key, shape, jnp.float32) * spread * factor_of
    return jnp.minimum(jnp.maximum(result, -reach), reach).astype(held_as)


def setup_inputs(seed: int = 0) -> dict:
    keys = jax.random.split(jax.random.key(seed), 8)
    volume = noise(keys[0], (MB, C1, D1, H1, W1), 1.0, 6.0, ((2, 64),))
    labels = place_ends(jax.random.randint(keys[1], (MB, D3, H3, W3), 0, NCLS), jax.random.fold_in(keys[1], 1), 0, NCLS - 1).astype(jnp.int32)
    down_weight_two = noise(keys[2], (C2, C1, 2, 2, 2), (4 * C1) ** -0.5, 0.5)
    w_conv_two = noise(keys[3], (C2, C2, 3, 3, 3), (27 * C2 // 2) ** -0.5, 0.21875)
    down_weight_three = noise(keys[4], (C3, C2, 2, 2, 2), (4 * C2) ** -0.5, 0.375)
    w_conv_three = noise(keys[5], (C3, C3, 3, 3, 3), (27 * C3 // 2) ** -0.5, 0.15625)
    w_head = noise(keys[6], (C3, NCLS), (C3 // 8) ** -0.5, 1.5)
    return dict(volume=volume, labels=labels, down_weight_two=down_weight_two, w_conv_two=w_conv_two, down_weight_three=down_weight_three, w_conv_three=w_conv_three, w_head=w_head)


SHIFT = math.log(2.0)
FORWARD_DIMS = ('NCDHW', 'OIDHW', 'NCDHW')
MIRROR_DIMS = ('NCDHW', 'IODHW', 'NCDHW')
KERNEL_DIMS = ('CNDHW', 'IODHW', 'CNDHW')

def leaky_rectifier(value):
    return jax.nn.softplus(value) - SHIFT

def slope_of(stored):
    return 1.0 - 0.5 * jnp.exp(-stored.astype(jnp.float32))

def strided_reduce(input_volumes, filter_weight):
    return lax.conv_general_dilated(input_volumes, filter_weight, (2, 2, 2), 'VALID', dimension_numbers=FORWARD_DIMS, preferred_element_type=jnp.float32)

def down_input_grad(grads, filter_weight):
    return lax.conv_general_dilated(grads, filter_weight[:, :, ::-1, ::-1, ::-1], (1, 1, 1), ((1, 1), (1, 1), (1, 1)), lhs_dilation=(2, 2, 2), dimension_numbers=MIRROR_DIMS, preferred_element_type=jnp.float32)

def down_weight_grad(input_volumes, grads):
    return lax.conv_general_dilated(input_volumes, grads, (1, 1, 1), 'VALID', rhs_dilation=(2, 2, 2), dimension_numbers=KERNEL_DIMS, preferred_element_type=jnp.float32)

def convolve(padded, filter_weight):
    return lax.conv_general_dilated(padded, filter_weight, (1, 1, 1), ((0, 0), (1, 1), (1, 1)), dimension_numbers=FORWARD_DIMS, preferred_element_type=jnp.float32)

def conv_input_grad(grads, filter_weight):
    return lax.conv_general_dilated(grads, filter_weight[:, :, ::-1, ::-1, ::-1], (1, 1, 1), ((2, 2), (1, 1), (1, 1)), dimension_numbers=MIRROR_DIMS, preferred_element_type=jnp.float32)

def conv_weight_grad(padded, grads):
    return lax.conv_general_dilated(padded, grads, (1, 1, 1), ((0, 0), (1, 1), (1, 1)), dimension_numbers=KERNEL_DIMS, preferred_element_type=jnp.float32)

def reference(volume, labels, down_weight_two, w_conv_two, down_weight_three, w_conv_three, w_head):
    classes = w_head.shape[1]
    scale = 1.0 / math.sqrt(labels.size)
    levels = jnp.arange(classes, dtype=jnp.int32).reshape(1, classes, 1, 1, 1)
    depth_pad = ((0, 0), (0, 0), (1, 1), (0, 0), (0, 0))
    head_wide = w_head.astype(jnp.float32)
    highest = lax.Precision.HIGHEST

    def one_crop(pair):
        input_volumes = pair[0][None]
        marks = pair[1][None]
        leading_volume = leaky_rectifier(strided_reduce(input_volumes, down_weight_two)).astype(jnp.bfloat16)
        first_padded = jnp.pad(leading_volume, depth_pad)
        hidden_features = leaky_rectifier(convolve(first_padded, w_conv_two)).astype(jnp.bfloat16)
        middle_features = leaky_rectifier(strided_reduce(hidden_features, down_weight_three)).astype(jnp.bfloat16)
        middle_padded = jnp.pad(middle_features, depth_pad)
        top = leaky_rectifier(convolve(middle_padded, w_conv_three)).astype(jnp.bfloat16)
        top_wide = top.astype(jnp.float32)
        logits = jnp.einsum('ncdhw,ck->nkdhw', top_wide, head_wide, precision=highest)
        powers = jnp.exp(logits)
        chosen = (marks[:, None] == levels).astype(jnp.float32)
        grad_logits = ((powers / lax.optimization_barrier(jnp.sum(powers, axis=1, keepdims=True)) - chosen) * scale).astype(jnp.bfloat16)
        grad_wide = grad_logits.astype(jnp.float32)
        grad_head = jnp.einsum('ncdhw,nkdhw->ck', top_wide, grad_wide, precision=highest)
        grad_top = jnp.einsum('nkdhw,ck->ncdhw', grad_wide, head_wide, precision=highest)
        grad_pre = (grad_top * slope_of(top)).astype(jnp.bfloat16)
        grad_conv_three = conv_weight_grad(middle_padded, grad_pre)
        grad_mid = conv_input_grad(grad_pre, w_conv_three)[:, :, 1:-1]
        grad_low = (grad_mid * slope_of(middle_features)).astype(jnp.bfloat16)
        grad_down_three = down_weight_grad(hidden_features, grad_low)
        grad_hidden = (down_input_grad(grad_low, down_weight_three) * slope_of(hidden_features)).astype(jnp.bfloat16)
        grad_conv_two = conv_weight_grad(first_padded, grad_hidden)
        grad_first = conv_input_grad(grad_hidden, w_conv_two)[:, :, 1:-1]
        grad_base = (grad_first * slope_of(leading_volume)).astype(jnp.bfloat16)
        grad_down_two = down_weight_grad(input_volumes, grad_base)
        return (grad_down_two, grad_conv_two, grad_down_three, grad_conv_three, grad_head)
    parts = lax.map(one_crop, (volume, labels))
    return (lax.optimization_barrier(jnp.sum(parts[0], axis=0)).reshape(-1), lax.optimization_barrier(jnp.sum(parts[1], axis=0)).reshape(-1), lax.optimization_barrier(jnp.sum(parts[2], axis=0)).reshape(-1), lax.optimization_barrier(jnp.sum(parts[3], axis=0)).reshape(-1), lax.optimization_barrier(jnp.sum(parts[4], axis=0)).reshape(-1))
```

```python
import functools
import math

import jax
import jax.numpy as jnp
from jax import lax
from jax.experimental import pallas as pl
from jax.experimental.pallas import tpu as pltpu
from jax.sharding import PartitionSpec as P


F32 = jnp.float32
BF16 = jnp.bfloat16
SHIFT = math.log(2.0)
CROPS = 2
T = 256
ROWS = 40
DOWN3, CONV2, DOWN2, HEAD = 27, 31, 38, 39


def params(megabytes=48):
    return pltpu.CompilerParams(vmem_limit_bytes=megabytes << 20)


def rectified(v):
    return jnp.maximum(v, 0.0) + jnp.log1p(jnp.exp(-jnp.abs(v))) - SHIFT


def slope(stored):
    return 1.0 - 0.5 * jnp.exp(-stored.astype(F32))


def dot(a, b):
    return jnp.dot(a, b, preferred_element_type=F32)


def dot_tn(a, b):
    return lax.dot_general(a, b, (((0,), (0,)), ((), ())), preferred_element_type=F32)


def dot_nt(a, b):
    return lax.dot_general(a, b, (((1,), (1,)), ((), ())), preferred_element_type=F32)


def moved(x, by):
    x = x.astype(F32)
    lane = lax.broadcasted_iota(jnp.int32, x.shape, 1)
    edge = 0 if by == 1 else 127
    return jnp.where(lane == edge, 0.0, pltpu.roll(x, by % 128, 1)).astype(BF16)


def three_two(x):
    even, odd = x[:, :128], x[:, 128:]
    return ((moved(odd, 1), even), (even, odd), (odd, moved(even, -1)))


def three_three(x):
    first, second = x[:, :128], x[:, 128:]
    return ((moved(first, 1), moved(second, 1)), (first, second), (moved(first, -1), moved(second, -1)))


def put_three(ref, row, shifted):
    for j, (left, right) in enumerate(shifted):
        ref[pl.ds(row + j * T, T), 0:128] = left
        ref[pl.ds(row + j * T, T), 128:256] = right


def call(kernel, outs, *args, scratch=(), **more):
    return pl.pallas_call(
        kernel,
        out_shape=[jax.ShapeDtypeStruct(s, d) for s, d in outs],
        scratch_shapes=list(scratch),
        compiler_params=params(),
        **more,
    )(*args)


def first_kernel(sec_ref, vol_ref, w_ref, vp_ref, a_ref, sort_ref, wt_ref):
    @pl.when(pl.program_id(0) == 0)
    def _():
        w = lax.broadcasted_iota(jnp.int32, (512, 512), 0)
        to = lax.broadcasted_iota(jnp.int32, (512, 512), 1)
        source = (to % 128) * 4 + (to // 128) % 2 * 2 + to // 256
        sort_ref[...] = jnp.where(w == source, 1.0, 0.0).astype(BF16)
        for d in range(2):
            wt_ref[:, pl.ds(d * 512, 512)] = w_ref[d].astype(F32).T.astype(BF16)

    for d in range(2):
        v = vol_ref[0, :, d].astype(F32).reshape(256, 512).astype(BF16)
        s = dot(v, sort_ref[...]).astype(BF16)
        vp_ref[0, 0, pl.ds(d * 512, 256), :] = s[:, :256]
        vp_ref[0, 0, pl.ds(d * 512 + 256, 256), :] = s[:, 256:]
    a_ref[0, 0] = rectified(dot(wt_ref[...], vp_ref[0, 0])).astype(BF16)


def first(sec, volume, w1):
    return pl.pallas_call(
        first_kernel,
        grid_spec=pltpu.PrefetchScalarGridSpec(
            num_scalar_prefetch=1,
            grid=(4,),
            in_specs=[
                pl.BlockSpec((1, 32, 2, 8, 512), lambda i, s: (2 * s[0] + i // 2, 0, i % 2, 0, 0)),
                pl.BlockSpec((2, 512, 256), lambda i, s: (0, 0, 0)),
            ],
            out_specs=[
                pl.BlockSpec((1, 1, 1024, 256), lambda i, s: (i // 2, i % 2, 0, 0)),
                pl.BlockSpec((1, 1, 256, 256), lambda i, s: (i // 2, i % 2, 0, 0)),
            ],
            scratch_shapes=[pltpu.VMEM((512, 512), BF16), pltpu.VMEM((256, 1024), BF16)],
        ),
        out_shape=[
            jax.ShapeDtypeStruct((CROPS, 2, 1024, 256), BF16),
            jax.ShapeDtypeStruct((CROPS, 2, 256, 256), BF16),
        ],
        compiler_params=params(),
    )(sec, volume, w1)


def prepare_kernel(w2_ref, w3_ref, f2_ref, b2_ref, f3_ref, b3_ref, perm_ref):
    low = lax.broadcasted_iota(jnp.int32, (64, 128), 1) < 64
    zero = jnp.zeros((64, 128), F32)
    for d in range(3):
        for j in range(3):
            at = (d * 3 + j) * T
            back = (8 - d * 3 - j) * T
            w = [w2_ref[d * 9 + h * 3 + j].astype(F32) for h in range(3)]
            pairs = {
                (0, 0): jnp.where(low, w[1], w[2]),
                (0, 1): zero,
                (1, 0): jnp.where(low, w[0], w[1]),
                (1, 1): jnp.where(low, w[2], 0.0),
                (2, 0): jnp.where(low, 0.0, w[0]),
                (2, 1): jnp.where(low, w[1], w[2]),
                (3, 0): zero,
                (3, 1): jnp.where(low, w[0], w[1]),
            }
            for (row, col), block in pairs.items():
                f2_ref[pl.ds(row * 64, 64), pl.ds(at + col * 128, 128)] = block.astype(BF16)
            b2_ref[:, pl.ds(back, T)] = f2_ref[:, pl.ds(at, T)].astype(F32).T.astype(BF16)
            for row in range(2):
                for col in range(2):
                    block = w3_ref[d * 9 + (col - row + 1) * 3 + j]
                    f3_ref[pl.ds(row * 128, 128), pl.ds(at + col * 128, 128)] = block
                    b3_ref[pl.ds(col * 128, 128), pl.ds(back + row * 128, 128)] = block.astype(F32).T.astype(BF16)
    r = lax.broadcasted_iota(jnp.int32, (1024, 256), 0)
    to = lax.broadcasted_iota(jnp.int32, (1024, 256), 1)
    c, h = r // 8 % 32, r % 8
    target = c // 16 * 128 + c % 16 * 8 + r // 512 * 4 + h * 2 + r // 256 % 2
    perm_ref[...] = jnp.where((target == to) & (h < 2), 1.0, 0.0).astype(BF16)


def prepare(w2, w3):
    wide = ((T, 9 * T), BF16)
    return call(prepare_kernel, [wide] * 4 + [((1024, 256), BF16)], w2, w3)


def second_kernel(lo_ref, a_ref, hi_ref, f2_ref, wd_ref, h_ref, a3_ref, b_ref):
    for n in range(CROPS):
        planes = (lo_ref[n, 0], a_ref[n, 0], a_ref[n, 1], hi_ref[n, 0])
        for k, plane in enumerate(planes):
            put_three(b_ref, k * 3 * T, three_two(plane))
        for d in range(2):
            h = rectified(dot(f2_ref[...], b_ref[pl.ds(d * 3 * T, 9 * T), :])).astype(BF16)
            for p in range(2):
                h_ref[2 * d + p, :, pl.ds(n * 128, 128)] = h[:, p * 128 : (p + 1) * 128]
    total = dot_tn(wd_ref[0], h_ref[0])
    for k in range(1, 4):
        total += dot_tn(wd_ref[k], h_ref[k])
    a3_ref[...] = rectified(total).astype(BF16)


def second(lo, a, hi, f2, wd):
    return call(
        second_kernel,
        [((4, T, T), BF16), ((T, T), BF16)],
        lo, a, hi, f2, wd,
        scratch=[pltpu.VMEM((12 * T, T), BF16)],
    )


def head_kernel(scale, lo_ref, a_ref, hi_ref, f3_ref, wh_ref, wht_ref, marks_ref, gz_ref, gh_ref, b_ref):
    for k, ref in enumerate((lo_ref, a_ref, hi_ref)):
        put_three(b_ref, k * 3 * T, three_three(ref[...]))
    top = rectified(dot(f3_ref[...], b_ref[...])).astype(BF16)
    row = lax.broadcasted_iota(jnp.int32, (128, T), 0)
    total = jnp.zeros((128, 128), F32)
    for h in range(2):
        mine = top[h * 128 : (h + 1) * 128]
        logits = dot(wht_ref[...], mine)
        powers = jnp.where(row < 4, jnp.exp(logits), 0.0)
        share = powers / jnp.sum(powers, axis=0, keepdims=True)
        chosen = jnp.where(row == marks_ref[pl.ds(h, 1), :], 1.0, 0.0)
        g = jnp.where(row < 4, (share - chosen) * scale, 0.0).astype(BF16)
        total += dot_nt(mine, g)
        gz_ref[pl.ds(h * 128, 128), :] = (dot(wh_ref[...], g) * slope(mine)).astype(BF16)
    gh_ref[...] = total


def head(lo, a, hi, f3, wh, wht, marks, scale):
    return call(
        functools.partial(head_kernel, scale),
        [((T, T), BF16), ((128, 128), F32)],
        lo, a, hi, f3, wh, wht, marks,
        scratch=[pltpu.VMEM((9 * T, T), BF16)],
    )


def weight_three_kernel(g_ref, lo_ref, a_ref, hi_ref, out_ref, s_ref):
    put_three(s_ref, 0, three_three(g_ref[...]))
    for d, ref in enumerate((lo_ref, a_ref, hi_ref)):
        a = ref[...]
        for j in range(3):
            t = dot_nt(s_ref[pl.ds((2 - j) * T, T), :], a)
            out_ref[d * 9 + j] = t[128:, :128]
            out_ref[d * 9 + 3 + j] = t[:128, :128] + t[128:, 128:]
            out_ref[d * 9 + 6 + j] = t[:128, 128:]


def weight_three(g, lo, a, hi):
    return call(
        weight_three_kernel,
        [((27, 128, 128), F32)],
        g, lo, a, hi,
        scratch=[pltpu.VMEM((3 * T, T), BF16)],
    )[0]


def middle_kernel(lo_ref, g_ref, hi_ref, b3_ref, a3_ref, h_ref, wd_ref, gz2_ref, gd_ref, b_ref):
    for k, ref in enumerate((lo_ref, g_ref, hi_ref)):
        put_three(b_ref, k * 3 * T, three_three(ref[...]))
    gy = (dot(b3_ref[...], b_ref[...]) * slope(a3_ref[...])).astype(BF16)
    for d in range(2):
        for p in range(2):
            k = 2 * d + p
            q = (dot(wd_ref[k], gy) * slope(h_ref[k])).astype(BF16)
            for n in range(CROPS):
                gz2_ref[n, d, :, pl.ds(p * 128, 128)] = q[:, n * 128 : (n + 1) * 128]
    for k in range(4):
        gd_ref[k] = dot_nt(gy[:128], h_ref[k, :128]) + dot_nt(gy[128:], h_ref[k, 128:])


def middle(lo, g, hi, b3, a3, h, wd):
    return call(
        middle_kernel,
        [((CROPS, 2, T, T), BF16), ((4, 128, 128), F32)],
        lo, g, hi, b3, a3, h, wd,
        scratch=[pltpu.VMEM((9 * T, T), BF16)],
    )


def weight_two_kernel(g_ref, lo_ref, a_ref, hi_ref, out_ref, gs_ref, as_ref):
    for n in range(CROPS):
        planes = (lo_ref[n, 0], a_ref[n, 0], a_ref[n, 1], hi_ref[n, 0])
        for d in range(2):
            at = (2 * n + d) * T
            for j, (left, right) in enumerate(three_two(g_ref[n, d])):
                gs_ref[2 - j, :, pl.ds(at, 128)] = left
                gs_ref[2 - j, :, pl.ds(at + 128, 128)] = right
            for k in range(3):
                as_ref[k, :, pl.ds(at, T)] = planes[d + k]
    low = lax.broadcasted_iota(jnp.int32, (64, 128), 1) < 64
    block = (lax.broadcasted_iota(jnp.int32, (64, 128), 1) // 32) % 2 == 0
    sums = {}
    for d in range(3):
        for j in range(3):
            t = dot_nt(gs_ref[j], as_ref[d])
            q = lambda r, c: t[r * 64 : (r + 1) * 64, c * 128 : (c + 1) * 128]
            sums[d, 0, j] = jnp.where(low, q(1, 0) + q(3, 1), q(2, 0))
            sums[d, 1, j] = jnp.where(low, q(0, 0) + q(2, 1), q(1, 0) + q(3, 1))
            sums[d, 2, j] = jnp.where(low, q(1, 1), q(0, 0) + q(2, 1))
        for h in range(3):
            for j in range(3):
                s = sums[d, h, j]
                sums[d, h, j] = s + pltpu.roll(s, 64, 1)
    taps = [sums[t // 9, t // 3 % 3, t % 3] for t in range(27)] + [jnp.zeros((64, 128), F32)]
    for g in range(7):
        four = taps[4 * g : 4 * g + 4]
        turned = [pltpu.roll(x, 32, 1) for x in four]
        out_ref[g, 0] = jnp.where(low, jnp.where(block, four[0], turned[1]), jnp.where(block, four[2], turned[3]))
        out_ref[g, 1] = jnp.where(low, jnp.where(block, turned[0], four[1]), jnp.where(block, turned[2], four[3]))


def weight_two(g, lo, a, hi):
    return call(
        weight_two_kernel,
        [((7, 2, 64, 128), F32)],
        g, lo, a, hi,
        scratch=[pltpu.VMEM((3, T, 4 * T), BF16), pltpu.VMEM((3, T, 4 * T), BF16)],
    )[0]


def last_kernel(
    lo_ref, g_ref, hi_ref, b2_ref, a_ref, vp_ref, perm_ref, w3_ref, d3_ref, w2_ref, gh_ref, out_ref, b_ref, t_ref, pack_ref
):
    for n in range(CROPS):
        planes = (lo_ref[n, 0], g_ref[n, 0], g_ref[n, 1], hi_ref[n, 0])
        for k, plane in enumerate(planes):
            put_three(b_ref, k * 3 * T, three_two(plane))
        for d in range(2):
            gy = (dot(b2_ref[...], b_ref[pl.ds(d * 3 * T, 9 * T), :]) * slope(a_ref[n, d])).astype(BF16)
            t = dot_nt(gy, vp_ref[n, d])
            if n + d == 0:
                t_ref[...] = t
            else:
                t_ref[...] += t
    pairs = []
    lane = lax.broadcasted_iota(jnp.int32, (64, 128), 1)
    for tile in range(8):
        at = pl.ds(tile * 128, 128)
        x = jnp.zeros((64, 128), F32)
        for h in range(4):
            x = jnp.where(lane % 8 // 2 == h, t_ref[pl.ds(h * 64, 64), at], x)
        x = x + pltpu.roll(x, 126, 1)
        x = x + pltpu.roll(x, 124, 1)
        pairs.append(x.astype(BF16))
    down = dot(jnp.concatenate(pairs, axis=1), perm_ref[...])
    for t in range(27):
        pack_ref[pl.ds(t, 128, stride=ROWS), :] = w3_ref[t]
    for k in range(4):
        pack_ref[pl.ds(DOWN3 + k, 128, stride=ROWS), :] = d3_ref[k]
    for half in range(2):
        for g in range(7):
            pack_ref[pl.ds(half * ROWS + CONV2 + g, 64, stride=2 * ROWS), :] = w2_ref[g, half]
        pack_ref[pl.ds(half * ROWS + DOWN2, 64, stride=2 * ROWS), :] = down[:, half * 128 : (half + 1) * 128]
    pack_ref[pl.ds(HEAD, 128, stride=ROWS), :] = gh_ref[...]
    out_ref[...] = pack_ref[...].astype(BF16)


def last(*args):
    return call(
        last_kernel,
        [((128 * ROWS, 128), BF16)],
        *args,
        scratch=[pltpu.VMEM((12 * T, T), BF16), pltpu.VMEM((T, 1024), F32), pltpu.VMEM((128 * ROWS, 128), F32)],
    )[0]


def neighbours(to_upper, to_lower):
    count = lax.axis_size("space")
    up = [(i, i + 1) for i in range(count - 1)]
    down = [(i + 1, i) for i in range(count - 1)]
    return lax.ppermute(to_upper, "space", up), lax.ppermute(to_lower, "space", down)


def unpack(sums):
    return (
        sums[DOWN2],
        sums[CONV2:DOWN2].reshape(28, 32)[:27].T.reshape(-1),
        sums[DOWN3:CONV2].reshape(2, 2, 2, 64).transpose(3, 0, 2, 1).reshape(-1),
        sums[:27].T.reshape(-1),
        sums[HEAD, :4],
    )


def finish(pack):
    terms = lax.all_to_all(pack, ("section", "space"), 0, 0, tiled=True)
    return unpack(jnp.sum(terms.astype(F32), axis=0))


def per_device(volume, labels, down_weight_two, w_conv_two, down_weight_three, w_conv_three, w_head):
    count = lax.axis_size("space")
    voxels = labels.shape[0] * labels.shape[1] * count * labels.shape[2] * labels.shape[3]
    scale = 1.0 / math.sqrt(voxels)
    sec = lax.axis_index("section").astype(jnp.int32)

    eye4 = jnp.eye(4, dtype=BF16)
    w1 = down_weight_two.transpose(2, 4, 1, 3, 0)[:, :, :, None, :, None, :] * eye4[:, None, :, None]
    w1 = w1.reshape(2, 512, 256)
    eye2 = jnp.eye(2, dtype=BF16)
    wd = down_weight_three.transpose(2, 4, 3, 1, 0)[:, :, None, :, :, None, :] * eye2[:, None, None, :, None]
    wd = wd.reshape(4, 256, 256)
    w2 = w_conv_two.transpose(2, 3, 4, 0, 1).reshape(27, 64, 64)
    w2 = jnp.concatenate([w2, w2], axis=2)
    w3 = w_conv_three.transpose(2, 3, 4, 0, 1).reshape(27, 128, 128)
    wh = jnp.pad(w_head, ((0, 0), (0, 124)))
    wht = jnp.pad(w_head.T, ((0, 124), (0, 0)))
    marks = lax.dynamic_slice_in_dim(labels[:, 0], CROPS * sec, CROPS, axis=0)
    marks = marks.transpose(1, 0, 2).reshape(2, 256)

    vp, a2 = first(sec[None], volume, w1)
    a2_lo, a2_hi = neighbours(a2[:, 1:], a2[:, :1])
    f2, b2, f3, b3, perm = prepare(w2, w3)
    h2, a3 = second(a2_lo, a2, a2_hi, f2, wd)
    a3_lo, a3_hi = neighbours(a3, a3)
    gz4, gh = head(a3_lo, a3, a3_hi, f3, wh, wht, marks, scale)
    gz4_lo, gz4_hi = neighbours(gz4, gz4)
    gw3 = weight_three(gz4, a3_lo, a3, a3_hi)
    gz2, gd3 = middle(gz4_lo, gz4, gz4_hi, b3, a3, h2, wd)
    gz2_lo, gz2_hi = neighbours(gz2[:, 1:], gz2[:, :1])
    gw2 = weight_two(gz2, a2_lo, a2, a2_hi)
    pack = last(gz2_lo, gz2, gz2_hi, b2, a2, vp, perm, gw3, gd3, gw2, gh)

    return finish(pack.reshape(128, ROWS, 128))


def solution(mesh):
    whole = P(("section", "space"))
    return jax.shard_map(
        per_device,
        mesh=mesh,
        in_specs=(P(None, None, "space", None, None), P(None, "space", None, None), P(), P(), P(), P(), P()),
        out_specs=(whole,) * 5,
        check_vma=False,
    )
```

```python
import functools
import math

import jax
import jax.numpy as jnp
from jax import lax
from jax.experimental import pallas as pl
from jax.experimental.pallas import tpu as pltpu
from jax.sharding import PartitionSpec as P


F32 = jnp.float32
BF16 = jnp.bfloat16
SHIFT = math.log(2.0)
CROPS = 2
T = 256
ROWS = 40
DOWN3, CONV2, DOWN2, HEAD = 27, 31, 38, 39


def params(megabytes=24):
    return pltpu.CompilerParams(vmem_limit_bytes=megabytes << 20)


def rectified(v):
    return jnp.maximum(v, 0.0) + jnp.log1p(jnp.exp(-jnp.abs(v))) - SHIFT


def slope(stored):
    return 1.0 - 0.5 * jnp.exp(-stored.astype(F32))


def dot(a, b):
    return jnp.dot(a, b, preferred_element_type=F32)


def dot_tn(a, b):
    return lax.dot_general(a, b, (((0,), (0,)), ((), ())), preferred_element_type=F32)


def dot_nt(a, b):
    return lax.dot_general(a, b, (((1,), (1,)), ((), ())), preferred_element_type=F32)


def moved(x, by):
    x = x.astype(F32)
    lane = lax.broadcasted_iota(jnp.int32, x.shape, 1)
    edge = 0 if by == 1 else 127
    return jnp.where(lane == edge, 0.0, pltpu.roll(x, by % 128, 1)).astype(BF16)


def three_two(x):
    even, odd = x[:, :128], x[:, 128:]
    return ((moved(odd, 1), even), (even, odd), (odd, moved(even, -1)))


def three_three(x):
    first, second = x[:, :128], x[:, 128:]
    return ((moved(first, 1), moved(second, 1)), (first, second), (moved(first, -1), moved(second, -1)))


def put_three(ref, row, shifted):
    for j, (left, right) in enumerate(shifted):
        ref[pl.ds(row + j * T, T), 0:128] = left
        ref[pl.ds(row + j * T, T), 128:256] = right


def call(kernel, outs, *args, scratch=()):
    spec = pl.BlockSpec(memory_space=pltpu.VMEM)
    scalar = pl.BlockSpec(memory_space=pltpu.SMEM)
    return pl.pallas_call(
        kernel,
        in_specs=[scalar if a.dtype == jnp.int32 and a.ndim == 1 else spec for a in args],
        out_specs=[spec] * len(outs),
        out_shape=[jax.ShapeDtypeStruct(s, d) for s, d in outs],
        scratch_shapes=list(scratch),
        compiler_params=params(),
    )(*args)


def sorted_out(where_ref, one, two):
    even = where_ref[1] == 0
    return jnp.where(even, two, one), jnp.where(even, one, two)


def first_kernel(where_ref, vol_ref, w_ref, vp_ref, a_ref, one_ref, two_ref, sort_ref, wt_ref):
    @pl.when(pl.program_id(0) == 0)
    def _():
        to = lax.broadcasted_iota(jnp.int32, (1, 512), 1)
        source = (to % 128) * 4 + (to // 128) % 2 * 2 + to // 256
        sort_ref[...] = jnp.where(lax.broadcasted_iota(jnp.int32, (512, 512), 0) == source, 1.0, 0.0).astype(BF16)
        to = lax.broadcasted_iota(jnp.int32, (1, 1024), 1)
        height = to % 8
        source = to // 8 % 32 * 8 + to // 512 * 4 + height % 2 * 2 + to // 256 % 2
        pick = jnp.where(lax.broadcasted_iota(jnp.int32, (256, 1024), 0) == source, 1.0, 0.0).astype(BF16)
        w = dot_tn(w_ref[...], pick)
        for h in range(4):
            wt_ref[pl.ds(h * 64, 64), :] = jnp.where(height // 2 == h, w, 0.0).astype(BF16)

    for d in range(2):
        v = vol_ref[0, :, d].astype(F32).reshape(256, 512).astype(BF16)
        s = dot(v, sort_ref[...]).astype(BF16)
        vp_ref[0, 0, pl.ds(d * 512, 256), :] = s[:, :256]
        vp_ref[0, 0, pl.ds(d * 512 + 256, 256), :] = s[:, 256:]
    a = rectified(dot(wt_ref[...], vp_ref[0, 0])).astype(BF16)
    a_ref[0, 0] = a
    upper = pl.program_id(0) % 2

    @pl.when(upper == where_ref[1])
    def _():
        two_ref[0] = a

    @pl.when(upper != where_ref[1])
    def _():
        one_ref[0] = a


def first(where, volume, w1):
    half = pl.BlockSpec((1, T, T), lambda i, s: (i // 2, 0, 0))
    return pl.pallas_call(
        first_kernel,
        grid_spec=pltpu.PrefetchScalarGridSpec(
            num_scalar_prefetch=1,
            grid=(4,),
            in_specs=[
                pl.BlockSpec((1, 32, 2, 8, 512), lambda i, s: (2 * s[0] + i // 2, 0, i % 2, 0, 0)),
                pl.BlockSpec((256, 64), lambda i, s: (0, 0)),
            ],
            out_specs=[
                pl.BlockSpec((1, 1, 1024, 256), lambda i, s: (i // 2, i % 2, 0, 0)),
                pl.BlockSpec((1, 1, 256, 256), lambda i, s: (i // 2, i % 2, 0, 0)),
                half,
                half,
            ],
            scratch_shapes=[pltpu.VMEM((512, 512), BF16), pltpu.VMEM((256, 1024), BF16)],
        ),
        out_shape=[
            jax.ShapeDtypeStruct((CROPS, 2, 1024, 256), BF16),
            jax.ShapeDtypeStruct((CROPS, 2, 256, 256), BF16),
            jax.ShapeDtypeStruct((CROPS, 256, 256), BF16),
            jax.ShapeDtypeStruct((CROPS, 256, 256), BF16),
        ],
        compiler_params=params(),
    )(where, volume, w1)


def prepare_kernel(
    w2_ref, w3_ref, wd_ref, head_ref, f2_ref, b2_ref, f3_ref, b3_ref, perm_ref, d_ref, wh_ref, wht_ref, rows_ref
):
    low = lax.broadcasted_iota(jnp.int32, (64, 128), 1) < 64
    zero = jnp.zeros((64, 128), F32)
    for d in range(3):
        for j in range(3):
            at = (d * 3 + j) * T
            back = (8 - d * 3 - j) * T
            w = [w2_ref[d * 9 + h * 3 + j].astype(F32) for h in range(3)]
            pairs = {
                (0, 0): jnp.where(low, w[1], w[2]),
                (0, 1): zero,
                (1, 0): jnp.where(low, w[0], w[1]),
                (1, 1): jnp.where(low, w[2], 0.0),
                (2, 0): jnp.where(low, 0.0, w[0]),
                (2, 1): jnp.where(low, w[1], w[2]),
                (3, 0): zero,
                (3, 1): jnp.where(low, w[0], w[1]),
            }
            for (row, col), block in pairs.items():
                f2_ref[pl.ds(row * 64, 64), pl.ds(at + col * 128, 128)] = block.astype(BF16)
            b2_ref[:, pl.ds(back, T)] = f2_ref[:, pl.ds(at, T)].astype(F32).T.astype(BF16)
            for row in range(2):
                for col in range(2):
                    block = w3_ref[d * 9 + (col - row + 1) * 3 + j]
                    f3_ref[pl.ds(row * 128, 128), pl.ds(at + col * 128, 128)] = block
                    b3_ref[pl.ds(col * 128, 128), pl.ds(back + row * 128, 128)] = block.astype(F32).T.astype(BF16)
    rows_ref[...] = wd_ref[...].astype(F32)
    for d in range(2):
        for p in range(2):
            for h in range(4):
                block = rows_ref[pl.ds(d * 4 + h % 2 * 2 + p, 64, stride=8), :].astype(BF16)
                d_ref[2 * d + p, pl.ds(h * 64, 64), pl.ds(h // 2 * 128, 128)] = block
                d_ref[2 * d + p, pl.ds(h * 64, 64), pl.ds(128 - h // 2 * 128, 128)] = jnp.zeros_like(block)
    rows_ref[pl.ds(0, 128), :] = jnp.zeros((128, 128), F32)
    rows_ref[pl.ds(0, 4), :] = head_ref[...].astype(F32)
    wht = rows_ref[pl.ds(0, 128), :]
    wht_ref[...] = wht.astype(BF16)
    wh_ref[...] = wht.T.astype(BF16)
    to = lax.broadcasted_iota(jnp.int32, (1, 256), 1)
    source = to // 4 % 2 * 512 + to % 2 * 256 + (to // 128 * 16 + to // 8 % 16) * 8 + to // 2 % 2
    perm_ref[...] = jnp.where(lax.broadcasted_iota(jnp.int32, (1024, 256), 0) == source, 1.0, 0.0).astype(BF16)


def prepare(w2, w3, wd, wh):
    wide = ((T, 9 * T), BF16)
    square = ((128, 128), BF16)
    return call(
        prepare_kernel,
        [wide] * 4 + [((1024, 256), BF16), ((4, T, T), BF16), square, square],
        w2, w3, wd, wh,
        scratch=[pltpu.VMEM((512, 128), F32)],
    )


def second_kernel(where_ref, one_ref, a_ref, two_ref, f2_ref, wd_ref, h_ref, a3_ref, b_ref):
    for n in range(CROPS):
        lo, hi = sorted_out(where_ref, one_ref[n], two_ref[n])
        planes = (lo, a_ref[n, 0], a_ref[n, 1], hi)
        for k, plane in enumerate(planes):
            put_three(b_ref, k * 3 * T, three_two(plane))
        for d in range(2):
            h = rectified(dot(f2_ref[...], b_ref[pl.ds(d * 3 * T, 9 * T), :])).astype(BF16)
            for p in range(2):
                h_ref[2 * d + p, :, pl.ds(n * 128, 128)] = h[:, p * 128 : (p + 1) * 128]
    total = dot_tn(wd_ref[0], h_ref[0])
    for k in range(1, 4):
        total += dot_tn(wd_ref[k], h_ref[k])
    a3_ref[...] = rectified(total).astype(BF16)


def second(where, one, a, two, f2, wd):
    return call(
        second_kernel,
        [((4, T, T), BF16), ((T, T), BF16)],
        where, one, a, two, f2, wd,
        scratch=[pltpu.VMEM((12 * T, T), BF16)],
    )


def head_kernel(scale, where_ref, one_ref, a_ref, two_ref, f3_ref, wh_ref, wht_ref, marks_ref, gz_ref, gh_ref, b_ref):
    lo, hi = sorted_out(where_ref, one_ref[...], two_ref[...])
    for k, plane in enumerate((lo, a_ref[...], hi)):
        put_three(b_ref, k * 3 * T, three_three(plane))
    top = rectified(dot(f3_ref[...], b_ref[...])).astype(BF16)
    row = lax.broadcasted_iota(jnp.int32, (128, T), 0)
    total = jnp.zeros((128, 128), F32)
    for h in range(2):
        mine = top[h * 128 : (h + 1) * 128]
        logits = dot(wht_ref[...], mine)
        powers = jnp.where(row < 4, jnp.exp(logits), 0.0)
        share = powers / jnp.sum(powers, axis=0, keepdims=True)
        chosen = jnp.where(row == marks_ref[pl.ds(h, 1), :], 1.0, 0.0)
        g = jnp.where(row < 4, (share - chosen) * scale, 0.0).astype(BF16)
        total += dot_nt(mine, g)
        gz_ref[pl.ds(h * 128, 128), :] = (dot(wh_ref[...], g) * slope(mine)).astype(BF16)
    gh_ref[...] = total


def head(where, one, a, two, f3, wh, wht, marks, scale):
    return call(
        functools.partial(head_kernel, scale),
        [((T, T), BF16), ((128, 128), F32)],
        where, one, a, two, f3, wh, wht, marks,
        scratch=[pltpu.VMEM((9 * T, T), BF16)],
    )


def weight_three_kernel(where_ref, g_ref, one_ref, a_ref, two_ref, out_ref, s_ref):
    put_three(s_ref, 0, three_three(g_ref[...]))
    lo, hi = sorted_out(where_ref, one_ref[...], two_ref[...])
    for d, a in enumerate((lo, a_ref[...], hi)):
        for j in range(3):
            t = dot_nt(s_ref[pl.ds((2 - j) * T, T), :], a)
            out_ref[d * 9 + j] = t[128:, :128]
            out_ref[d * 9 + 3 + j] = t[:128, :128] + t[128:, 128:]
            out_ref[d * 9 + 6 + j] = t[:128, 128:]


def weight_three(where, g, one, a, two):
    return call(
        weight_three_kernel,
        [((27, 128, 128), F32)],
        where, g, one, a, two,
        scratch=[pltpu.VMEM((3 * T, T), BF16)],
    )[0]


def middle_kernel(
    where_ref, one_ref, g_ref, two_ref, b3_ref, a3_ref, h_ref, wd_ref, gz2_ref, gone_ref, gtwo_ref, gd_ref, b_ref
):
    lo, hi = sorted_out(where_ref, one_ref[...], two_ref[...])
    for k, plane in enumerate((lo, g_ref[...], hi)):
        put_three(b_ref, k * 3 * T, three_three(plane))
    gy = (dot(b3_ref[...], b_ref[...]) * slope(a3_ref[...])).astype(BF16)
    for d in range(2):
        for p in range(2):
            k = 2 * d + p
            q = (dot(wd_ref[k], gy) * slope(h_ref[k])).astype(BF16)
            for n in range(CROPS):
                gz2_ref[n, d, :, pl.ds(p * 128, 128)] = q[:, n * 128 : (n + 1) * 128]
    even = where_ref[1] == 0
    for n in range(CROPS):
        gone_ref[n] = jnp.where(even, gz2_ref[n, 1], gz2_ref[n, 0])
        gtwo_ref[n] = jnp.where(even, gz2_ref[n, 0], gz2_ref[n, 1])
    for k in range(4):
        gd_ref[k] = dot_nt(gy[:128], h_ref[k, :128]) + dot_nt(gy[128:], h_ref[k, 128:])


def middle(where, one, g, two, b3, a3, h, wd):
    return call(
        middle_kernel,
        [((CROPS, 2, T, T), BF16), ((CROPS, T, T), BF16), ((CROPS, T, T), BF16), ((4, 128, 128), F32)],
        where, one, g, two, b3, a3, h, wd,
        scratch=[pltpu.VMEM((9 * T, T), BF16)],
    )


def weight_two_kernel(where_ref, g_ref, one_ref, a_ref, two_ref, out_ref, gs_ref, as_ref):
    for n in range(CROPS):
        lo, hi = sorted_out(where_ref, one_ref[n], two_ref[n])
        planes = (lo, a_ref[n, 0], a_ref[n, 1], hi)
        for d in range(2):
            at = (2 * n + d) * T
            for j, (left, right) in enumerate(three_two(g_ref[n, d])):
                gs_ref[2 - j, :, pl.ds(at, 128)] = left
                gs_ref[2 - j, :, pl.ds(at + 128, 128)] = right
            for k in range(3):
                as_ref[k, :, pl.ds(at, T)] = planes[d + k]
    low = lax.broadcasted_iota(jnp.int32, (64, 128), 1) < 64
    block = (lax.broadcasted_iota(jnp.int32, (64, 128), 1) // 32) % 2 == 0
    sums = {}
    for d in range(3):
        for j in range(3):
            t = dot_nt(gs_ref[j], as_ref[d])
            q = lambda r, c: t[r * 64 : (r + 1) * 64, c * 128 : (c + 1) * 128]
            sums[d, 0, j] = jnp.where(low, q(1, 0) + q(3, 1), q(2, 0))
            sums[d, 1, j] = jnp.where(low, q(0, 0) + q(2, 1), q(1, 0) + q(3, 1))
            sums[d, 2, j] = jnp.where(low, q(1, 1), q(0, 0) + q(2, 1))
        for h in range(3):
            for j in range(3):
                s = sums[d, h, j]
                sums[d, h, j] = s + pltpu.roll(s, 64, 1)
    taps = [sums[t // 9, t // 3 % 3, t % 3] for t in range(27)] + [jnp.zeros((64, 128), F32)]
    for g in range(7):
        four = taps[4 * g : 4 * g + 4]
        turned = [pltpu.roll(x, 32, 1) for x in four]
        out_ref[g, 0] = jnp.where(low, jnp.where(block, four[0], turned[1]), jnp.where(block, four[2], turned[3]))
        out_ref[g, 1] = jnp.where(low, jnp.where(block, turned[0], four[1]), jnp.where(block, turned[2], four[3]))


def weight_two(where, g, one, a, two):
    return call(
        weight_two_kernel,
        [((7, 2, 64, 128), F32)],
        where, g, one, a, two,
        scratch=[pltpu.VMEM((3, T, 4 * T), BF16), pltpu.VMEM((3, T, 4 * T), BF16)],
    )[0]


def pack_kernel(w3_ref, d3_ref, w2_ref, gh_ref, out_ref):
    for t in range(27):
        out_ref[pl.ds(t, 128, stride=ROWS), :] = w3_ref[t]
    for k in range(4):
        out_ref[pl.ds(DOWN3 + k, 128, stride=ROWS), :] = d3_ref[k]
    for half in range(2):
        for g in range(7):
            out_ref[pl.ds(half * ROWS + CONV2 + g, 64, stride=2 * ROWS), :] = w2_ref[g, half]
    out_ref[pl.ds(DOWN2, 128, stride=ROWS), :] = jnp.zeros((128, 128), F32)
    out_ref[pl.ds(HEAD, 128, stride=ROWS), :] = gh_ref[...]


def packed(*args):
    return call(pack_kernel, [((128 * ROWS, 128), F32)], *args)[0]


def last_kernel(
    where_ref, one_ref, g_ref, two_ref, b2_ref, a_ref, vp_ref, perm_ref, pack_ref, out_ref, b_ref, t_ref, d_ref
):
    for n in range(CROPS):
        lo, hi = sorted_out(where_ref, one_ref[n], two_ref[n])
        planes = (lo, g_ref[n, 0], g_ref[n, 1], hi)
        for k, plane in enumerate(planes):
            put_three(b_ref, k * 3 * T, three_two(plane))
        for d in range(2):
            gy = (dot(b2_ref[...], b_ref[pl.ds(d * 3 * T, 9 * T), :]) * slope(a_ref[n, d])).astype(BF16)
            t = dot_nt(gy, vp_ref[n, d])
            if n + d == 0:
                t_ref[...] = t
            else:
                t_ref[...] += t
    pairs = []
    lane = lax.broadcasted_iota(jnp.int32, (64, 128), 1)
    for tile in range(8):
        at = pl.ds(tile * 128, 128)
        x = jnp.zeros((64, 128), F32)
        for h in range(4):
            x = jnp.where(lane % 8 // 2 == h, t_ref[pl.ds(h * 64, 64), at], x)
        x = x + pltpu.roll(x, 126, 1)
        x = x + pltpu.roll(x, 124, 1)
        pairs.append(x.astype(BF16))
    down = dot(jnp.concatenate(pairs, axis=1), perm_ref[...])
    for half in range(2):
        d_ref[pl.ds(half * ROWS + DOWN2, 64, stride=2 * ROWS), :] = down[:, half * 128 : (half + 1) * 128]
    row = lax.broadcasted_iota(jnp.int32, (ROWS, 128), 0)
    for j in range(128):
        at = pl.ds(j * ROWS, ROWS)
        out_ref[at, :] = jnp.where(row == DOWN2, d_ref[at, :], pack_ref[at, :]).astype(BF16)


def last(*args):
    return call(
        last_kernel,
        [((128 * ROWS, 128), BF16)],
        *args,
        scratch=[pltpu.VMEM((12 * T, T), BF16), pltpu.VMEM((T, 1024), F32), pltpu.VMEM((128 * ROWS, 128), F32)],
    )[0]


def swapped(one, two):
    count = lax.axis_size("space")
    near = [(i, i ^ 1) for i in range(count)]
    far = [(i, ((i + 1) ^ 1) - 1) for i in range(1, count - 1)]
    two = lax.ppermute(two, "space", far)
    return lax.ppermute(one, "space", near), two


def unpack(sums):
    return (
        sums[DOWN2],
        sums[CONV2:DOWN2].reshape(28, 32)[:27].T.reshape(-1),
        sums[DOWN3:CONV2].reshape(2, 2, 2, 64).transpose(3, 0, 2, 1).reshape(-1),
        sums[:27].T.reshape(-1),
        sums[HEAD, :4],
    )


def finish(pack):
    terms = lax.all_to_all(pack, ("section", "space"), 0, 0, tiled=True)
    return unpack(jnp.sum(terms.astype(F32), axis=0))


def per_device(volume, labels, down_weight_two, w_conv_two, down_weight_three, w_conv_three, w_head):
    count = lax.axis_size("space")
    voxels = labels.shape[0] * labels.shape[1] * count * labels.shape[2] * labels.shape[3]
    scale = 1.0 / math.sqrt(voxels)
    sec = lax.axis_index("section").astype(jnp.int32)
    where = jnp.stack([sec, lax.axis_index("space").astype(jnp.int32) % 2])

    w1 = down_weight_two.transpose(1, 2, 3, 4, 0).reshape(256, 64)
    wd = down_weight_three.transpose(1, 2, 3, 4, 0).reshape(512, 128)
    w2 = w_conv_two.transpose(2, 3, 4, 0, 1).reshape(27, 64, 64)
    w2 = jnp.concatenate([w2, w2], axis=2)
    w3 = w_conv_three.transpose(2, 3, 4, 0, 1).reshape(27, 128, 128)
    marks = lax.dynamic_slice_in_dim(labels[:, 0], CROPS * sec, CROPS, axis=0)
    marks = marks.transpose(1, 0, 2).reshape(2, 256)

    vp, a2, one, two = first(where, volume, w1)
    a2_one, a2_two = swapped(one, two)
    f2, b2, f3, b3, perm, wd, wh, wht = prepare(w2, w3, wd, w_head.T)
    h2, a3 = second(where, a2_one, a2, a2_two, f2, wd)
    a3_one, a3_two = swapped(a3, a3)
    gz4, gh = head(where, a3_one, a3, a3_two, f3, wh, wht, marks, scale)
    gz4_one, gz4_two = swapped(gz4, gz4)
    gw3 = weight_three(where, gz4, a3_one, a3, a3_two)
    gz4_one, gz4_two, gw3 = lax.optimization_barrier((gz4_one, gz4_two, gw3))
    gz2, one, two, gd3 = middle(where, gz4_one, gz4, gz4_two, b3, a3, h2, wd)
    gz2_one, gz2_two = swapped(one, two)
    gw2 = weight_two(where, gz2, a2_one, a2, a2_two)
    pack = packed(gw3, gd3, gw2, gh)
    pack = last(where, gz2_one, gz2, gz2_two, b2, a2, vp, perm, pack)
    return finish(pack.reshape(128, ROWS, 128))


def solution(mesh):
    whole = P(("section", "space"))
    return jax.shard_map(
        per_device,
        mesh=mesh,
        in_specs=(P(None, None, "space", None, None), P(None, "space", None, None), P(), P(), P(), P(), P()),
        out_specs=(whole,) * 5,
        check_vma=False,
    )
```

```python
import functools
import math

import jax
import jax.numpy as jnp
from jax import lax
from jax.experimental import pallas as pl
from jax.experimental.pallas import tpu as pltpu
from jax.sharding import PartitionSpec as P


F32 = jnp.float32
BF16 = jnp.bfloat16
SHIFT = math.log(2.0)
CROPS = 2
T = 256
ROWS = 40
DOWN3, CONV2, DOWN2, HEAD = 27, 31, 38, 39


def params(megabytes=24):
    return pltpu.CompilerParams(vmem_limit_bytes=megabytes << 20)


def rectified(v):
    return jnp.maximum(v, 0.0) + jnp.log1p(jnp.exp(-jnp.abs(v))) - SHIFT


def slope(stored):
    return 1.0 - 0.5 * jnp.exp(-stored.astype(F32))


def dot(a, b):
    return jnp.dot(a, b, preferred_element_type=F32)


def dot_tn(a, b):
    return lax.dot_general(a, b, (((0,), (0,)), ((), ())), preferred_element_type=F32)


def dot_nt(a, b):
    return lax.dot_general(a, b, (((1,), (1,)), ((), ())), preferred_element_type=F32)


def moved(x, by):
    x = x.astype(F32)
    lane = lax.broadcasted_iota(jnp.int32, x.shape, 1)
    edge = 0 if by == 1 else 127
    return jnp.where(lane == edge, 0.0, pltpu.roll(x, by % 128, 1)).astype(BF16)


def three_two(x):
    even, odd = x[:, :128], x[:, 128:]
    return ((moved(odd, 1), even), (even, odd), (odd, moved(even, -1)))


def three_three(x):
    first, second = x[:, :128], x[:, 128:]
    return ((moved(first, 1), moved(second, 1)), (first, second), (moved(first, -1), moved(second, -1)))


def put_three(ref, row, shifted):
    for j, (left, right) in enumerate(shifted):
        ref[pl.ds(row + j * T, T), 0:128] = left
        ref[pl.ds(row + j * T, T), 128:256] = right


def call(kernel, outs, *args, scratch=()):
    spec = pl.BlockSpec(memory_space=pltpu.VMEM)
    scalar = pl.BlockSpec(memory_space=pltpu.SMEM)
    return pl.pallas_call(
        kernel,
        in_specs=[scalar if a.dtype == jnp.int32 and a.ndim == 1 else spec for a in args],
        out_specs=[spec] * len(outs),
        out_shape=[pltpu.VMEM(s, d) for s, d in outs],
        scratch_shapes=list(scratch),
        compiler_params=params(),
    )(*args)


def sorted_out(where_ref, one, two):
    even = where_ref[1] == 0
    return jnp.where(even, two, one), jnp.where(even, one, two)


def first_kernel(where_ref, vol_ref, w_ref, vp_ref, a_ref, one_ref, two_ref, sort_ref, wt_ref):
    @pl.when(pl.program_id(0) == 0)
    def _():
        to = lax.broadcasted_iota(jnp.int32, (1, 512), 1)
        source = (to % 128) * 4 + (to // 128) % 2 * 2 + to // 256
        sort_ref[...] = jnp.where(lax.broadcasted_iota(jnp.int32, (512, 512), 0) == source, 1.0, 0.0).astype(BF16)
        to = lax.broadcasted_iota(jnp.int32, (1, 1024), 1)
        height = to % 8
        source = to // 8 % 32 * 8 + to // 512 * 4 + height % 2 * 2 + to // 256 % 2
        pick = jnp.where(lax.broadcasted_iota(jnp.int32, (256, 1024), 0) == source, 1.0, 0.0).astype(BF16)
        w = dot_tn(w_ref[...], pick)
        for h in range(4):
            wt_ref[pl.ds(h * 64, 64), :] = jnp.where(height // 2 == h, w, 0.0).astype(BF16)

    for d in range(2):
        v = vol_ref[0, :, d].astype(F32).reshape(256, 512).astype(BF16)
        s = dot(v, sort_ref[...]).astype(BF16)
        vp_ref[0, 0, pl.ds(d * 512, 256), :] = s[:, :256]
        vp_ref[0, 0, pl.ds(d * 512 + 256, 256), :] = s[:, 256:]
    a = rectified(dot(wt_ref[...], vp_ref[0, 0])).astype(BF16)
    a_ref[0, 0] = a
    upper = pl.program_id(0) % 2

    @pl.when(upper == where_ref[1])
    def _():
        two_ref[0] = a

    @pl.when(upper != where_ref[1])
    def _():
        one_ref[0] = a


def first(where, volume, w1):
    half = pl.BlockSpec((1, T, T), lambda i, s: (i // 2, 0, 0))
    return pl.pallas_call(
        first_kernel,
        grid_spec=pltpu.PrefetchScalarGridSpec(
            num_scalar_prefetch=1,
            grid=(4,),
            in_specs=[
                pl.BlockSpec((1, 32, 2, 8, 512), lambda i, s: (2 * s[0] + i // 2, 0, i % 2, 0, 0)),
                pl.BlockSpec((256, 64), lambda i, s: (0, 0)),
            ],
            out_specs=[
                pl.BlockSpec((1, 1, 1024, 256), lambda i, s: (i // 2, i % 2, 0, 0)),
                pl.BlockSpec((1, 1, 256, 256), lambda i, s: (i // 2, i % 2, 0, 0)),
                half,
                half,
            ],
            scratch_shapes=[pltpu.VMEM((512, 512), BF16), pltpu.VMEM((256, 1024), BF16)],
        ),
        out_shape=[
            pltpu.VMEM((CROPS, 2, 1024, 256), BF16),
            pltpu.VMEM((CROPS, 2, 256, 256), BF16),
            pltpu.VMEM((CROPS, 256, 256), BF16),
            pltpu.VMEM((CROPS, 256, 256), BF16),
        ],
        compiler_params=params(),
    )(where, pltpu.with_memory_space_constraint(volume, pltpu.HBM), pltpu.with_memory_space_constraint(w1, pltpu.HBM))


def prepare_kernel(
    w2_ref, w3_ref, wd_ref, head_ref, f2_ref, b2_ref, f3_ref, b3_ref, perm_ref, d_ref, wh_ref, wht_ref, rows_ref
):
    low = lax.broadcasted_iota(jnp.int32, (64, 128), 1) < 64
    zero = jnp.zeros((64, 128), F32)
    for d in range(3):
        for j in range(3):
            at = (d * 3 + j) * T
            back = (8 - d * 3 - j) * T
            w = [w2_ref[d * 9 + h * 3 + j].astype(F32) for h in range(3)]
            pairs = {
                (0, 0): jnp.where(low, w[1], w[2]),
                (0, 1): zero,
                (1, 0): jnp.where(low, w[0], w[1]),
                (1, 1): jnp.where(low, w[2], 0.0),
                (2, 0): jnp.where(low, 0.0, w[0]),
                (2, 1): jnp.where(low, w[1], w[2]),
                (3, 0): zero,
                (3, 1): jnp.where(low, w[0], w[1]),
            }
            for (row, col), block in pairs.items():
                f2_ref[pl.ds(row * 64, 64), pl.ds(at + col * 128, 128)] = block.astype(BF16)
            b2_ref[:, pl.ds(back, T)] = f2_ref[:, pl.ds(at, T)].astype(F32).T.astype(BF16)
            for row in range(2):
                for col in range(2):
                    block = w3_ref[d * 9 + (col - row + 1) * 3 + j]
                    f3_ref[pl.ds(row * 128, 128), pl.ds(at + col * 128, 128)] = block
                    b3_ref[pl.ds(col * 128, 128), pl.ds(back + row * 128, 128)] = block.astype(F32).T.astype(BF16)
    rows_ref[...] = wd_ref[...].astype(F32)
    for d in range(2):
        for p in range(2):
            for h in range(4):
                block = rows_ref[pl.ds(d * 4 + h % 2 * 2 + p, 64, stride=8), :].astype(BF16)
                d_ref[2 * d + p, pl.ds(h * 64, 64), pl.ds(h // 2 * 128, 128)] = block
                d_ref[2 * d + p, pl.ds(h * 64, 64), pl.ds(128 - h // 2 * 128, 128)] = jnp.zeros_like(block)
    rows_ref[pl.ds(0, 128), :] = jnp.zeros((128, 128), F32)
    rows_ref[pl.ds(0, 4), :] = head_ref[...].astype(F32)
    wht = rows_ref[pl.ds(0, 128), :]
    wht_ref[...] = wht.astype(BF16)
    wh_ref[...] = wht.T.astype(BF16)
    to = lax.broadcasted_iota(jnp.int32, (1, 256), 1)
    source = to // 4 % 2 * 512 + to % 2 * 256 + (to // 128 * 16 + to // 8 % 16) * 8 + to // 2 % 2
    perm_ref[...] = jnp.where(lax.broadcasted_iota(jnp.int32, (1024, 256), 0) == source, 1.0, 0.0).astype(BF16)


def prepare(w2, w3, wd, wh):
    wide = ((T, 9 * T), BF16)
    square = ((128, 128), BF16)
    return call(
        prepare_kernel,
        [wide] * 4 + [((1024, 256), BF16), ((4, T, T), BF16), square, square],
        w2, w3, wd, wh,
        scratch=[pltpu.VMEM((512, 128), F32)],
    )


def second_kernel(where_ref, one_ref, a_ref, two_ref, f2_ref, wd_ref, h_ref, a3_ref, b_ref):
    for n in range(CROPS):
        lo, hi = sorted_out(where_ref, one_ref[n], two_ref[n])
        planes = (lo, a_ref[n, 0], a_ref[n, 1], hi)
        for k, plane in enumerate(planes):
            put_three(b_ref, k * 3 * T, three_two(plane))
        for d in range(2):
            h = rectified(dot(f2_ref[...], b_ref[pl.ds(d * 3 * T, 9 * T), :])).astype(BF16)
            for p in range(2):
                h_ref[2 * d + p, :, pl.ds(n * 128, 128)] = h[:, p * 128 : (p + 1) * 128]
    total = dot_tn(wd_ref[0], h_ref[0])
    for k in range(1, 4):
        total += dot_tn(wd_ref[k], h_ref[k])
    a3_ref[...] = rectified(total).astype(BF16)


def second(where, one, a, two, f2, wd):
    return call(
        second_kernel,
        [((4, T, T), BF16), ((T, T), BF16)],
        where, one, a, two, f2, wd,
        scratch=[pltpu.VMEM((12 * T, T), BF16)],
    )


def head_kernel(scale, where_ref, one_ref, a_ref, two_ref, f3_ref, wh_ref, wht_ref, marks_ref, gz_ref, gh_ref, b_ref):
    lo, hi = sorted_out(where_ref, one_ref[...], two_ref[...])
    for k, plane in enumerate((lo, a_ref[...], hi)):
        put_three(b_ref, k * 3 * T, three_three(plane))
    top = rectified(dot(f3_ref[...], b_ref[...])).astype(BF16)
    row = lax.broadcasted_iota(jnp.int32, (128, T), 0)
    total = jnp.zeros((128, 128), F32)
    for h in range(2):
        mine = top[h * 128 : (h + 1) * 128]
        logits = dot(wht_ref[...], mine)
        powers = jnp.where(row < 4, jnp.exp(logits), 0.0)
        share = powers / jnp.sum(powers, axis=0, keepdims=True)
        chosen = jnp.where(row == marks_ref[pl.ds(h, 1), :], 1.0, 0.0)
        g = jnp.where(row < 4, (share - chosen) * scale, 0.0).astype(BF16)
        total += dot_nt(mine, g)
        gz_ref[pl.ds(h * 128, 128), :] = (dot(wh_ref[...], g) * slope(mine)).astype(BF16)
    gh_ref[...] = total


def head(where, one, a, two, f3, wh, wht, marks, scale):
    return call(
        functools.partial(head_kernel, scale),
        [((T, T), BF16), ((128, 128), F32)],
        where, one, a, two, f3, wh, wht, marks,
        scratch=[pltpu.VMEM((9 * T, T), BF16)],
    )


def weight_three_kernel(where_ref, g_ref, one_ref, a_ref, two_ref, out_ref, s_ref):
    put_three(s_ref, 0, three_three(g_ref[...]))
    lo, hi = sorted_out(where_ref, one_ref[...], two_ref[...])
    for d, a in enumerate((lo, a_ref[...], hi)):
        for j in range(3):
            t = dot_nt(s_ref[pl.ds((2 - j) * T, T), :], a)
            out_ref[d * 9 + j] = t[128:, :128]
            out_ref[d * 9 + 3 + j] = t[:128, :128] + t[128:, 128:]
            out_ref[d * 9 + 6 + j] = t[:128, 128:]


def weight_three(where, g, one, a, two):
    return call(
        weight_three_kernel,
        [((27, 128, 128), F32)],
        where, g, one, a, two,
        scratch=[pltpu.VMEM((3 * T, T), BF16)],
    )[0]


def middle_kernel(
    where_ref, one_ref, g_ref, two_ref, b3_ref, a3_ref, h_ref, wd_ref, gz2_ref, gone_ref, gtwo_ref, gd_ref, b_ref
):
    lo, hi = sorted_out(where_ref, one_ref[...], two_ref[...])
    for k, plane in enumerate((lo, g_ref[...], hi)):
        put_three(b_ref, k * 3 * T, three_three(plane))
    gy = (dot(b3_ref[...], b_ref[...]) * slope(a3_ref[...])).astype(BF16)
    for d in range(2):
        for p in range(2):
            k = 2 * d + p
            q = (dot(wd_ref[k], gy) * slope(h_ref[k])).astype(BF16)
            for n in range(CROPS):
                gz2_ref[n, d, :, pl.ds(p * 128, 128)] = q[:, n * 128 : (n + 1) * 128]
    even = where_ref[1] == 0
    for n in range(CROPS):
        gone_ref[n] = jnp.where(even, gz2_ref[n, 1], gz2_ref[n, 0])
        gtwo_ref[n] = jnp.where(even, gz2_ref[n, 0], gz2_ref[n, 1])
    for k in range(4):
        gd_ref[k] = dot_nt(gy[:128], h_ref[k, :128]) + dot_nt(gy[128:], h_ref[k, 128:])


def middle(where, one, g, two, b3, a3, h, wd):
    return call(
        middle_kernel,
        [((CROPS, 2, T, T), BF16), ((CROPS, T, T), BF16), ((CROPS, T, T), BF16), ((4, 128, 128), F32)],
        where, one, g, two, b3, a3, h, wd,
        scratch=[pltpu.VMEM((9 * T, T), BF16)],
    )


def weight_two_kernel(where_ref, g_ref, one_ref, a_ref, two_ref, out_ref, gs_ref, as_ref):
    for n in range(CROPS):
        lo, hi = sorted_out(where_ref, one_ref[n], two_ref[n])
        planes = (lo, a_ref[n, 0], a_ref[n, 1], hi)
        for d in range(2):
            at = (2 * n + d) * T
            for j, (left, right) in enumerate(three_two(g_ref[n, d])):
                gs_ref[2 - j, :, pl.ds(at, 128)] = left
                gs_ref[2 - j, :, pl.ds(at + 128, 128)] = right
            for k in range(3):
                as_ref[k, :, pl.ds(at, T)] = planes[d + k]
    low = lax.broadcasted_iota(jnp.int32, (64, 128), 1) < 64
    block = (lax.broadcasted_iota(jnp.int32, (64, 128), 1) // 32) % 2 == 0
    sums = {}
    for d in range(3):
        for j in range(3):
            t = dot_nt(gs_ref[j], as_ref[d])
            q = lambda r, c: t[r * 64 : (r + 1) * 64, c * 128 : (c + 1) * 128]
            sums[d, 0, j] = jnp.where(low, q(1, 0) + q(3, 1), q(2, 0))
            sums[d, 1, j] = jnp.where(low, q(0, 0) + q(2, 1), q(1, 0) + q(3, 1))
            sums[d, 2, j] = jnp.where(low, q(1, 1), q(0, 0) + q(2, 1))
        for h in range(3):
            for j in range(3):
                s = sums[d, h, j]
                sums[d, h, j] = s + pltpu.roll(s, 64, 1)
    taps = [sums[t // 9, t // 3 % 3, t % 3] for t in range(27)] + [jnp.zeros((64, 128), F32)]
    for g in range(7):
        four = taps[4 * g : 4 * g + 4]
        turned = [pltpu.roll(x, 32, 1) for x in four]
        out_ref[g, 0] = jnp.where(low, jnp.where(block, four[0], turned[1]), jnp.where(block, four[2], turned[3]))
        out_ref[g, 1] = jnp.where(low, jnp.where(block, turned[0], four[1]), jnp.where(block, turned[2], four[3]))


def weight_two(where, g, one, a, two):
    return call(
        weight_two_kernel,
        [((7, 2, 64, 128), F32)],
        where, g, one, a, two,
        scratch=[pltpu.VMEM((3, T, 4 * T), BF16), pltpu.VMEM((3, T, 4 * T), BF16)],
    )[0]


def pack_kernel(w3_ref, d3_ref, w2_ref, gh_ref, out_ref):
    for t in range(27):
        out_ref[pl.ds(t, 128, stride=ROWS), :] = w3_ref[t]
    for k in range(4):
        out_ref[pl.ds(DOWN3 + k, 128, stride=ROWS), :] = d3_ref[k]
    for half in range(2):
        for g in range(7):
            out_ref[pl.ds(half * ROWS + CONV2 + g, 64, stride=2 * ROWS), :] = w2_ref[g, half]
    out_ref[pl.ds(DOWN2, 128, stride=ROWS), :] = jnp.zeros((128, 128), F32)
    out_ref[pl.ds(HEAD, 128, stride=ROWS), :] = gh_ref[...]


def packed(*args):
    return call(pack_kernel, [((128 * ROWS, 128), F32)], *args)[0]


def last_kernel(
    where_ref, one_ref, g_ref, two_ref, b2_ref, a_ref, vp_ref, perm_ref, pack_ref, out_ref, b_ref, t_ref, d_ref
):
    for n in range(CROPS):
        lo, hi = sorted_out(where_ref, one_ref[n], two_ref[n])
        planes = (lo, g_ref[n, 0], g_ref[n, 1], hi)
        for k, plane in enumerate(planes):
            put_three(b_ref, k * 3 * T, three_two(plane))
        for d in range(2):
            gy = (dot(b2_ref[...], b_ref[pl.ds(d * 3 * T, 9 * T), :]) * slope(a_ref[n, d])).astype(BF16)
            t = dot_nt(gy, vp_ref[n, d])
            if n + d == 0:
                t_ref[...] = t
            else:
                t_ref[...] += t
    pairs = []
    lane = lax.broadcasted_iota(jnp.int32, (64, 128), 1)
    for tile in range(8):
        at = pl.ds(tile * 128, 128)
        x = jnp.zeros((64, 128), F32)
        for h in range(4):
            x = jnp.where(lane % 8 // 2 == h, t_ref[pl.ds(h * 64, 64), at], x)
        x = x + pltpu.roll(x, 126, 1)
        x = x + pltpu.roll(x, 124, 1)
        pairs.append(x.astype(BF16))
    down = dot(jnp.concatenate(pairs, axis=1), perm_ref[...])
    for half in range(2):
        d_ref[pl.ds(half * ROWS + DOWN2, 64, stride=2 * ROWS), :] = down[:, half * 128 : (half + 1) * 128]
    row = lax.broadcasted_iota(jnp.int32, (ROWS, 128), 0)
    for j in range(128):
        at = pl.ds(j * ROWS, ROWS)
        out_ref[at, :] = jnp.where(row == DOWN2, d_ref[at, :], pack_ref[at, :]).astype(BF16)


def last(*args):
    return call(
        last_kernel,
        [((128 * ROWS, 128), BF16)],
        *args,
        scratch=[pltpu.VMEM((12 * T, T), BF16), pltpu.VMEM((T, 1024), F32), pltpu.VMEM((128 * ROWS, 128), F32)],
    )[0]


def swapped(one, two):
    count = lax.axis_size("space")
    near = [(i, i ^ 1) for i in range(count)]
    far = [(i, ((i + 1) ^ 1) - 1) for i in range(1, count - 1)]
    two = lax.ppermute(two, "space", far)
    return lax.ppermute(one, "space", near), two


def unpack(sums):
    return (
        sums[DOWN2],
        sums[CONV2:DOWN2].reshape(28, 32)[:27].T.reshape(-1),
        sums[DOWN3:CONV2].reshape(2, 2, 2, 64).transpose(3, 0, 2, 1).reshape(-1),
        sums[:27].T.reshape(-1),
        sums[HEAD, :4],
    )


def finish(pack):
    terms = lax.all_to_all(pack, ("section", "space"), 0, 0, tiled=True)
    return unpack(jnp.sum(terms.astype(F32), axis=0))


def per_device(volume, labels, down_weight_two, w_conv_two, down_weight_three, w_conv_three, w_head):
    count = lax.axis_size("space")
    voxels = labels.shape[0] * labels.shape[1] * count * labels.shape[2] * labels.shape[3]
    scale = 1.0 / math.sqrt(voxels)
    sec = lax.axis_index("section").astype(jnp.int32)
    where = jnp.stack([sec, lax.axis_index("space").astype(jnp.int32) % 2])

    w1 = down_weight_two.transpose(1, 2, 3, 4, 0).reshape(256, 64)
    wd = down_weight_three.transpose(1, 2, 3, 4, 0).reshape(512, 128)
    w2 = w_conv_two.transpose(2, 3, 4, 0, 1).reshape(27, 64, 64)
    w2 = jnp.concatenate([w2, w2], axis=2)
    w3 = w_conv_three.transpose(2, 3, 4, 0, 1).reshape(27, 128, 128)
    marks = lax.dynamic_slice_in_dim(labels[:, 0], CROPS * sec, CROPS, axis=0)
    marks = marks.transpose(1, 0, 2).reshape(2, 256)

    vp, a2, one, two = first(where, volume, w1)
    a2_one, a2_two = swapped(one, two)
    f2, b2, f3, b3, perm, wd, wh, wht = prepare(w2, w3, wd, w_head.T)
    h2, a3 = second(where, a2_one, a2, a2_two, f2, wd)
    a3_one, a3_two = swapped(a3, a3)
    gz4, gh = head(where, a3_one, a3, a3_two, f3, wh, wht, marks, scale)
    gz4_one, gz4_two = swapped(gz4, gz4)
    gw3 = weight_three(where, gz4, a3_one, a3, a3_two)
    gz4_one, gz4_two, gw3 = lax.optimization_barrier((gz4_one, gz4_two, gw3))
    gz2, one, two, gd3 = middle(where, gz4_one, gz4, gz4_two, b3, a3, h2, wd)
    gz2_one, gz2_two = swapped(one, two)
    gw2 = weight_two(where, gz2, a2_one, a2, a2_two)
    pack = packed(gw3, gd3, gw2, gh)
    pack = last(where, gz2_one, gz2, gz2_two, b2, a2, vp, perm, pack)
    return finish(pack.reshape(128, ROWS, 128))


def solution(mesh):
    whole = P(("section", "space"))
    return jax.shard_map(
        per_device,
        mesh=mesh,
        in_specs=(P(None, None, "space", None, None), P(None, "space", None, None), P(), P(), P(), P(), P()),
        out_specs=(whole,) * 5,
        check_vma=False,
    )
```

```python
import functools
import math

import jax
import jax.numpy as jnp
from jax import lax
from jax.experimental import pallas as pl
from jax.experimental.pallas import tpu as pltpu
from jax.sharding import PartitionSpec as P


F32 = jnp.float32
BF16 = jnp.bfloat16
SHIFT = math.log(2.0)
CROPS = 2
T = 256
ROWS = 40
DOWN3, CONV2, DOWN2 = 27, 31, 38


def params(megabytes=24):
    return pltpu.CompilerParams(vmem_limit_bytes=megabytes << 20)


def rectified(v):
    return jnp.maximum(v, 0.0) + jnp.log1p(jnp.exp(-jnp.abs(v))) - SHIFT


def slope(stored):
    return 1.0 - 0.5 * jnp.exp(-stored.astype(F32))


def dot(a, b):
    return jnp.dot(a, b, preferred_element_type=F32)


def dot_tn(a, b):
    return lax.dot_general(a, b, (((0,), (0,)), ((), ())), preferred_element_type=F32)


def dot_nt(a, b):
    return lax.dot_general(a, b, (((1,), (1,)), ((), ())), preferred_element_type=F32)


def moved(x, by):
    x = x.astype(F32)
    lane = lax.broadcasted_iota(jnp.int32, x.shape, 1)
    edge = 0 if by == 1 else 127
    return jnp.where(lane == edge, 0.0, pltpu.roll(x, by % 128, 1)).astype(BF16)


def three_two(x):
    even, odd = x[:, :128], x[:, 128:]
    return ((moved(odd, 1), even), (even, odd), (odd, moved(even, -1)))


def three_three(x):
    first, second = x[:, :128], x[:, 128:]
    return ((moved(first, 1), moved(second, 1)), (first, second), (moved(first, -1), moved(second, -1)))


def put_three(ref, row, shifted):
    for j, (left, right) in enumerate(shifted):
        ref[pl.ds(row + j * T, T), 0:128] = left
        ref[pl.ds(row + j * T, T), 128:256] = right


def call(kernel, outs, *args, scratch=(), far=()):
    spec = pl.BlockSpec(memory_space=pltpu.VMEM)
    scalar = pl.BlockSpec(memory_space=pltpu.SMEM)
    remote = pl.BlockSpec(memory_space=pl.ANY)
    return pl.pallas_call(
        kernel,
        in_specs=[remote if i in far else scalar if a.dtype == jnp.int32 and a.ndim == 1 else spec for i, a in enumerate(args)],
        out_specs=[spec] * len(outs),
        out_shape=[space(s, d) for s, d, space in outs],
        scratch_shapes=list(scratch),
        compiler_params=params(),
    )(*[pltpu.with_memory_space_constraint(a, pltpu.HBM) if i in far else a for i, a in enumerate(args)])


def sorted_out(where_ref, one, two):
    even = where_ref[1] == 0
    return jnp.where(even, two, one), jnp.where(even, one, two)


def first_kernel(where_ref, vol_ref, w_ref, vp_ref, a_ref, one_ref, two_ref, sort_ref, wt_ref):
    @pl.when(pl.program_id(0) == 0)
    def _():
        to = lax.broadcasted_iota(jnp.int32, (1, 512), 1)
        source = (to % 128) * 4 + (to // 128) % 2 * 2 + to // 256
        sort_ref[...] = jnp.where(lax.broadcasted_iota(jnp.int32, (512, 512), 0) == source, 1.0, 0.0).astype(BF16)
        to = lax.broadcasted_iota(jnp.int32, (1, 1024), 1)
        height = to % 8
        source = to // 8 % 32 * 8 + to // 512 * 4 + height % 2 * 2 + to // 256 % 2
        pick = jnp.where(lax.broadcasted_iota(jnp.int32, (256, 1024), 0) == source, 1.0, 0.0).astype(BF16)
        w = dot_tn(w_ref[...], pick)
        for h in range(4):
            wt_ref[pl.ds(h * 64, 64), :] = jnp.where(height // 2 == h, w, 0.0).astype(BF16)

    for d in range(2):
        v = vol_ref[0, :, d].astype(F32).reshape(256, 512).astype(BF16)
        s = dot(v, sort_ref[...]).astype(BF16)
        vp_ref[0, 0, pl.ds(d * 512, 256), :] = s[:, :256]
        vp_ref[0, 0, pl.ds(d * 512 + 256, 256), :] = s[:, 256:]
    a = rectified(dot(wt_ref[...], vp_ref[0, 0])).astype(BF16)
    a_ref[0, 0] = a
    upper = pl.program_id(0) % 2

    @pl.when(upper == where_ref[1])
    def _():
        two_ref[0] = a

    @pl.when(upper != where_ref[1])
    def _():
        one_ref[0] = a


def first(where, volume, w1):
    half = pl.BlockSpec((1, T, T), lambda i, s: (i // 2, 0, 0))
    return pl.pallas_call(
        first_kernel,
        grid_spec=pltpu.PrefetchScalarGridSpec(
            num_scalar_prefetch=1,
            grid=(4,),
            in_specs=[
                pl.BlockSpec((1, 32, 2, 8, 512), lambda i, s: (2 * s[0] + i // 2, 0, i % 2, 0, 0)),
                pl.BlockSpec((256, 64), lambda i, s: (0, 0)),
            ],
            out_specs=[
                pl.BlockSpec((1, 1, 1024, 256), lambda i, s: (i // 2, i % 2, 0, 0)),
                pl.BlockSpec((1, 1, 256, 256), lambda i, s: (i // 2, i % 2, 0, 0)),
                half,
                half,
            ],
            scratch_shapes=[pltpu.VMEM((512, 512), BF16), pltpu.VMEM((256, 1024), BF16)],
        ),
        out_shape=[
            pltpu.HBM((CROPS, 2, 1024, 256), BF16),
            pltpu.VMEM((CROPS, 2, 256, 256), BF16),
            pltpu.VMEM((CROPS, 256, 256), BF16),
            pltpu.VMEM((CROPS, 256, 256), BF16),
        ],
        compiler_params=params(),
    )(where, pltpu.with_memory_space_constraint(volume, pltpu.HBM), pltpu.with_memory_space_constraint(w1, pltpu.HBM))


def prepare_kernel(
    w2_ref, w3_ref, wd_ref, head_ref, f2_ref, b2_ref, f3_ref, b3_ref, perm_ref, d_ref, wh_ref, rows_ref
):
    low = lax.broadcasted_iota(jnp.int32, (64, 128), 1) < 64
    zero = jnp.zeros((64, 128), F32)
    for d in range(3):
        for j in range(3):
            at = (d * 3 + j) * T
            back = (8 - d * 3 - j) * T
            w = [w2_ref[d * 9 + h * 3 + j].astype(F32) for h in range(3)]
            pairs = {
                (0, 0): jnp.where(low, w[1], w[2]),
                (0, 1): zero,
                (1, 0): jnp.where(low, w[0], w[1]),
                (1, 1): jnp.where(low, w[2], 0.0),
                (2, 0): jnp.where(low, 0.0, w[0]),
                (2, 1): jnp.where(low, w[1], w[2]),
                (3, 0): zero,
                (3, 1): jnp.where(low, w[0], w[1]),
            }
            for (row, col), block in pairs.items():
                f2_ref[pl.ds(row * 64, 64), pl.ds(at + col * 128, 128)] = block.astype(BF16)
            b2_ref[:, pl.ds(back, T)] = f2_ref[:, pl.ds(at, T)].astype(F32).T.astype(BF16)
            for row in range(2):
                for col in range(2):
                    block = w3_ref[d * 9 + (col - row + 1) * 3 + j]
                    f3_ref[pl.ds(row * 128, 128), pl.ds(at + col * 128, 128)] = block
                    b3_ref[pl.ds(col * 128, 128), pl.ds(back + row * 128, 128)] = block.astype(F32).T.astype(BF16)
    rows_ref[...] = wd_ref[...].astype(F32)
    for d in range(2):
        for p in range(2):
            for h in range(4):
                block = rows_ref[pl.ds(d * 4 + h % 2 * 2 + p, 64, stride=8), :].astype(BF16)
                d_ref[2 * d + p, pl.ds(h * 64, 64), pl.ds(h // 2 * 128, 128)] = block
                d_ref[2 * d + p, pl.ds(h * 64, 64), pl.ds(128 - h // 2 * 128, 128)] = jnp.zeros_like(block)
    rows_ref[pl.ds(0, 128), :] = jnp.zeros((128, 128), F32)
    rows_ref[pl.ds(0, 4), :] = head_ref[...].astype(F32)
    wht = rows_ref[pl.ds(0, 128), :]
    wh_ref[pl.ds(0, 128), :] = wht.T.astype(BF16)
    wh_ref[pl.ds(128, 128), :] = wht.astype(BF16)
    to = lax.broadcasted_iota(jnp.int32, (1, 256), 1)
    source = to // 4 % 2 * 512 + to % 2 * 256 + (to // 128 * 16 + to // 8 % 16) * 8 + to // 2 % 2
    perm_ref[...] = jnp.where(lax.broadcasted_iota(jnp.int32, (1024, 256), 0) == source, 1.0, 0.0).astype(BF16)


def prepare(w2, w3, wd, wh):
    def wide(space):
        return ((T, 9 * T), BF16, space)

    return call(
        prepare_kernel,
        [wide(pltpu.VMEM), wide(pltpu.HBM), wide(pltpu.HBM), wide(pltpu.HBM)]
        + [((1024, 256), BF16, pltpu.HBM), ((4, T, T), BF16, pltpu.VMEM), ((256, 128), BF16, pltpu.HBM)],
        w2, w3, wd, wh,
        scratch=[pltpu.VMEM((512, 128), F32)],
    )


def second_kernel(where_ref, one_ref, a_ref, two_ref, f2_ref, wd_ref, h_ref, a3_ref, b_ref):
    for n in range(CROPS):
        lo, hi = sorted_out(where_ref, one_ref[n], two_ref[n])
        planes = (lo, a_ref[n, 0], a_ref[n, 1], hi)
        for k, plane in enumerate(planes):
            put_three(b_ref, k * 3 * T, three_two(plane))
        for d in range(2):
            h = rectified(dot(f2_ref[...], b_ref[pl.ds(d * 3 * T, 9 * T), :])).astype(BF16)
            for p in range(2):
                h_ref[2 * d + p, :, pl.ds(n * 128, 128)] = h[:, p * 128 : (p + 1) * 128]
    total = dot_tn(wd_ref[0], h_ref[0])
    for k in range(1, 4):
        total += dot_tn(wd_ref[k], h_ref[k])
    a3_ref[...] = rectified(total).astype(BF16)


def second(where, one, a, two, f2, wd):
    return call(
        second_kernel,
        [((4, T, T), BF16, pltpu.HBM), ((T, T), BF16, pltpu.VMEM)],
        where, one, a, two, f2, wd,
        scratch=[pltpu.VMEM((12 * T, T), BF16)],
    )


def head_kernel(
    scale, where_ref, one_ref, a_ref, two_ref, f3_far, wh_far, marks_ref, gz_ref, gh_ref, b_ref, f3_ref, wh_ref, sems
):
    fetches = [
        pltpu.make_async_copy(f3_far, f3_ref, sems.at[0]),
        pltpu.make_async_copy(wh_far, wh_ref, sems.at[1]),
    ]
    for fetch in fetches:
        fetch.start()
    lo, hi = sorted_out(where_ref, one_ref[...], two_ref[...])
    for k, plane in enumerate((lo, a_ref[...], hi)):
        put_three(b_ref, k * 3 * T, three_three(plane))
    for fetch in fetches:
        fetch.wait()
    top = rectified(dot(f3_ref[...], b_ref[...])).astype(BF16)
    row = lax.broadcasted_iota(jnp.int32, (128, T), 0)
    total = jnp.zeros((128, 128), F32)
    for h in range(2):
        mine = top[h * 128 : (h + 1) * 128]
        logits = dot(wh_ref[pl.ds(128, 128), :], mine)
        powers = jnp.where(row < 4, jnp.exp(logits), 0.0)
        share = powers / jnp.sum(powers, axis=0, keepdims=True)
        chosen = jnp.where(row == marks_ref[pl.ds(h, 1), :], 1.0, 0.0)
        g = jnp.where(row < 4, (share - chosen) * scale, 0.0).astype(BF16)
        total += dot_nt(mine, g)
        gz_ref[pl.ds(h * 128, 128), :] = (dot(wh_ref[pl.ds(0, 128), :], g) * slope(mine)).astype(BF16)
    gh_ref[...] = total


def head(where, one, a, two, f3, wh, marks, scale):
    return call(
        functools.partial(head_kernel, scale),
        [((T, T), BF16, pltpu.VMEM), ((128, 128), F32, pltpu.VMEM)],
        where, one, a, two, f3, wh, marks,
        scratch=[
            pltpu.VMEM((9 * T, T), BF16),
            pltpu.VMEM((T, 9 * T), BF16),
            pltpu.VMEM((256, 128), BF16),
            pltpu.SemaphoreType.DMA((2,)),
        ],
        far=(4, 5),
    )


def weight_three_kernel(where_ref, g_ref, one_ref, a_ref, two_ref, out_ref, s_ref):
    put_three(s_ref, 0, three_three(g_ref[...]))
    lo, hi = sorted_out(where_ref, one_ref[...], two_ref[...])
    for d, a in enumerate((lo, a_ref[...], hi)):
        for j in range(3):
            t = dot_nt(s_ref[pl.ds((2 - j) * T, T), :], a)
            out_ref[d * 9 + j] = t[128:, :128]
            out_ref[d * 9 + 3 + j] = t[:128, :128] + t[128:, 128:]
            out_ref[d * 9 + 6 + j] = t[:128, 128:]


def weight_three(where, g, one, a, two):
    return call(
        weight_three_kernel,
        [((27, 128, 128), F32, pltpu.VMEM)],
        where, g, one, a, two,
        scratch=[pltpu.VMEM((3 * T, T), BF16)],
    )[0]


def middle_kernel(
    where_ref, one_ref, g_ref, two_ref, b3_ref, a3_ref, h_ref, wd_ref, gz2_ref, gone_ref, gtwo_ref, gd_ref, b_ref
):
    lo, hi = sorted_out(where_ref, one_ref[...], two_ref[...])
    for k, plane in enumerate((lo, g_ref[...], hi)):
        put_three(b_ref, k * 3 * T, three_three(plane))
    gy = (dot(b3_ref[...], b_ref[...]) * slope(a3_ref[...])).astype(BF16)
    for d in range(2):
        for p in range(2):
            k = 2 * d + p
            q = (dot(wd_ref[k], gy) * slope(h_ref[k])).astype(BF16)
            for n in range(CROPS):
                gz2_ref[n, d, :, pl.ds(p * 128, 128)] = q[:, n * 128 : (n + 1) * 128]
    even = where_ref[1] == 0
    for n in range(CROPS):
        gone_ref[n] = jnp.where(even, gz2_ref[n, 1], gz2_ref[n, 0])
        gtwo_ref[n] = jnp.where(even, gz2_ref[n, 0], gz2_ref[n, 1])
    for k in range(4):
        gd_ref[k] = dot_nt(gy[:128], h_ref[k, :128]) + dot_nt(gy[128:], h_ref[k, 128:])


def middle(where, one, g, two, b3, a3, h, wd):
    return call(
        middle_kernel,
        [
            ((CROPS, 2, T, T), BF16, pltpu.VMEM),
            ((CROPS, T, T), BF16, pltpu.VMEM),
            ((CROPS, T, T), BF16, pltpu.VMEM),
            ((4, 128, 128), F32, pltpu.VMEM),
        ],
        where, one, g, two, b3, a3, h, wd,
        scratch=[pltpu.VMEM((9 * T, T), BF16)],
    )


def weight_two_kernel(where_ref, g_ref, one_ref, a_ref, two_ref, out_ref, gs_ref, as_ref):
    for n in range(CROPS):
        lo, hi = sorted_out(where_ref, one_ref[n], two_ref[n])
        planes = (lo, a_ref[n, 0], a_ref[n, 1], hi)
        for d in range(2):
            at = (2 * n + d) * T
            for j, (left, right) in enumerate(three_two(g_ref[n, d])):
                gs_ref[2 - j, :, pl.ds(at, 128)] = left
                gs_ref[2 - j, :, pl.ds(at + 128, 128)] = right
            for k in range(3):
                as_ref[k, :, pl.ds(at, T)] = planes[d + k]
    low = lax.broadcasted_iota(jnp.int32, (64, 128), 1) < 64
    block = (lax.broadcasted_iota(jnp.int32, (64, 128), 1) // 32) % 2 == 0
    sums = {}
    for d in range(3):
        for j in range(3):
            t = dot_nt(gs_ref[j], as_ref[d])
            q = lambda r, c: t[r * 64 : (r + 1) * 64, c * 128 : (c + 1) * 128]
            sums[d, 0, j] = jnp.where(low, q(1, 0) + q(3, 1), q(2, 0))
            sums[d, 1, j] = jnp.where(low, q(0, 0) + q(2, 1), q(1, 0) + q(3, 1))
            sums[d, 2, j] = jnp.where(low, q(1, 1), q(0, 0) + q(2, 1))
        for h in range(3):
            for j in range(3):
                s = sums[d, h, j]
                sums[d, h, j] = s + pltpu.roll(s, 64, 1)
    taps = [sums[t // 9, t // 3 % 3, t % 3] for t in range(27)] + [jnp.zeros((64, 128), F32)]
    for g in range(7):
        four = taps[4 * g : 4 * g + 4]
        turned = [pltpu.roll(x, 32, 1) for x in four]
        out_ref[g, 0] = jnp.where(low, jnp.where(block, four[0], turned[1]), jnp.where(block, four[2], turned[3]))
        out_ref[g, 1] = jnp.where(low, jnp.where(block, turned[0], four[1]), jnp.where(block, turned[2], four[3]))


def weight_two(where, g, one, a, two):
    return call(
        weight_two_kernel,
        [((7, 2, 64, 128), F32, pltpu.VMEM)],
        where, g, one, a, two,
        scratch=[pltpu.VMEM((3, T, 4 * T), BF16), pltpu.VMEM((3, T, 4 * T), BF16)],
    )[0]


def pack_kernel(where_ref, w3_ref, d3_ref, w2_ref, gh_ref, keep_ref, send_ref, pack_ref):
    for t in range(27):
        pack_ref[pl.ds(t, 128, stride=ROWS), :] = w3_ref[t]
    for k in range(4):
        pack_ref[pl.ds(DOWN3 + k, 128, stride=ROWS), :] = d3_ref[k]
    lane = lax.broadcasted_iota(jnp.int32, (64, 128), 1)
    for half in range(2):
        for g in range(6):
            pack_ref[pl.ds(half * ROWS + CONV2 + g, 64, stride=2 * ROWS), :] = w2_ref[g, half]
        heads = pltpu.roll(gh_ref[pl.ds(half, 64, stride=2), :], 96, 1)
        pack_ref[pl.ds(half * ROWS + CONV2 + 6, 64, stride=2 * ROWS), :] = jnp.where(lane < 96, w2_ref[6, half], heads)
    zero = jnp.zeros((128, 128), F32)
    pack_ref[pl.ds(DOWN2, 128, stride=ROWS), :] = zero
    pack_ref[pl.ds(DOWN2 + 1, 128, stride=ROWS), :] = zero
    keep_ref[...] = pack_ref[pl.ds(pl.multiple_of(where_ref[0] * 64 * ROWS, 64 * ROWS), 64 * ROWS), :]
    send_ref[...] = pack_ref[pl.ds(pl.multiple_of((1 - where_ref[0]) * 64 * ROWS, 64 * ROWS), 64 * ROWS), :].astype(BF16)


def packed(*args):
    half = (64 * ROWS, 128)
    return call(
        pack_kernel,
        [(half, F32, pltpu.VMEM), (half, BF16, pltpu.VMEM)],
        *args,
        scratch=[pltpu.VMEM((128 * ROWS, 128), F32)],
    )


def last_kernel(
    where_ref, one_ref, g_ref, two_ref, b2_far, a_ref, vp_far, perm_far, keep_ref, came_ref, out_ref, b_ref, t_ref, d_ref,
    down_ref, b2_ref, vp_ref, perm_ref, sems
):
    fetches = [
        pltpu.make_async_copy(far, ref, sems.at[i])
        for i, (far, ref) in enumerate(((b2_far, b2_ref), (vp_far, vp_ref), (perm_far, perm_ref)))
    ]
    for fetch in fetches:
        fetch.start()
    for n in range(CROPS):
        lo, hi = sorted_out(where_ref, one_ref[n], two_ref[n])
        planes = (lo, g_ref[n, 0], g_ref[n, 1], hi)
        for k, plane in enumerate(planes):
            put_three(b_ref, k * 3 * T, three_two(plane))
        for d in range(2):
            if n + d == 0:
                fetches[0].wait()
            gy = (dot(b2_ref[...], b_ref[pl.ds(d * 3 * T, 9 * T), :]) * slope(a_ref[n, d])).astype(BF16)
            if n + d == 0:
                fetches[1].wait()
            t = dot_nt(gy, vp_ref[n, d])
            if n + d == 0:
                t_ref[...] = t
            else:
                t_ref[...] += t
    pairs = []
    lane = lax.broadcasted_iota(jnp.int32, (64, 128), 1)
    for tile in range(8):
        at = pl.ds(tile * 128, 128)
        x = jnp.zeros((64, 128), F32)
        for h in range(4):
            x = jnp.where(lane % 8 // 2 == h, t_ref[pl.ds(h * 64, 64), at], x)
        x = x + pltpu.roll(x, 126, 1)
        x = x + pltpu.roll(x, 124, 1)
        pairs.append(x.astype(BF16))
    fetches[2].wait()
    down_ref[...] = dot(jnp.concatenate(pairs, axis=1), perm_ref[...])
    for k, sec in enumerate((where_ref[0], 1 - where_ref[0])):
        mine = pl.ds(pl.multiple_of(sec * 32, 32), 32)
        for half in range(2):
            to = pl.ds(half * ROWS + DOWN2 + k, 32, stride=2 * ROWS)
            d_ref[to, :] = down_ref[mine, half * 128 : (half + 1) * 128]
    row = lax.broadcasted_iota(jnp.int32, (ROWS, 128), 0)
    for j in range(64):
        at = pl.ds(j * ROWS, ROWS)
        both = keep_ref[at, :] + came_ref[at, :].astype(F32)
        out_ref[at, :] = jnp.where(row >= DOWN2, d_ref[at, :], both).astype(BF16)


def last(*args):
    return call(
        last_kernel,
        [((64 * ROWS, 128), BF16, pltpu.VMEM)],
        *args,
        scratch=[
            pltpu.VMEM((12 * T, T), BF16),
            pltpu.VMEM((T, 1024), F32),
            pltpu.VMEM((64 * ROWS, 128), F32),
            pltpu.VMEM((64, 256), F32),
            pltpu.VMEM((T, 9 * T), BF16),
            pltpu.VMEM((CROPS, 2, 1024, T), BF16),
            pltpu.VMEM((1024, 256), BF16),
            pltpu.SemaphoreType.DMA((3,)),
        ],
        far=(4, 6, 7),
    )[0]


def swapped(one, two):
    count = lax.axis_size("space")
    near = [(i, i ^ 1) for i in range(count)]
    far = [(i, ((i + 1) ^ 1) - 1) for i in range(1, count - 1)]
    two = lax.ppermute(two, "space", far)
    return lax.ppermute(one, "space", near), two


def partner(x):
    return lax.ppermute(x, "section", [(0, 1), (1, 0)])


def unpack(sums, down):
    return (
        down,
        sums[CONV2:DOWN2].reshape(28, 32)[:27].T.reshape(-1),
        sums[DOWN3:CONV2].reshape(2, 2, 2, 64).transpose(3, 0, 2, 1).reshape(-1),
        sums[:27].T.reshape(-1),
        sums[DOWN2 - 1, 96:100],
    )


def finish(pack):
    terms = lax.all_to_all(pack, "space", 0, 0, tiled=True)
    sums = jnp.sum(terms.astype(F32), axis=0)
    return unpack(sums, sums[DOWN2] + partner(sums[DOWN2 + 1]))


def per_device(volume, labels, down_weight_two, w_conv_two, down_weight_three, w_conv_three, w_head):
    count = lax.axis_size("space")
    voxels = labels.shape[0] * labels.shape[1] * count * labels.shape[2] * labels.shape[3]
    scale = 1.0 / math.sqrt(voxels)
    sec = lax.axis_index("section").astype(jnp.int32)
    where = jnp.stack([sec, lax.axis_index("space").astype(jnp.int32) % 2])

    w1 = down_weight_two.transpose(1, 2, 3, 4, 0).reshape(256, 64)
    wd = down_weight_three.transpose(1, 2, 3, 4, 0).reshape(512, 128)
    w2 = w_conv_two.transpose(2, 3, 4, 0, 1).reshape(27, 64, 64)
    w2 = jnp.concatenate([w2, w2], axis=2)
    w3 = w_conv_three.transpose(2, 3, 4, 0, 1).reshape(27, 128, 128)
    marks = lax.dynamic_slice_in_dim(labels[:, 0], CROPS * sec, CROPS, axis=0)
    marks = marks.transpose(1, 0, 2).reshape(2, 256)

    vp, a2, one, two = first(where, volume, w1)
    a2_one, a2_two = swapped(one, two)
    f2, b2, f3, b3, perm, wd, wh = prepare(w2, w3, wd, w_head.T)
    h2, a3 = second(where, a2_one, a2, a2_two, f2, wd)
    a3_one, a3_two = swapped(a3, a3)
    gz4, gh = head(where, a3_one, a3, a3_two, f3, wh, marks, scale)
    gz4_one, gz4_two = swapped(gz4, gz4)
    gw3 = weight_three(where, gz4, a3_one, a3, a3_two)
    gz4_one, gz4_two, gw3 = lax.optimization_barrier((gz4_one, gz4_two, gw3))
    gz2, one, two, gd3 = middle(where, gz4_one, gz4, gz4_two, b3, a3, h2, wd)
    gz2_one, gz2_two = swapped(one, two)
    gw2 = weight_two(where, gz2, a2_one, a2, a2_two)
    keep, send = packed(where, gw3, gd3, gw2, gh)
    came = partner(send)
    pack = last(where, gz2_one, gz2, gz2_two, b2, a2, vp, perm, keep, came)
    return finish(pack.reshape(64, ROWS, 128))


def solution(mesh):
    whole = P(("section", "space"))
    return jax.shard_map(
        per_device,
        mesh=mesh,
        in_specs=(P(None, None, "space", None, None), P(None, "space", None, None), P(), P(), P(), P(), P()),
        out_specs=(whole,) * 5,
        check_vma=False,
    )
```

```python
import functools
import math

import jax
import jax.numpy as jnp
from jax import lax
from jax.experimental import pallas as pl
from jax.experimental.pallas import tpu as pltpu
from jax.sharding import PartitionSpec as P


F32 = jnp.float32
BF16 = jnp.bfloat16
SHIFT = math.log(2.0)
CROPS = 2
T = 256
ROWS = 40
DOWN3, CONV2, DOWN2 = 27, 31, 38


def params(megabytes=24):
    return pltpu.CompilerParams(vmem_limit_bytes=megabytes << 20)


def rectified(v):
    return jnp.maximum(v, 0.0) + jnp.log1p(jnp.exp(-jnp.abs(v))) - SHIFT


def slope(stored):
    return 1.0 - 0.5 * jnp.exp(-stored.astype(F32))


def dot(a, b):
    return jnp.dot(a, b, preferred_element_type=F32)


def dot_tn(a, b):
    return lax.dot_general(a, b, (((0,), (0,)), ((), ())), preferred_element_type=F32)


def dot_nt(a, b):
    return lax.dot_general(a, b, (((1,), (1,)), ((), ())), preferred_element_type=F32)


def moved(x, by):
    x = x.astype(F32)
    lane = lax.broadcasted_iota(jnp.int32, x.shape, 1)
    edge = 0 if by == 1 else 127
    return jnp.where(lane == edge, 0.0, pltpu.roll(x, by % 128, 1)).astype(BF16)


def three_two(x):
    even, odd = x[:, :128], x[:, 128:]
    return ((moved(odd, 1), even), (even, odd), (odd, moved(even, -1)))


def three_three(x):
    first, second = x[:, :128], x[:, 128:]
    return ((moved(first, 1), moved(second, 1)), (first, second), (moved(first, -1), moved(second, -1)))


def put_three(ref, row, shifted):
    for j, (left, right) in enumerate(shifted):
        ref[pl.ds(row + j * T, T), 0:128] = left
        ref[pl.ds(row + j * T, T), 128:256] = right


def call(kernel, outs, *args, scratch=(), far=()):
    spec = pl.BlockSpec(memory_space=pltpu.VMEM)
    scalar = pl.BlockSpec(memory_space=pltpu.SMEM)
    remote = pl.BlockSpec(memory_space=pl.ANY)
    return pl.pallas_call(
        kernel,
        in_specs=[remote if i in far else scalar if a.dtype == jnp.int32 and a.ndim == 1 else spec for i, a in enumerate(args)],
        out_specs=[spec] * len(outs),
        out_shape=[space(s, d) for s, d, space in outs],
        scratch_shapes=list(scratch),
        compiler_params=params(),
    )(*[pltpu.with_memory_space_constraint(a, pltpu.HBM) if i in far else a for i, a in enumerate(args)])


def sorted_out(where_ref, one, two):
    even = where_ref[1] == 0
    return jnp.where(even, two, one), jnp.where(even, one, two)


def first_kernel(where_ref, vol_ref, w_ref, vp_ref, a_ref, one_ref, two_ref, sort_ref, wt_ref):
    @pl.when(pl.program_id(0) == 0)
    def _():
        to = lax.broadcasted_iota(jnp.int32, (1, 512), 1)
        source = (to % 128) * 4 + (to // 128) % 2 * 2 + to // 256
        sort_ref[...] = jnp.where(lax.broadcasted_iota(jnp.int32, (512, 512), 0) == source, 1.0, 0.0).astype(BF16)
        to = lax.broadcasted_iota(jnp.int32, (1, 1024), 1)
        height = to % 8
        source = to // 8 % 32 * 8 + to // 512 * 4 + height % 2 * 2 + to // 256 % 2
        pick = jnp.where(lax.broadcasted_iota(jnp.int32, (256, 1024), 0) == source, 1.0, 0.0).astype(BF16)
        w = dot_tn(w_ref[...], pick)
        for h in range(4):
            wt_ref[pl.ds(h * 64, 64), :] = jnp.where(height // 2 == h, w, 0.0).astype(BF16)

    for d in range(2):
        v = vol_ref[0, :, d].astype(F32).reshape(256, 512).astype(BF16)
        s = dot(v, sort_ref[...]).astype(BF16)
        vp_ref[0, 0, pl.ds(d * 512, 256), :] = s[:, :256]
        vp_ref[0, 0, pl.ds(d * 512 + 256, 256), :] = s[:, 256:]
    a = rectified(dot(wt_ref[...], vp_ref[0, 0])).astype(BF16)
    a_ref[0, 0] = a
    upper = pl.program_id(0) % 2

    @pl.when(upper == where_ref[1])
    def _():
        two_ref[0] = a

    @pl.when(upper != where_ref[1])
    def _():
        one_ref[0] = a


def first(where, volume, w1):
    half = pl.BlockSpec((1, T, T), lambda i, s: (i // 2, 0, 0))
    return pl.pallas_call(
        first_kernel,
        grid_spec=pltpu.PrefetchScalarGridSpec(
            num_scalar_prefetch=1,
            grid=(4,),
            in_specs=[
                pl.BlockSpec((1, 32, 2, 8, 512), lambda i, s: (2 * s[0] + i // 2, 0, i % 2, 0, 0)),
                pl.BlockSpec((256, 64), lambda i, s: (0, 0)),
            ],
            out_specs=[
                pl.BlockSpec((1, 1, 1024, 256), lambda i, s: (i // 2, i % 2, 0, 0)),
                pl.BlockSpec((1, 1, 256, 256), lambda i, s: (i // 2, i % 2, 0, 0)),
                half,
                half,
            ],
            scratch_shapes=[pltpu.VMEM((512, 512), BF16), pltpu.VMEM((256, 1024), BF16)],
        ),
        out_shape=[
            pltpu.VMEM((CROPS, 2, 1024, 256), BF16),
            pltpu.VMEM((CROPS, 2, 256, 256), BF16),
            pltpu.VMEM((CROPS, 256, 256), BF16),
            pltpu.VMEM((CROPS, 256, 256), BF16),
        ],
        compiler_params=params(),
    )(where, pltpu.with_memory_space_constraint(volume, pltpu.HBM), pltpu.with_memory_space_constraint(w1, pltpu.HBM))


def prepare_kernel(
    w2_ref, w3_ref, wd_ref, head_ref, f2_ref, b2_ref, f3_ref, b3_ref, perm_ref, d_ref, wh_ref, rows_ref
):
    low = lax.broadcasted_iota(jnp.int32, (64, 128), 1) < 64
    zero = jnp.zeros((64, 128), F32)
    for d in range(3):
        for j in range(3):
            at = (d * 3 + j) * T
            back = (8 - d * 3 - j) * T
            w = [w2_ref[d * 9 + h * 3 + j].astype(F32) for h in range(3)]
            pairs = {
                (0, 0): jnp.where(low, w[1], w[2]),
                (0, 1): zero,
                (1, 0): jnp.where(low, w[0], w[1]),
                (1, 1): jnp.where(low, w[2], 0.0),
                (2, 0): jnp.where(low, 0.0, w[0]),
                (2, 1): jnp.where(low, w[1], w[2]),
                (3, 0): zero,
                (3, 1): jnp.where(low, w[0], w[1]),
            }
            for (row, col), block in pairs.items():
                f2_ref[pl.ds(row * 64, 64), pl.ds(at + col * 128, 128)] = block.astype(BF16)
            b2_ref[:, pl.ds(back, T)] = f2_ref[:, pl.ds(at, T)].astype(F32).T.astype(BF16)
            for row in range(2):
                for col in range(2):
                    block = w3_ref[d * 9 + (col - row + 1) * 3 + j]
                    f3_ref[pl.ds(row * 128, 128), pl.ds(at + col * 128, 128)] = block
                    b3_ref[pl.ds(col * 128, 128), pl.ds(back + row * 128, 128)] = block.astype(F32).T.astype(BF16)
    rows_ref[...] = wd_ref[...].astype(F32)
    for d in range(2):
        for p in range(2):
            for h in range(4):
                block = rows_ref[pl.ds(d * 4 + h % 2 * 2 + p, 64, stride=8), :].astype(BF16)
                d_ref[2 * d + p, pl.ds(h * 64, 64), pl.ds(h // 2 * 128, 128)] = block
                d_ref[2 * d + p, pl.ds(h * 64, 64), pl.ds(128 - h // 2 * 128, 128)] = jnp.zeros_like(block)
    rows_ref[pl.ds(0, 128), :] = jnp.zeros((128, 128), F32)
    rows_ref[pl.ds(0, 4), :] = head_ref[...].astype(F32)
    wht = rows_ref[pl.ds(0, 128), :]
    wh_ref[pl.ds(0, 128), :] = wht.T.astype(BF16)
    wh_ref[pl.ds(128, 128), :] = wht.astype(BF16)
    to = lax.broadcasted_iota(jnp.int32, (1, 256), 1)
    source = to // 4 % 2 * 512 + to % 2 * 256 + (to // 128 * 16 + to // 8 % 16) * 8 + to // 2 % 2
    perm_ref[...] = jnp.where(lax.broadcasted_iota(jnp.int32, (1024, 256), 0) == source, 1.0, 0.0).astype(BF16)


def prepare(w2, w3, wd, wh):
    def wide(space):
        return ((T, 9 * T), BF16, space)

    return call(
        prepare_kernel,
        [wide(pltpu.VMEM), wide(pltpu.VMEM), wide(pltpu.HBM), wide(pltpu.VMEM)]
        + [((1024, 256), BF16, pltpu.VMEM), ((4, T, T), BF16, pltpu.VMEM), ((256, 128), BF16, pltpu.HBM)],
        w2, w3, wd, wh,
        scratch=[pltpu.VMEM((512, 128), F32)],
    )


def second_kernel(where_ref, one_ref, a_ref, two_ref, f2_ref, wd_ref, h_ref, a3_ref, b_ref):
    for n in range(CROPS):
        lo, hi = sorted_out(where_ref, one_ref[n], two_ref[n])
        planes = (lo, a_ref[n, 0], a_ref[n, 1], hi)
        for k, plane in enumerate(planes):
            put_three(b_ref, k * 3 * T, three_two(plane))
        for d in range(2):
            h = rectified(dot(f2_ref[...], b_ref[pl.ds(d * 3 * T, 9 * T), :])).astype(BF16)
            for p in range(2):
                h_ref[2 * d + p, :, pl.ds(n * 128, 128)] = h[:, p * 128 : (p + 1) * 128]
    total = dot_tn(wd_ref[0], h_ref[0])
    for k in range(1, 4):
        total += dot_tn(wd_ref[k], h_ref[k])
    a3_ref[...] = rectified(total).astype(BF16)


def second(where, one, a, two, f2, wd):
    return call(
        second_kernel,
        [((4, T, T), BF16, pltpu.HBM), ((T, T), BF16, pltpu.VMEM)],
        where, one, a, two, f2, wd,
        scratch=[pltpu.VMEM((12 * T, T), BF16)],
    )


def head_kernel(
    scale, where_ref, one_ref, a_ref, two_ref, f3_far, wh_far, marks_ref, gz_ref, gh_ref, b_ref, f3_ref, wh_ref, sems
):
    fetches = [
        pltpu.make_async_copy(f3_far, f3_ref, sems.at[0]),
        pltpu.make_async_copy(wh_far, wh_ref, sems.at[1]),
    ]
    for fetch in fetches:
        fetch.start()
    lo, hi = sorted_out(where_ref, one_ref[...], two_ref[...])
    for k, plane in enumerate((lo, a_ref[...], hi)):
        put_three(b_ref, k * 3 * T, three_three(plane))
    for fetch in fetches:
        fetch.wait()
    top = rectified(dot(f3_ref[...], b_ref[...])).astype(BF16)
    row = lax.broadcasted_iota(jnp.int32, (128, T), 0)
    total = jnp.zeros((128, 128), F32)
    for h in range(2):
        mine = top[h * 128 : (h + 1) * 128]
        logits = dot(wh_ref[pl.ds(128, 128), :], mine)
        powers = jnp.where(row < 4, jnp.exp(logits), 0.0)
        share = powers / jnp.sum(powers, axis=0, keepdims=True)
        chosen = jnp.where(row == marks_ref[pl.ds(h, 1), :], 1.0, 0.0)
        g = jnp.where(row < 4, (share - chosen) * scale, 0.0).astype(BF16)
        total += dot_nt(mine, g)
        gz_ref[pl.ds(h * 128, 128), :] = (dot(wh_ref[pl.ds(0, 128), :], g) * slope(mine)).astype(BF16)
    gh_ref[...] = total


def head(where, one, a, two, f3, wh, marks, scale):
    return call(
        functools.partial(head_kernel, scale),
        [((T, T), BF16, pltpu.VMEM), ((128, 128), F32, pltpu.VMEM)],
        where, one, a, two, f3, wh, marks,
        scratch=[
            pltpu.VMEM((9 * T, T), BF16),
            pltpu.VMEM((T, 9 * T), BF16),
            pltpu.VMEM((256, 128), BF16),
            pltpu.SemaphoreType.DMA((2,)),
        ],
        far=(4, 5),
    )


def weight_three_kernel(where_ref, g_ref, one_ref, a_ref, two_ref, out_ref, s_ref):
    put_three(s_ref, 0, three_three(g_ref[...]))
    lo, hi = sorted_out(where_ref, one_ref[...], two_ref[...])
    for d, a in enumerate((lo, a_ref[...], hi)):
        for j in range(3):
            t = dot_nt(s_ref[pl.ds((2 - j) * T, T), :], a)
            out_ref[d * 9 + j] = t[128:, :128]
            out_ref[d * 9 + 3 + j] = t[:128, :128] + t[128:, 128:]
            out_ref[d * 9 + 6 + j] = t[:128, 128:]


def weight_three(where, g, one, a, two):
    return call(
        weight_three_kernel,
        [((27, 128, 128), F32, pltpu.VMEM)],
        where, g, one, a, two,
        scratch=[pltpu.VMEM((3 * T, T), BF16)],
    )[0]


def middle_kernel(
    where_ref, one_ref, g_ref, two_ref, b3_ref, a3_ref, h_ref, wd_ref, gz2_ref, gone_ref, gtwo_ref, gd_ref, b_ref
):
    lo, hi = sorted_out(where_ref, one_ref[...], two_ref[...])
    for k, plane in enumerate((lo, g_ref[...], hi)):
        put_three(b_ref, k * 3 * T, three_three(plane))
    gy = (dot(b3_ref[...], b_ref[...]) * slope(a3_ref[...])).astype(BF16)
    for d in range(2):
        for p in range(2):
            k = 2 * d + p
            q = (dot(wd_ref[k], gy) * slope(h_ref[k])).astype(BF16)
            for n in range(CROPS):
                gz2_ref[n, d, :, pl.ds(p * 128, 128)] = q[:, n * 128 : (n + 1) * 128]
    even = where_ref[1] == 0
    for n in range(CROPS):
        gone_ref[n] = jnp.where(even, gz2_ref[n, 1], gz2_ref[n, 0])
        gtwo_ref[n] = jnp.where(even, gz2_ref[n, 0], gz2_ref[n, 1])
    for k in range(4):
        gd_ref[k] = dot_nt(gy[:128], h_ref[k, :128]) + dot_nt(gy[128:], h_ref[k, 128:])


def middle(where, one, g, two, b3, a3, h, wd):
    return call(
        middle_kernel,
        [
            ((CROPS, 2, T, T), BF16, pltpu.VMEM),
            ((CROPS, T, T), BF16, pltpu.VMEM),
            ((CROPS, T, T), BF16, pltpu.VMEM),
            ((4, 128, 128), F32, pltpu.VMEM),
        ],
        where, one, g, two, b3, a3, h, wd,
        scratch=[pltpu.VMEM((9 * T, T), BF16)],
    )


def weight_two_kernel(where_ref, g_ref, one_ref, a_ref, two_ref, out_ref, gs_ref, as_ref):
    for n in range(CROPS):
        lo, hi = sorted_out(where_ref, one_ref[n], two_ref[n])
        planes = (lo, a_ref[n, 0], a_ref[n, 1], hi)
        for d in range(2):
            at = (2 * n + d) * T
            for j, (left, right) in enumerate(three_two(g_ref[n, d])):
                gs_ref[2 - j, :, pl.ds(at, 128)] = left
                gs_ref[2 - j, :, pl.ds(at + 128, 128)] = right
            for k in range(3):
                as_ref[k, :, pl.ds(at, T)] = planes[d + k]
    low = lax.broadcasted_iota(jnp.int32, (64, 128), 1) < 64
    block = (lax.broadcasted_iota(jnp.int32, (64, 128), 1) // 32) % 2 == 0
    sums = {}
    for d in range(3):
        for j in range(3):
            t = dot_nt(gs_ref[j], as_ref[d])
            q = lambda r, c: t[r * 64 : (r + 1) * 64, c * 128 : (c + 1) * 128]
            sums[d, 0, j] = jnp.where(low, q(1, 0) + q(3, 1), q(2, 0))
            sums[d, 1, j] = jnp.where(low, q(0, 0) + q(2, 1), q(1, 0) + q(3, 1))
            sums[d, 2, j] = jnp.where(low, q(1, 1), q(0, 0) + q(2, 1))
        for h in range(3):
            for j in range(3):
                s = sums[d, h, j]
                sums[d, h, j] = s + pltpu.roll(s, 64, 1)
    taps = [sums[t // 9, t // 3 % 3, t % 3] for t in range(27)] + [jnp.zeros((64, 128), F32)]
    for g in range(7):
        four = taps[4 * g : 4 * g + 4]
        turned = [pltpu.roll(x, 32, 1) for x in four]
        out_ref[g, 0] = jnp.where(low, jnp.where(block, four[0], turned[1]), jnp.where(block, four[2], turned[3]))
        out_ref[g, 1] = jnp.where(low, jnp.where(block, turned[0], four[1]), jnp.where(block, turned[2], four[3]))


def weight_two(where, g, one, a, two):
    return call(
        weight_two_kernel,
        [((7, 2, 64, 128), F32, pltpu.VMEM)],
        where, g, one, a, two,
        scratch=[pltpu.VMEM((3, T, 4 * T), BF16), pltpu.VMEM((3, T, 4 * T), BF16)],
    )[0]


def pack_kernel(where_ref, w3_ref, d3_ref, w2_ref, gh_ref, keep_ref, send_ref, pack_ref):
    for t in range(27):
        pack_ref[pl.ds(t, 128, stride=ROWS), :] = w3_ref[t]
    for k in range(4):
        pack_ref[pl.ds(DOWN3 + k, 128, stride=ROWS), :] = d3_ref[k]
    lane = lax.broadcasted_iota(jnp.int32, (64, 128), 1)
    for half in range(2):
        for g in range(6):
            pack_ref[pl.ds(half * ROWS + CONV2 + g, 64, stride=2 * ROWS), :] = w2_ref[g, half]
        heads = pltpu.roll(gh_ref[pl.ds(half, 64, stride=2), :], 96, 1)
        pack_ref[pl.ds(half * ROWS + CONV2 + 6, 64, stride=2 * ROWS), :] = jnp.where(lane < 96, w2_ref[6, half], heads)
    zero = jnp.zeros((128, 128), F32)
    pack_ref[pl.ds(DOWN2, 128, stride=ROWS), :] = zero
    pack_ref[pl.ds(DOWN2 + 1, 128, stride=ROWS), :] = zero
    keep_ref[...] = pack_ref[pl.ds(pl.multiple_of(where_ref[0] * 64 * ROWS, 64 * ROWS), 64 * ROWS), :]
    send_ref[...] = pack_ref[pl.ds(pl.multiple_of((1 - where_ref[0]) * 64 * ROWS, 64 * ROWS), 64 * ROWS), :].astype(BF16)


def packed(*args):
    half = (64 * ROWS, 128)
    return call(
        pack_kernel,
        [(half, F32, pltpu.VMEM), (half, BF16, pltpu.VMEM)],
        *args,
        scratch=[pltpu.VMEM((128 * ROWS, 128), F32)],
    )


def last_kernel(where_ref, one_ref, g_ref, two_ref, b2_ref, a_ref, vp_ref, perm_ref, down_ref, b_ref, t_ref):
    for n in range(CROPS):
        lo, hi = sorted_out(where_ref, one_ref[n], two_ref[n])
        planes = (lo, g_ref[n, 0], g_ref[n, 1], hi)
        for k, plane in enumerate(planes):
            put_three(b_ref, k * 3 * T, three_two(plane))
        gy = [
            (dot(b2_ref[...], b_ref[pl.ds(d * 3 * T, 9 * T), :]) * slope(a_ref[n, d])).astype(BF16) for d in range(2)
        ]
        t = dot_nt(gy[0], vp_ref[n, 0]) + dot_nt(gy[1], vp_ref[n, 1])
        if n == 0:
            t_ref[...] = t
        else:
            t_ref[...] += t
    pairs = []
    lane = lax.broadcasted_iota(jnp.int32, (64, 128), 1)
    for tile in range(8):
        at = pl.ds(tile * 128, 128)
        x = jnp.zeros((64, 128), F32)
        for h in range(4):
            x = jnp.where(lane % 8 // 2 == h, t_ref[pl.ds(h * 64, 64), at], x)
        x = x + pltpu.roll(x, 126, 1)
        x = x + pltpu.roll(x, 124, 1)
        pairs.append(x.astype(BF16))
    down_ref[...] = dot(jnp.concatenate(pairs, axis=1), perm_ref[...])


def last(*args):
    return call(
        last_kernel,
        [((64, 256), F32, pltpu.VMEM)],
        *args,
        scratch=[pltpu.VMEM((12 * T, T), BF16), pltpu.VMEM((T, 1024), F32)],
    )[0]


def join_kernel(where_ref, down_ref, keep_ref, came_ref, out_ref, d_ref):
    for k, sec in enumerate((where_ref[0], 1 - where_ref[0])):
        mine = pl.ds(pl.multiple_of(sec * 32, 32), 32)
        for half in range(2):
            to = pl.ds(half * ROWS + DOWN2 + k, 32, stride=2 * ROWS)
            d_ref[to, :] = down_ref[mine, half * 128 : (half + 1) * 128]
    row = lax.broadcasted_iota(jnp.int32, (ROWS, 128), 0)
    for j in range(64):
        at = pl.ds(j * ROWS, ROWS)
        both = keep_ref[at, :] + came_ref[at, :].astype(F32)
        out_ref[at, :] = jnp.where(row >= DOWN2, d_ref[at, :], both).astype(BF16)


def joined(*args):
    return call(
        join_kernel,
        [((64 * ROWS, 128), BF16, pltpu.VMEM)],
        *args,
        scratch=[pltpu.VMEM((64 * ROWS, 128), F32)],
    )[0]


def swapped(one, two):
    count = lax.axis_size("space")
    near = [(i, i ^ 1) for i in range(count)]
    far = [(i, ((i + 1) ^ 1) - 1) for i in range(1, count - 1)]
    two = lax.ppermute(two, "space", far)
    return lax.ppermute(one, "space", near), two


def partner(x):
    return lax.ppermute(x, "section", [(0, 1), (1, 0)])


def unpack(sums, down):
    return (
        down,
        sums[CONV2:DOWN2].reshape(28, 32)[:27].T.reshape(-1),
        sums[DOWN3:CONV2].reshape(2, 2, 2, 64).transpose(3, 0, 2, 1).reshape(-1),
        sums[:27].T.reshape(-1),
        sums[DOWN2 - 1, 96:100],
    )


def finish(pack):
    terms = lax.all_to_all(pack, "space", 0, 0, tiled=True)
    sums = jnp.sum(terms.astype(F32), axis=0)
    return unpack(sums, sums[DOWN2] + partner(sums[DOWN2 + 1]))


def per_device(volume, labels, down_weight_two, w_conv_two, down_weight_three, w_conv_three, w_head):
    count = lax.axis_size("space")
    voxels = labels.shape[0] * labels.shape[1] * count * labels.shape[2] * labels.shape[3]
    scale = 1.0 / math.sqrt(voxels)
    sec = lax.axis_index("section").astype(jnp.int32)
    where = jnp.stack([sec, lax.axis_index("space").astype(jnp.int32) % 2])

    w1 = down_weight_two.transpose(1, 2, 3, 4, 0).reshape(256, 64)
    wd = down_weight_three.transpose(1, 2, 3, 4, 0).reshape(512, 128)
    w2 = w_conv_two.transpose(2, 3, 4, 0, 1).reshape(27, 64, 64)
    w2 = jnp.concatenate([w2, w2], axis=2)
    w3 = w_conv_three.transpose(2, 3, 4, 0, 1).reshape(27, 128, 128)
    marks = lax.dynamic_slice_in_dim(labels[:, 0], CROPS * sec, CROPS, axis=0)
    marks = marks.transpose(1, 0, 2).reshape(2, 256)

    vp, a2, one, two = first(where, volume, w1)
    a2_one, a2_two = swapped(one, two)
    f2, b2, f3, b3, perm, wd, wh = prepare(w2, w3, wd, w_head.T)
    h2, a3 = second(where, a2_one, a2, a2_two, f2, wd)
    a3_one, a3_two = swapped(a3, a3)
    gz4, gh = head(where, a3_one, a3, a3_two, f3, wh, marks, scale)
    gz4_one, gz4_two = swapped(gz4, gz4)
    gw3 = weight_three(where, gz4, a3_one, a3, a3_two)
    gz4_one, gz4_two, gw3 = lax.optimization_barrier((gz4_one, gz4_two, gw3))
    gz2, one, two, gd3 = middle(where, gz4_one, gz4, gz4_two, b3, a3, h2, wd)
    gz2_one, gz2_two = swapped(one, two)
    gw2 = weight_two(where, gz2, a2_one, a2, a2_two)
    keep, send = packed(where, gw3, gd3, gw2, gh)
    gz2_one, gz2_two, send = lax.optimization_barrier((gz2_one, gz2_two, send))
    came = partner(send)
    down = last(where, gz2_one, gz2, gz2_two, b2, a2, vp, perm)
    pack = joined(where, down, keep, came)
    return finish(pack.reshape(64, ROWS, 128))


def solution(mesh):
    whole = P(("section", "space"))
    return jax.shard_map(
        per_device,
        mesh=mesh,
        in_specs=(P(None, None, "space", None, None), P(None, "space", None, None), P(), P(), P(), P(), P()),
        out_specs=(whole,) * 5,
        check_vma=False,
    )
```

```python
import functools
import math

import jax
import jax.numpy as jnp
from jax import lax
from jax.experimental import pallas as pl
from jax.experimental.pallas import tpu as pltpu
from jax.sharding import PartitionSpec as P


F32 = jnp.float32
BF16 = jnp.bfloat16
SHIFT = math.log(2.0)
CROPS = 2
T = 256
ROWS = 40
DOWN3, CONV2, DOWN2 = 27, 31, 38


def params(megabytes=12):
    return pltpu.CompilerParams(vmem_limit_bytes=megabytes << 20)


def rectified(v):
    return jnp.maximum(v, 0.0) + jnp.log1p(jnp.exp(-jnp.abs(v))) - SHIFT


def slope(stored):
    return 1.0 - 0.5 * jnp.exp(-stored.astype(F32))


def dot(a, b):
    return jnp.dot(a, b, preferred_element_type=F32)


def dot_tn(a, b):
    return lax.dot_general(a, b, (((0,), (0,)), ((), ())), preferred_element_type=F32)


def dot_nt(a, b):
    return lax.dot_general(a, b, (((1,), (1,)), ((), ())), preferred_element_type=F32)


def moved(x, by):
    x = x.astype(F32)
    lane = lax.broadcasted_iota(jnp.int32, x.shape, 1)
    edge = 0 if by == 1 else 127
    return jnp.where(lane == edge, 0.0, pltpu.roll(x, by % 128, 1)).astype(BF16)


def three_two(x):
    even, odd = x[:, :128], x[:, 128:]
    return ((moved(odd, 1), even), (even, odd), (odd, moved(even, -1)))


def three_three(x):
    first, second = x[:, :128], x[:, 128:]
    return ((moved(first, 1), moved(second, 1)), (first, second), (moved(first, -1), moved(second, -1)))


def put_three(ref, row, shifted):
    for j, (left, right) in enumerate(shifted):
        ref[pl.ds(row + j * T, T), 0:128] = left
        ref[pl.ds(row + j * T, T), 128:256] = right


def call(kernel, outs, *args, scratch=(), far=()):
    spec = pl.BlockSpec(memory_space=pltpu.VMEM)
    scalar = pl.BlockSpec(memory_space=pltpu.SMEM)
    remote = pl.BlockSpec(memory_space=pl.ANY)
    return pl.pallas_call(
        kernel,
        in_specs=[remote if i in far else scalar if a.dtype == jnp.int32 and a.ndim == 1 else spec for i, a in enumerate(args)],
        out_specs=[spec] * len(outs),
        out_shape=[space(s, d) for s, d, space in outs],
        scratch_shapes=list(scratch),
        compiler_params=params(),
    )(*[pltpu.with_memory_space_constraint(a, pltpu.HBM) if i in far else a for i, a in enumerate(args)])


def sorted_out(where_ref, one, two):
    even = where_ref[1] == 0
    return jnp.where(even, two, one), jnp.where(even, one, two)


def first_kernel(
    where_ref, vol_far, w_ref, vp_far, a_ref, one_ref, two_ref, sort_ref, wt_ref, vol_ref, vp_ref, in_sems, out_sems
):
    steps = [(n, d) for n in range(CROPS) for d in range(2)]
    fetches = [
        pltpu.make_async_copy(vol_far.at[CROPS * where_ref[0] + n, :, pl.ds(2 * d, 2)], vol_ref.at[i], in_sems.at[i])
        for i, (n, d) in enumerate(steps)
    ]
    stores = [
        pltpu.make_async_copy(vp_ref.at[i], vp_far.at[n, d], out_sems.at[i]) for i, (n, d) in enumerate(steps)
    ]
    for fetch in fetches:
        fetch.start()
    to = lax.broadcasted_iota(jnp.int32, (1, 512), 1)
    source = (to % 128) * 4 + (to // 128) % 2 * 2 + to // 256
    sort_ref[...] = jnp.where(lax.broadcasted_iota(jnp.int32, (512, 512), 0) == source, 1.0, 0.0).astype(BF16)
    to = lax.broadcasted_iota(jnp.int32, (1, 1024), 1)
    height = to % 8
    source = to // 8 % 32 * 8 + to // 512 * 4 + height % 2 * 2 + to // 256 % 2
    pick = jnp.where(lax.broadcasted_iota(jnp.int32, (256, 1024), 0) == source, 1.0, 0.0).astype(BF16)
    w = dot_tn(w_ref[...], pick)
    for h in range(4):
        wt_ref[pl.ds(h * 64, 64), :] = jnp.where(height // 2 == h, w, 0.0).astype(BF16)
    for i, (n, d) in enumerate(steps):
        fetches[i].wait()
        for k in range(2):
            v = vol_ref[i, :, k].astype(F32).reshape(256, 512).astype(BF16)
            s = dot(v, sort_ref[...]).astype(BF16)
            vp_ref[i, pl.ds(k * 512, 256), :] = s[:, :256]
            vp_ref[i, pl.ds(k * 512 + 256, 256), :] = s[:, 256:]
        stores[i].start()
        a_ref[n, d] = rectified(dot(wt_ref[...], vp_ref[i])).astype(BF16)
    even = where_ref[1] == 0
    for n in range(CROPS):
        one_ref[n] = jnp.where(even, a_ref[n, 1], a_ref[n, 0])
        two_ref[n] = jnp.where(even, a_ref[n, 0], a_ref[n, 1])
    for store in stores:
        store.wait()


def first(where, volume, w1):
    spec = pl.BlockSpec(memory_space=pltpu.VMEM)
    far = pl.BlockSpec(memory_space=pl.ANY)
    return pl.pallas_call(
        first_kernel,
        in_specs=[pl.BlockSpec(memory_space=pltpu.SMEM), far, spec],
        out_specs=[far, spec, spec, spec],
        out_shape=[
            pltpu.HBM((CROPS, 2, 1024, 256), BF16),
            pltpu.VMEM((CROPS, 2, 256, 256), BF16),
            pltpu.VMEM((CROPS, 256, 256), BF16),
            pltpu.VMEM((CROPS, 256, 256), BF16),
        ],
        scratch_shapes=[
            pltpu.VMEM((512, 512), BF16),
            pltpu.VMEM((256, 1024), BF16),
            pltpu.VMEM((4, 32, 2, 8, 512), BF16),
            pltpu.VMEM((4, 1024, 256), BF16),
            pltpu.SemaphoreType.DMA((4,)),
            pltpu.SemaphoreType.DMA((4,)),
        ],
        compiler_params=params(),
    )(where, pltpu.with_memory_space_constraint(volume, pltpu.HBM), pltpu.with_memory_space_constraint(w1, pltpu.HBM))


def prepare_kernel(
    w2_ref, w3_ref, wd_ref, head_ref, f2_ref, b2_ref, f3_ref, b3_ref, perm_ref, d_ref, wh_ref, rows_ref
):
    low = lax.broadcasted_iota(jnp.int32, (64, 128), 1) < 64
    zero = jnp.zeros((64, 128), F32)
    for d in range(3):
        for j in range(3):
            at = (d * 3 + j) * T
            back = (8 - d * 3 - j) * T
            w = [w2_ref[d * 9 + h * 3 + j].astype(F32) for h in range(3)]
            pairs = {
                (0, 0): jnp.where(low, w[1], w[2]),
                (0, 1): zero,
                (1, 0): jnp.where(low, w[0], w[1]),
                (1, 1): jnp.where(low, w[2], 0.0),
                (2, 0): jnp.where(low, 0.0, w[0]),
                (2, 1): jnp.where(low, w[1], w[2]),
                (3, 0): zero,
                (3, 1): jnp.where(low, w[0], w[1]),
            }
            for (row, col), block in pairs.items():
                f2_ref[pl.ds(row * 64, 64), pl.ds(at + col * 128, 128)] = block.astype(BF16)
            b2_ref[:, pl.ds(back, T)] = f2_ref[:, pl.ds(at, T)].astype(F32).T.astype(BF16)
            for row in range(2):
                for col in range(2):
                    block = w3_ref[d * 9 + (col - row + 1) * 3 + j]
                    f3_ref[pl.ds(row * 128, 128), pl.ds(at + col * 128, 128)] = block
                    b3_ref[pl.ds(col * 128, 128), pl.ds(back + row * 128, 128)] = block.astype(F32).T.astype(BF16)
    rows_ref[...] = wd_ref[...].astype(F32)
    for d in range(2):
        for p in range(2):
            for h in range(4):
                block = rows_ref[pl.ds(d * 4 + h % 2 * 2 + p, 64, stride=8), :].astype(BF16)
                d_ref[2 * d + p, pl.ds(h * 64, 64), pl.ds(h // 2 * 128, 128)] = block
                d_ref[2 * d + p, pl.ds(h * 64, 64), pl.ds(128 - h // 2 * 128, 128)] = jnp.zeros_like(block)
    rows_ref[pl.ds(0, 128), :] = jnp.zeros((128, 128), F32)
    rows_ref[pl.ds(0, 4), :] = head_ref[...].astype(F32)
    wht = rows_ref[pl.ds(0, 128), :]
    wh_ref[pl.ds(0, 128), :] = wht.T.astype(BF16)
    wh_ref[pl.ds(128, 128), :] = wht.astype(BF16)
    to = lax.broadcasted_iota(jnp.int32, (1, 256), 1)
    source = to // 4 % 2 * 512 + to % 2 * 256 + (to // 128 * 16 + to // 8 % 16) * 8 + to // 2 % 2
    perm_ref[...] = jnp.where(lax.broadcasted_iota(jnp.int32, (1024, 256), 0) == source, 1.0, 0.0).astype(BF16)


def prepare(w2, w3, wd, wh):
    def wide(space):
        return ((T, 9 * T), BF16, space)

    return call(
        prepare_kernel,
        [wide(pltpu.VMEM), wide(pltpu.VMEM), wide(pltpu.HBM), wide(pltpu.VMEM)]
        + [((1024, 256), BF16, pltpu.VMEM), ((4, T, T), BF16, pltpu.VMEM), ((256, 128), BF16, pltpu.HBM)],
        w2, w3, wd, wh,
        scratch=[pltpu.VMEM((512, 128), F32)],
    )


def second_own_kernel(a_ref, f2_ref, out_ref, b_ref):
    for n in range(CROPS):
        for d in range(2):
            put_three(b_ref, (2 * n + d) * 3 * T, three_two(a_ref[n, d]))
        own = pl.ds(n * 6 * T, 6 * T)
        out_ref[n, 0] = dot(f2_ref[:, 3 * T :], b_ref[own, :])
        out_ref[n, 1] = dot(f2_ref[:, : 6 * T], b_ref[own, :])


def second_own(a, f2):
    return call(
        second_own_kernel,
        [((CROPS, 2, T, T), F32, pltpu.VMEM)],
        a, f2,
        scratch=[pltpu.VMEM((12 * T, T), BF16)],
    )[0]


def second_kernel(where_ref, one_ref, own_ref, two_ref, f2_ref, wd_ref, h_ref, a3_ref, b_ref):
    for n in range(CROPS):
        for d, plane in enumerate(sorted_out(where_ref, one_ref[n], two_ref[n])):
            at = (2 * n + d) * 3 * T
            put_three(b_ref, at, three_two(plane))
            rest = dot(f2_ref[:, d * 6 * T : d * 6 * T + 3 * T], b_ref[pl.ds(at, 3 * T), :])
            h = rectified(own_ref[n, d] + rest).astype(BF16)
            for p in range(2):
                h_ref[2 * d + p, :, pl.ds(n * 128, 128)] = h[:, p * 128 : (p + 1) * 128]
    total = dot_tn(wd_ref[0], h_ref[0])
    for k in range(1, 4):
        total += dot_tn(wd_ref[k], h_ref[k])
    a3_ref[...] = rectified(total).astype(BF16)


def second(where, one, own, two, f2, wd):
    return call(
        second_kernel,
        [((4, T, T), BF16, pltpu.HBM), ((T, T), BF16, pltpu.VMEM)],
        where, one, own, two, f2, wd,
        scratch=[pltpu.VMEM((12 * T, T), BF16)],
    )


def head_own_kernel(a_ref, f3_ref, wh_ref, out_ref, sides_ref, wh_out_ref, b_ref):
    put_three(b_ref, 0, three_three(a_ref[...]))
    out_ref[...] = dot(f3_ref[:, 3 * T : 6 * T], b_ref[...])
    sides_ref[:, : 3 * T] = f3_ref[:, : 3 * T]
    sides_ref[:, 3 * T :] = f3_ref[:, 6 * T :]
    wh_out_ref[...] = wh_ref[...]


def head_own(a, f3, wh):
    return call(
        head_own_kernel,
        [((T, T), F32, pltpu.VMEM), ((T, 6 * T), BF16, pltpu.VMEM), ((256, 128), BF16, pltpu.VMEM)],
        a, f3, wh,
        scratch=[pltpu.VMEM((3 * T, T), BF16)],
    )


def head_kernel(scale, where_ref, one_ref, own_ref, two_ref, sides_ref, wh_ref, marks_ref, gz_ref, gh_ref, b_ref):
    for k, plane in enumerate(sorted_out(where_ref, one_ref[...], two_ref[...])):
        put_three(b_ref, k * 3 * T, three_three(plane))
    top = rectified(own_ref[...] + dot(sides_ref[...], b_ref[...])).astype(BF16)
    row = lax.broadcasted_iota(jnp.int32, (128, T), 0)
    total = jnp.zeros((128, 128), F32)
    for h in range(2):
        mine = top[h * 128 : (h + 1) * 128]
        logits = dot(wh_ref[pl.ds(128, 128), :], mine)
        powers = jnp.where(row < 4, jnp.exp(logits), 0.0)
        share = powers / jnp.sum(powers, axis=0, keepdims=True)
        chosen = jnp.where(row == marks_ref[pl.ds(h, 1), :], 1.0, 0.0)
        g = jnp.where(row < 4, (share - chosen) * scale, 0.0).astype(BF16)
        total += dot_nt(mine, g)
        gz_ref[pl.ds(h * 128, 128), :] = (dot(wh_ref[pl.ds(0, 128), :], g) * slope(mine)).astype(BF16)
    gh_ref[...] = total


def head(where, one, own, two, sides, wh, marks, scale):
    return call(
        functools.partial(head_kernel, scale),
        [((T, T), BF16, pltpu.VMEM), ((128, 128), F32, pltpu.VMEM)],
        where, one, own, two, sides, wh, marks,
        scratch=[pltpu.VMEM((6 * T, T), BF16)],
    )


def weight_three_kernel(where_ref, g_ref, one_ref, a_ref, two_ref, out_ref, s_ref):
    put_three(s_ref, 0, three_three(g_ref[...]))
    lo, hi = sorted_out(where_ref, one_ref[...], two_ref[...])
    for d, a in enumerate((lo, a_ref[...], hi)):
        for j in range(3):
            t = dot_nt(s_ref[pl.ds((2 - j) * T, T), :], a)
            out_ref[d * 9 + j] = t[128:, :128]
            out_ref[d * 9 + 3 + j] = t[:128, :128] + t[128:, 128:]
            out_ref[d * 9 + 6 + j] = t[:128, 128:]


def weight_three(where, g, one, a, two):
    return call(
        weight_three_kernel,
        [((27, 128, 128), F32, pltpu.VMEM)],
        where, g, one, a, two,
        scratch=[pltpu.VMEM((3 * T, T), BF16)],
    )[0]


def middle_own_kernel(g_ref, b3_ref, out_ref, b_ref):
    put_three(b_ref, 0, three_three(g_ref[...]))
    out_ref[...] = dot(b3_ref[:, 3 * T : 6 * T], b_ref[...])


def middle_own(g, b3):
    return call(
        middle_own_kernel,
        [((T, T), F32, pltpu.VMEM)],
        g, b3,
        scratch=[pltpu.VMEM((3 * T, T), BF16)],
    )[0]


def middle_kernel(
    where_ref, one_ref, own_ref, two_ref, b3_ref, a3_ref, h_ref, wd_ref, gz2_ref, gone_ref, gtwo_ref, gd_ref, b_ref
):
    rest = own_ref[...]
    for k, plane in enumerate(sorted_out(where_ref, one_ref[...], two_ref[...])):
        put_three(b_ref, k * 3 * T, three_three(plane))
        rest += dot(b3_ref[:, k * 6 * T : k * 6 * T + 3 * T], b_ref[pl.ds(k * 3 * T, 3 * T), :])
    gy = (rest * slope(a3_ref[...])).astype(BF16)
    for d in range(2):
        for p in range(2):
            k = 2 * d + p
            q = (dot(wd_ref[k], gy) * slope(h_ref[k])).astype(BF16)
            for n in range(CROPS):
                gz2_ref[n, d, :, pl.ds(p * 128, 128)] = q[:, n * 128 : (n + 1) * 128]
    even = where_ref[1] == 0
    for n in range(CROPS):
        gone_ref[n] = jnp.where(even, gz2_ref[n, 1], gz2_ref[n, 0])
        gtwo_ref[n] = jnp.where(even, gz2_ref[n, 0], gz2_ref[n, 1])
    for k in range(4):
        gd_ref[k] = dot_nt(gy[:128], h_ref[k, :128]) + dot_nt(gy[128:], h_ref[k, 128:])


def middle(where, one, own, two, b3, a3, h, wd):
    return call(
        middle_kernel,
        [
            ((CROPS, 2, T, T), BF16, pltpu.VMEM),
            ((CROPS, T, T), BF16, pltpu.VMEM),
            ((CROPS, T, T), BF16, pltpu.VMEM),
            ((4, 128, 128), F32, pltpu.VMEM),
        ],
        where, one, own, two, b3, a3, h, wd,
        scratch=[pltpu.VMEM((6 * T, T), BF16)],
    )


def weight_two_kernel(where_ref, g_ref, one_ref, a_ref, two_ref, out_ref, gs_ref, as_ref):
    for n in range(CROPS):
        lo, hi = sorted_out(where_ref, one_ref[n], two_ref[n])
        planes = (lo, a_ref[n, 0], a_ref[n, 1], hi)
        for d in range(2):
            at = (2 * n + d) * T
            for j, (left, right) in enumerate(three_two(g_ref[n, d])):
                gs_ref[2 - j, :, pl.ds(at, 128)] = left
                gs_ref[2 - j, :, pl.ds(at + 128, 128)] = right
            for k in range(3):
                as_ref[k, :, pl.ds(at, T)] = planes[d + k]
    low = lax.broadcasted_iota(jnp.int32, (64, 128), 1) < 64
    block = (lax.broadcasted_iota(jnp.int32, (64, 128), 1) // 32) % 2 == 0
    sums = {}
    for d in range(3):
        for j in range(3):
            t = dot_nt(gs_ref[j], as_ref[d])
            q = lambda r, c: t[r * 64 : (r + 1) * 64, c * 128 : (c + 1) * 128]
            sums[d, 0, j] = jnp.where(low, q(1, 0) + q(3, 1), q(2, 0))
            sums[d, 1, j] = jnp.where(low, q(0, 0) + q(2, 1), q(1, 0) + q(3, 1))
            sums[d, 2, j] = jnp.where(low, q(1, 1), q(0, 0) + q(2, 1))
        for h in range(3):
            for j in range(3):
                s = sums[d, h, j]
                sums[d, h, j] = s + pltpu.roll(s, 64, 1)
    taps = [sums[t // 9, t // 3 % 3, t % 3] for t in range(27)] + [jnp.zeros((64, 128), F32)]
    for g in range(7):
        four = taps[4 * g : 4 * g + 4]
        turned = [pltpu.roll(x, 32, 1) for x in four]
        out_ref[g, 0] = jnp.where(low, jnp.where(block, four[0], turned[1]), jnp.where(block, four[2], turned[3]))
        out_ref[g, 1] = jnp.where(low, jnp.where(block, turned[0], four[1]), jnp.where(block, turned[2], four[3]))


def weight_two(where, g, one, a, two):
    return call(
        weight_two_kernel,
        [((7, 2, 64, 128), F32, pltpu.VMEM)],
        where, g, one, a, two,
        scratch=[pltpu.VMEM((3, T, 4 * T), BF16), pltpu.VMEM((3, T, 4 * T), BF16)],
    )[0]


def pack_kernel(where_ref, w3_ref, d3_ref, w2_ref, gh_ref, keep_ref, send_ref, pack_ref):
    for t in range(27):
        pack_ref[pl.ds(t, 128, stride=ROWS), :] = w3_ref[t]
    for k in range(4):
        pack_ref[pl.ds(DOWN3 + k, 128, stride=ROWS), :] = d3_ref[k]
    lane = lax.broadcasted_iota(jnp.int32, (64, 128), 1)
    for half in range(2):
        for g in range(6):
            pack_ref[pl.ds(half * ROWS + CONV2 + g, 64, stride=2 * ROWS), :] = w2_ref[g, half]
        heads = pltpu.roll(gh_ref[pl.ds(half, 64, stride=2), :], 96, 1)
        pack_ref[pl.ds(half * ROWS + CONV2 + 6, 64, stride=2 * ROWS), :] = jnp.where(lane < 96, w2_ref[6, half], heads)
    zero = jnp.zeros((128, 128), F32)
    pack_ref[pl.ds(DOWN2, 128, stride=ROWS), :] = zero
    pack_ref[pl.ds(DOWN2 + 1, 128, stride=ROWS), :] = zero
    keep_ref[...] = pack_ref[pl.ds(pl.multiple_of(where_ref[0] * 64 * ROWS, 64 * ROWS), 64 * ROWS), :]
    send_ref[...] = pack_ref[pl.ds(pl.multiple_of((1 - where_ref[0]) * 64 * ROWS, 64 * ROWS), 64 * ROWS), :].astype(BF16)


def packed(*args):
    half = (64 * ROWS, 128)
    return call(
        pack_kernel,
        [(half, F32, pltpu.VMEM), (half, BF16, pltpu.VMEM)],
        *args,
        scratch=[pltpu.VMEM((128 * ROWS, 128), F32)],
    )


def last_own_kernel(g_ref, b2_ref, out_ref, b_ref):
    for n in range(CROPS):
        for d in range(2):
            put_three(b_ref, (2 * n + d) * 3 * T, three_two(g_ref[n, d]))
        own = pl.ds(n * 6 * T, 6 * T)
        out_ref[n, 0] = dot(b2_ref[:, 3 * T :], b_ref[own, :])
        out_ref[n, 1] = dot(b2_ref[:, : 6 * T], b_ref[own, :])


def last_own(g, b2):
    return call(
        last_own_kernel,
        [((CROPS, 2, T, T), F32, pltpu.VMEM)],
        g, b2,
        scratch=[pltpu.VMEM((12 * T, T), BF16)],
    )[0]


def last_kernel(where_ref, one_ref, own_ref, two_ref, b2_ref, a_ref, vp_ref, perm_ref, down_ref, b_ref, t_ref):
    for n in range(CROPS):
        gy = []
        for d, plane in enumerate(sorted_out(where_ref, one_ref[n], two_ref[n])):
            at = (2 * n + d) * 3 * T
            put_three(b_ref, at, three_two(plane))
            rest = dot(b2_ref[:, d * 6 * T : d * 6 * T + 3 * T], b_ref[pl.ds(at, 3 * T), :])
            gy.append(((own_ref[n, d] + rest) * slope(a_ref[n, d])).astype(BF16))
        t = dot_nt(gy[0], vp_ref[n, 0]) + dot_nt(gy[1], vp_ref[n, 1])
        if n == 0:
            t_ref[...] = t
        else:
            t_ref[...] += t
    pairs = []
    lane = lax.broadcasted_iota(jnp.int32, (64, 128), 1)
    for tile in range(8):
        at = pl.ds(tile * 128, 128)
        x = jnp.zeros((64, 128), F32)
        for h in range(4):
            x = jnp.where(lane % 8 // 2 == h, t_ref[pl.ds(h * 64, 64), at], x)
        x = x + pltpu.roll(x, 126, 1)
        x = x + pltpu.roll(x, 124, 1)
        pairs.append(x.astype(BF16))
    down_ref[...] = dot(jnp.concatenate(pairs, axis=1), perm_ref[...])


def last(*args):
    return call(
        last_kernel,
        [((64, 256), F32, pltpu.VMEM)],
        *args,
        scratch=[pltpu.VMEM((12 * T, T), BF16), pltpu.VMEM((T, 1024), F32)],
    )[0]


def join_kernel(where_ref, down_ref, keep_ref, came_ref, out_ref, d_ref):
    for k, sec in enumerate((where_ref[0], 1 - where_ref[0])):
        mine = pl.ds(pl.multiple_of(sec * 32, 32), 32)
        for half in range(2):
            to = pl.ds(half * ROWS + DOWN2 + k, 32, stride=2 * ROWS)
            d_ref[to, :] = down_ref[mine, half * 128 : (half + 1) * 128]
    row = lax.broadcasted_iota(jnp.int32, (ROWS, 128), 0)
    for j in range(64):
        at = pl.ds(j * ROWS, ROWS)
        both = keep_ref[at, :] + came_ref[at, :].astype(F32)
        out_ref[at, :] = jnp.where(row >= DOWN2, d_ref[at, :], both).astype(BF16)


def joined(*args):
    return call(
        join_kernel,
        [((64 * ROWS, 128), BF16, pltpu.VMEM)],
        *args,
        scratch=[pltpu.VMEM((64 * ROWS, 128), F32)],
    )[0]


def swapped(one, two):
    count = lax.axis_size("space")
    near = [(i, i ^ 1) for i in range(count)]
    far = [(i, ((i + 1) ^ 1) - 1) for i in range(1, count - 1)]
    two = lax.ppermute(two, "space", far)
    return lax.ppermute(one, "space", near), two


def partner(x):
    return lax.ppermute(x, "section", [(0, 1), (1, 0)])


def flat(x, step):
    c = lax.broadcasted_iota(jnp.int32, (128, 128), 0) * step
    lane = lax.broadcasted_iota(jnp.int32, (128, 128), 1)
    x = x.T
    pieces = []
    for k in range(16):
        piece = x[8 * k : 8 * k + 8]
        for part in (step // 2, step - step // 2):
            piece = pltpu.roll(piece, 0, 1, stride=part, stride_axis=0)
        pieces.append(pltpu.roll(piece, 8 * k * step % 128, 1) if 8 * k * step % 128 else piece)
    turned = jnp.concatenate(pieces, axis=0)
    row = lax.broadcasted_iota(jnp.int32, (32, 128), 0)
    start = lax.broadcasted_iota(jnp.int32, (32, 128), 1) * step // 128
    exact = functools.partial(jnp.dot, precision=lax.Precision.HIGHEST, preferred_element_type=F32)
    here = lane >= c % 128
    same = exact(jnp.where(row == start, 1.0, 0.0), jnp.where(here, turned, 0.0))
    return same + exact(jnp.where(row == start + 1, 1.0, 0.0), jnp.where(here, 0.0, turned))


def unpack_kernel(sums_ref, two_ref, three_ref, conv_ref, x_ref):
    zero = jnp.zeros((128, 128), F32)
    x_ref[...] = zero
    x_ref[pl.ds(0, DOWN3), :] = sums_ref[pl.ds(0, DOWN3), :]
    conv_ref[...] = flat(x_ref[...], 27)[:27]
    x_ref[...] = zero
    lane = lax.broadcasted_iota(jnp.int32, (7, 128), 1)
    rows = sums_ref[pl.ds(CONV2, 7), :]
    for i in range(4):
        x_ref[pl.ds(i, 7, stride=4), :] = jnp.where(lane < 32, rows if i == 0 else pltpu.roll(rows, 128 - 32 * i, 1), 0.0)
    x_ref[pl.ds(27, 1), :] = jnp.zeros((1, 128), F32)
    two_ref[...] = flat(x_ref[...], 27)[:7]
    x_ref[...] = zero
    lane = lax.broadcasted_iota(jnp.int32, (1, 128), 1)
    for k in range(4):
        row = sums_ref[pl.ds(DOWN3 + k, 1), :]
        at = k // 2 * 4 + k % 2
        x_ref[pl.ds(at, 1), :] = jnp.where(lane < 64, row, 0.0)
        x_ref[pl.ds(at + 2, 1), :] = jnp.where(lane < 64, pltpu.roll(row, 64, 1), 0.0)
    three_ref[...] = flat(x_ref[...], 8)[:4]


def unpack(sums, down):
    two, three, conv = call(
        unpack_kernel,
        [((7, 128), F32, pltpu.VMEM), ((4, 128), F32, pltpu.HBM), ((27, 128), F32, pltpu.HBM)],
        sums,
        scratch=[pltpu.VMEM((128, 128), F32)],
    )
    return (
        down,
        two.reshape(-1)[: 27 * 32],
        three.reshape(-1),
        conv.reshape(-1),
        sums[DOWN2 - 1, 96:100],
    )


def finish(pack):
    terms = lax.all_to_all(pack, "space", 0, 0, tiled=True)
    sums = jnp.sum(terms.astype(F32), axis=0)
    return unpack(sums, sums[DOWN2] + partner(sums[DOWN2 + 1]))


def per_device(volume, labels, down_weight_two, w_conv_two, down_weight_three, w_conv_three, w_head):
    count = lax.axis_size("space")
    voxels = labels.shape[0] * labels.shape[1] * count * labels.shape[2] * labels.shape[3]
    scale = 1.0 / math.sqrt(voxels)
    sec = lax.axis_index("section").astype(jnp.int32)
    where = jnp.stack([sec, lax.axis_index("space").astype(jnp.int32) % 2])

    w1 = down_weight_two.transpose(1, 2, 3, 4, 0).reshape(256, 64)
    wd = down_weight_three.transpose(1, 2, 3, 4, 0).reshape(512, 128)
    w2 = w_conv_two.transpose(2, 3, 4, 0, 1).reshape(27, 64, 64)
    w2 = jnp.concatenate([w2, w2], axis=2)
    w3 = w_conv_three.transpose(2, 3, 4, 0, 1).reshape(27, 128, 128)
    marks = lax.dynamic_slice_in_dim(labels[:, 0], CROPS * sec, CROPS, axis=0)
    marks = marks.transpose(1, 0, 2).reshape(2, 256)

    vp, a2, one, two = first(where, volume, w1)
    a2_one, a2_two = swapped(one, two)
    f2, b2, f3, b3, perm, wd, wh = prepare(w2, w3, wd, w_head.T)
    own = second_own(a2, f2)
    a2_one, a2_two, own = lax.optimization_barrier((a2_one, a2_two, own))
    h2, a3 = second(where, a2_one, own, a2_two, f2, wd)
    a3_one, a3_two = swapped(a3, a3)
    own, sides, wh = head_own(a3, f3, wh)
    a3_one, a3_two, own, sides, wh = lax.optimization_barrier((a3_one, a3_two, own, sides, wh))
    gz4, gh = head(where, a3_one, own, a3_two, sides, wh, marks, scale)
    gz4_one, gz4_two = swapped(gz4, gz4)
    own = middle_own(gz4, b3)
    gw3 = weight_three(where, gz4, a3_one, a3, a3_two)
    gz4_one, gz4_two, gw3, own = lax.optimization_barrier((gz4_one, gz4_two, gw3, own))
    gz2, one, two, gd3 = middle(where, gz4_one, own, gz4_two, b3, a3, h2, wd)
    gz2_one, gz2_two = swapped(one, two)
    own = last_own(gz2, b2)
    gw2 = weight_two(where, gz2, a2_one, a2, a2_two)
    keep, send = packed(where, gw3, gd3, gw2, gh)
    gz2_one, gz2_two, send, own = lax.optimization_barrier((gz2_one, gz2_two, send, own))
    came = partner(send)
    down = last(where, gz2_one, own, gz2_two, b2, a2, vp, perm)
    pack = joined(where, down, keep, came)
    return finish(pack.reshape(64, ROWS, 128))


def solution(mesh):
    whole = P(("section", "space"))
    return jax.shard_map(
        per_device,
        mesh=mesh,
        in_specs=(P(None, None, "space", None, None), P(None, "space", None, None), P(), P(), P(), P(), P()),
        out_specs=(whole,) * 5,
        check_vma=False,
    )
```

```python
import functools
import math

import jax
import jax.numpy as jnp
from jax import lax
from jax.experimental import pallas as pl
from jax.experimental.pallas import tpu as pltpu
from jax.sharding import PartitionSpec as P


F32 = jnp.float32
BF16 = jnp.bfloat16
SHIFT = math.log(2.0)
CROPS = 2
T = 256
ROWS = 40
DOWN3, CONV2, DOWN2 = 27, 31, 38


def params(megabytes=12):
    return pltpu.CompilerParams(vmem_limit_bytes=megabytes << 20)


def rectified(v):
    return jnp.maximum(v, 0.0) + jnp.log1p(jnp.exp(-jnp.abs(v))) - SHIFT


def slope(stored):
    return 1.0 - 0.5 * jnp.exp(-stored.astype(F32))


def dot(a, b):
    return jnp.dot(a, b, preferred_element_type=F32)


def dot_tn(a, b):
    return lax.dot_general(a, b, (((0,), (0,)), ((), ())), preferred_element_type=F32)


def dot_nt(a, b):
    return lax.dot_general(a, b, (((1,), (1,)), ((), ())), preferred_element_type=F32)


def moved(x, by):
    x = x.astype(F32)
    lane = lax.broadcasted_iota(jnp.int32, x.shape, 1)
    edge = 0 if by == 1 else 127
    return jnp.where(lane == edge, 0.0, pltpu.roll(x, by % 128, 1)).astype(BF16)


def three_two(x):
    even, odd = x[:, :128], x[:, 128:]
    return ((moved(odd, 1), even), (even, odd), (odd, moved(even, -1)))


def three_three(x):
    first, second = x[:, :128], x[:, 128:]
    return ((moved(first, 1), moved(second, 1)), (first, second), (moved(first, -1), moved(second, -1)))


def put_three(ref, row, shifted):
    for j, (left, right) in enumerate(shifted):
        ref[pl.ds(row + j * T, T), 0:128] = left
        ref[pl.ds(row + j * T, T), 128:256] = right


def call(kernel, outs, *args, scratch=(), far=()):
    spec = pl.BlockSpec(memory_space=pltpu.VMEM)
    scalar = pl.BlockSpec(memory_space=pltpu.SMEM)
    remote = pl.BlockSpec(memory_space=pl.ANY)
    return pl.pallas_call(
        kernel,
        in_specs=[remote if i in far else scalar if a.dtype == jnp.int32 and a.ndim == 1 else spec for i, a in enumerate(args)],
        out_specs=[spec] * len(outs),
        out_shape=[space(s, d) for s, d, space in outs],
        scratch_shapes=list(scratch),
        compiler_params=params(),
    )(*[pltpu.with_memory_space_constraint(a, pltpu.HBM) if i in far else a for i, a in enumerate(args)])


def sorted_out(where_ref, one, two):
    even = where_ref[1] == 0
    return jnp.where(even, two, one), jnp.where(even, one, two)


def first_kernel(
    where_ref, vol_far, w_ref, vp_far, a_ref, one_ref, two_ref, sort_ref, wt_ref, vol_ref, vp_ref, in_sems, out_sems
):
    steps = [(n, d) for n in range(CROPS) for d in range(2)]
    fetches = [
        pltpu.make_async_copy(vol_far.at[CROPS * where_ref[0] + n, :, pl.ds(2 * d, 2)], vol_ref.at[i], in_sems.at[i])
        for i, (n, d) in enumerate(steps)
    ]
    stores = [
        pltpu.make_async_copy(vp_ref.at[i], vp_far.at[n, d], out_sems.at[i]) for i, (n, d) in enumerate(steps)
    ]
    for fetch in fetches:
        fetch.start()
    to = lax.broadcasted_iota(jnp.int32, (1, 512), 1)
    source = (to % 128) * 4 + (to // 128) % 2 * 2 + to // 256
    sort_ref[...] = jnp.where(lax.broadcasted_iota(jnp.int32, (512, 512), 0) == source, 1.0, 0.0).astype(BF16)
    to = lax.broadcasted_iota(jnp.int32, (1, 1024), 1)
    height = to % 8
    source = to // 8 % 32 * 8 + to // 512 * 4 + height % 2 * 2 + to // 256 % 2
    pick = jnp.where(lax.broadcasted_iota(jnp.int32, (256, 1024), 0) == source, 1.0, 0.0).astype(BF16)
    w = dot_tn(w_ref[...], pick)
    for h in range(4):
        wt_ref[pl.ds(h * 64, 64), :] = jnp.where(height // 2 == h, w, 0.0).astype(BF16)
    for i, (n, d) in enumerate(steps):
        fetches[i].wait()
        for k in range(2):
            v = vol_ref[i, :, k].astype(F32).reshape(256, 512).astype(BF16)
            s = dot(v, sort_ref[...]).astype(BF16)
            vp_ref[i, pl.ds(k * 512, 256), :] = s[:, :256]
            vp_ref[i, pl.ds(k * 512 + 256, 256), :] = s[:, 256:]
        stores[i].start()
        a_ref[n, d] = rectified(dot(wt_ref[...], vp_ref[i])).astype(BF16)
    even = where_ref[1] == 0
    for n in range(CROPS):
        one_ref[n] = jnp.where(even, a_ref[n, 1], a_ref[n, 0])
        two_ref[n] = jnp.where(even, a_ref[n, 0], a_ref[n, 1])
    for store in stores:
        store.wait()


def first(where, volume, w1):
    spec = pl.BlockSpec(memory_space=pltpu.VMEM)
    far = pl.BlockSpec(memory_space=pl.ANY)
    return pl.pallas_call(
        first_kernel,
        in_specs=[pl.BlockSpec(memory_space=pltpu.SMEM), far, spec],
        out_specs=[far, spec, spec, spec],
        out_shape=[
            pltpu.HBM((CROPS, 2, 1024, 256), BF16),
            pltpu.VMEM((CROPS, 2, 256, 256), BF16),
            pltpu.VMEM((CROPS, 256, 256), BF16),
            pltpu.VMEM((CROPS, 256, 256), BF16),
        ],
        scratch_shapes=[
            pltpu.VMEM((512, 512), BF16),
            pltpu.VMEM((256, 1024), BF16),
            pltpu.VMEM((4, 32, 2, 8, 512), BF16),
            pltpu.VMEM((4, 1024, 256), BF16),
            pltpu.SemaphoreType.DMA((4,)),
            pltpu.SemaphoreType.DMA((4,)),
        ],
        compiler_params=params(),
    )(where, pltpu.with_memory_space_constraint(volume, pltpu.HBM), pltpu.with_memory_space_constraint(w1, pltpu.HBM))


def prepare_kernel(
    w2_ref, w3_far, wd_ref, head_ref, f2_ref, b2_ref, f3_ref, b3_ref, perm_ref, d_ref, wh_ref, rows_ref, w3_ref, sem
):
    fetch = pltpu.make_async_copy(w3_far, w3_ref, sem)
    fetch.start()
    low = lax.broadcasted_iota(jnp.int32, (64, 128), 1) < 64
    zero = jnp.zeros((64, 128), F32)
    for d in range(3):
        for j in range(3):
            at = (d * 3 + j) * T
            back = (8 - d * 3 - j) * T
            w = [w2_ref[d * 9 + h * 3 + j].astype(F32) for h in range(3)]
            pairs = {
                (0, 0): jnp.where(low, w[1], w[2]),
                (0, 1): zero,
                (1, 0): jnp.where(low, w[0], w[1]),
                (1, 1): jnp.where(low, w[2], 0.0),
                (2, 0): jnp.where(low, 0.0, w[0]),
                (2, 1): jnp.where(low, w[1], w[2]),
                (3, 0): zero,
                (3, 1): jnp.where(low, w[0], w[1]),
            }
            for (row, col), block in pairs.items():
                f2_ref[pl.ds(row * 64, 64), pl.ds(at + col * 128, 128)] = block.astype(BF16)
            b2_ref[:, pl.ds(back, T)] = f2_ref[:, pl.ds(at, T)].astype(F32).T.astype(BF16)
    rows_ref[...] = wd_ref[...].astype(F32)
    for d in range(2):
        for p in range(2):
            for h in range(4):
                block = rows_ref[pl.ds(d * 4 + h % 2 * 2 + p, 64, stride=8), :].astype(BF16)
                d_ref[2 * d + p, pl.ds(h * 64, 64), pl.ds(h // 2 * 128, 128)] = block
                d_ref[2 * d + p, pl.ds(h * 64, 64), pl.ds(128 - h // 2 * 128, 128)] = jnp.zeros_like(block)
    rows_ref[pl.ds(0, 128), :] = jnp.zeros((128, 128), F32)
    rows_ref[pl.ds(0, 4), :] = head_ref[...].astype(F32)
    wht = rows_ref[pl.ds(0, 128), :]
    wh_ref[pl.ds(0, 128), :] = wht.T.astype(BF16)
    wh_ref[pl.ds(128, 128), :] = wht.astype(BF16)
    to = lax.broadcasted_iota(jnp.int32, (1, 256), 1)
    source = to // 4 % 2 * 512 + to % 2 * 256 + (to // 128 * 16 + to // 8 % 16) * 8 + to // 2 % 2
    perm_ref[...] = jnp.where(lax.broadcasted_iota(jnp.int32, (1024, 256), 0) == source, 1.0, 0.0).astype(BF16)
    fetch.wait()
    for d in range(3):
        for j in range(3):
            at = (d * 3 + j) * T
            back = (8 - d * 3 - j) * T
            for row in range(2):
                for col in range(2):
                    block = w3_ref[d * 9 + (col - row + 1) * 3 + j]
                    f3_ref[pl.ds(row * 128, 128), pl.ds(at + col * 128, 128)] = block
                    b3_ref[pl.ds(col * 128, 128), pl.ds(back + row * 128, 128)] = block.astype(F32).T.astype(BF16)


def prepare(w2, w3, wd, wh):
    def wide(space):
        return ((T, 9 * T), BF16, space)

    return call(
        prepare_kernel,
        [wide(pltpu.VMEM), wide(pltpu.HBM), wide(pltpu.HBM), wide(pltpu.HBM)]
        + [((1024, 256), BF16, pltpu.HBM), ((4, T, T), BF16, pltpu.VMEM), ((256, 128), BF16, pltpu.HBM)],
        w2, w3, wd, wh,
        scratch=[pltpu.VMEM((512, 128), F32), pltpu.VMEM((27, 128, 128), BF16), pltpu.SemaphoreType.DMA],
        far=(1,),
    )


def second_own_kernel(a_ref, f2_ref, out_ref, b_ref):
    for n in range(CROPS):
        for d in range(2):
            put_three(b_ref, (2 * n + d) * 3 * T, three_two(a_ref[n, d]))
        own = pl.ds(n * 6 * T, 6 * T)
        out_ref[n, 0] = dot(f2_ref[:, 3 * T :], b_ref[own, :])
        out_ref[n, 1] = dot(f2_ref[:, : 6 * T], b_ref[own, :])


def second_own(a, f2):
    return call(
        second_own_kernel,
        [((CROPS, 2, T, T), F32, pltpu.VMEM)],
        a, f2,
        scratch=[pltpu.VMEM((12 * T, T), BF16)],
    )[0]


def second_kernel(
    where_ref, one_ref, own_ref, two_ref, f2_ref, wd_ref, marks_ref, h_ref, a3_ref, sent_ref, sides_ref, b_ref, m_ref
):
    for n in range(CROPS):
        for d, plane in enumerate(sorted_out(where_ref, one_ref[n], two_ref[n])):
            at = (2 * n + d) * 3 * T
            sides_ref[n, d] = plane
            put_three(b_ref, at, three_two(plane))
            rest = dot(f2_ref[:, d * 6 * T : d * 6 * T + 3 * T], b_ref[pl.ds(at, 3 * T), :])
            h = rectified(own_ref[n, d] + rest).astype(BF16)
            for p in range(2):
                h_ref[2 * d + p, :, pl.ds(n * 128, 128)] = h[:, p * 128 : (p + 1) * 128]
    total = dot_tn(wd_ref[0], h_ref[0])
    for k in range(1, 4):
        total += dot_tn(wd_ref[k], h_ref[k])
    a3 = rectified(total).astype(BF16)
    a3_ref[...] = a3
    m_ref[...] = jnp.zeros((16, T), F32)
    m_ref[pl.ds(0, 2), :] = marks_ref[...].astype(F32)
    sent_ref[pl.ds(0, T), :] = a3
    sent_ref[pl.ds(T, 16), :] = m_ref[...].astype(BF16)


def second(where, one, own, two, f2, wd, marks):
    return call(
        second_kernel,
        [
            ((4, T, T), BF16, pltpu.HBM),
            ((T, T), BF16, pltpu.VMEM),
            ((T + 16, T), BF16, pltpu.VMEM),
            ((CROPS, 2, T, T), BF16, pltpu.HBM),
        ],
        where, one, own, two, f2, wd, marks,
        scratch=[pltpu.VMEM((12 * T, T), BF16), pltpu.VMEM((16, T), F32)],
    )


def head_own_kernel(a_ref, f3_ref, wh_ref, out_ref, f3_out_ref, wh_out_ref, b_ref):
    put_three(b_ref, 0, three_three(a_ref[...]))
    for k in range(3):
        out_ref[k] = dot(f3_ref[:, (2 - k) * 3 * T : (3 - k) * 3 * T], b_ref[...])
    f3_out_ref[...] = f3_ref[...]
    wh_out_ref[...] = wh_ref[...]


def head_own(a, f3, wh):
    return call(
        head_own_kernel,
        [((3, T, T), F32, pltpu.VMEM), ((T, 9 * T), BF16, pltpu.VMEM), ((256, 128), BF16, pltpu.VMEM)],
        a, f3, wh,
        scratch=[pltpu.VMEM((3 * T, T), BF16)],
    )


def head_kernel(
    scale, where_ref, one_ref, two_ref, near_ref, away_ref, own_ref, f3_ref, wh_ref, marks_ref, gz_ref, gh_ref, b_ref
):
    lo, hi = sorted_out(where_ref, one_ref[...], two_ref[...])
    low_half = where_ref[2] == 0
    lo2 = jnp.where(low_half, away_ref[...], near_ref[...])
    hi2 = jnp.where(low_half, near_ref[...], away_ref[...])
    for k, plane in enumerate((lo2, lo[:T], hi[:T], hi2)):
        put_three(b_ref, k * 3 * T, three_three(plane))
    sums = (
        own_ref[0] + dot(f3_ref[:, : 6 * T], b_ref[: 6 * T, :]),
        own_ref[1] + dot(f3_ref[:, : 3 * T], b_ref[3 * T : 6 * T, :]) + dot(f3_ref[:, 6 * T :], b_ref[6 * T : 9 * T, :]),
        own_ref[2] + dot(f3_ref[:, 3 * T :], b_ref[6 * T :, :]),
    )
    marks = (lo[T:].astype(F32), marks_ref[...].astype(F32), hi[T:].astype(F32))
    row = lax.broadcasted_iota(jnp.int32, (128, T), 0)
    total = jnp.zeros((128, 128), F32)
    for k in range(3):
        top = rectified(sums[k]).astype(BF16)
        for h in range(2):
            mine = top[h * 128 : (h + 1) * 128]
            logits = dot(wh_ref[pl.ds(128, 128), :], mine)
            powers = jnp.where(row < 4, jnp.exp(logits), 0.0)
            share = powers / jnp.sum(powers, axis=0, keepdims=True)
            chosen = jnp.where(row.astype(F32) == marks[k][h : h + 1], 1.0, 0.0)
            g = jnp.where(row < 4, (share - chosen) * scale, 0.0)
            if k != 1:
                g = jnp.where(where_ref[3 + k // 2] == 1, g, 0.0)
            g = g.astype(BF16)
            if k == 1:
                total += dot_nt(mine, g)
            gz_ref[k, pl.ds(h * 128, 128), :] = (dot(wh_ref[pl.ds(0, 128), :], g) * slope(mine)).astype(BF16)
    gh_ref[...] = total


def head(where, one, two, near, away, own, f3, wh, marks, scale):
    return call(
        functools.partial(head_kernel, scale),
        [((3, T, T), BF16, pltpu.VMEM), ((128, 128), F32, pltpu.VMEM)],
        where, one, two, near, away, own, f3, wh, marks,
        scratch=[pltpu.VMEM((12 * T, T), BF16)],
    )


def weight_three_kernel(where_ref, g_ref, one_ref, a_ref, two_ref, out_ref, s_ref):
    put_three(s_ref, 0, three_three(g_ref[1]))
    lo, hi = sorted_out(where_ref, one_ref[:T], two_ref[:T])
    for d, a in enumerate((lo, a_ref[...], hi)):
        for j in range(3):
            t = dot_nt(s_ref[pl.ds((2 - j) * T, T), :], a)
            out_ref[d * 9 + j] = t[128:, :128]
            out_ref[d * 9 + 3 + j] = t[:128, :128] + t[128:, 128:]
            out_ref[d * 9 + 6 + j] = t[:128, 128:]


def weight_three(where, g, one, a, two):
    return call(
        weight_three_kernel,
        [((27, 128, 128), F32, pltpu.VMEM)],
        where, g, one, a, two,
        scratch=[pltpu.VMEM((3 * T, T), BF16)],
    )[0]


def middle_kernel(where_ref, g_ref, b3_ref, a3_ref, h_ref, wd_ref, gz2_ref, gone_ref, gtwo_ref, gd_ref, b_ref):
    for k in range(3):
        put_three(b_ref, k * 3 * T, three_three(g_ref[k]))
    rest = dot(b3_ref[...], b_ref[...])
    gy = (rest * slope(a3_ref[...])).astype(BF16)
    for d in range(2):
        for p in range(2):
            k = 2 * d + p
            q = (dot(wd_ref[k], gy) * slope(h_ref[k])).astype(BF16)
            for n in range(CROPS):
                gz2_ref[n, d, :, pl.ds(p * 128, 128)] = q[:, n * 128 : (n + 1) * 128]
    even = where_ref[1] == 0
    for n in range(CROPS):
        gone_ref[n] = jnp.where(even, gz2_ref[n, 1], gz2_ref[n, 0])
        gtwo_ref[n] = jnp.where(even, gz2_ref[n, 0], gz2_ref[n, 1])
    for k in range(4):
        gd_ref[k] = dot_nt(gy[:128], h_ref[k, :128]) + dot_nt(gy[128:], h_ref[k, 128:])


def middle(where, g, b3, a3, h, wd):
    return call(
        middle_kernel,
        [
            ((CROPS, 2, T, T), BF16, pltpu.VMEM),
            ((CROPS, T, T), BF16, pltpu.VMEM),
            ((CROPS, T, T), BF16, pltpu.VMEM),
            ((4, 128, 128), F32, pltpu.VMEM),
        ],
        where, g, b3, a3, h, wd,
        scratch=[pltpu.VMEM((9 * T, T), BF16)],
    )


def weight_two_kernel(g_ref, a_ref, sides_ref, out_ref, gs_ref, as_ref):
    for n in range(CROPS):
        planes = (sides_ref[n, 0], a_ref[n, 0], a_ref[n, 1], sides_ref[n, 1])
        for d in range(2):
            at = (2 * n + d) * T
            for j, (left, right) in enumerate(three_two(g_ref[n, d])):
                gs_ref[2 - j, :, pl.ds(at, 128)] = left
                gs_ref[2 - j, :, pl.ds(at + 128, 128)] = right
            for k in range(3):
                as_ref[k, :, pl.ds(at, T)] = planes[d + k]
    low = lax.broadcasted_iota(jnp.int32, (64, 128), 1) < 64
    block = (lax.broadcasted_iota(jnp.int32, (64, 128), 1) // 32) % 2 == 0
    sums = {}
    for d in range(3):
        for j in range(3):
            t = dot_nt(gs_ref[j], as_ref[d])
            q = lambda r, c: t[r * 64 : (r + 1) * 64, c * 128 : (c + 1) * 128]
            sums[d, 0, j] = jnp.where(low, q(1, 0) + q(3, 1), q(2, 0))
            sums[d, 1, j] = jnp.where(low, q(0, 0) + q(2, 1), q(1, 0) + q(3, 1))
            sums[d, 2, j] = jnp.where(low, q(1, 1), q(0, 0) + q(2, 1))
        for h in range(3):
            for j in range(3):
                s = sums[d, h, j]
                sums[d, h, j] = s + pltpu.roll(s, 64, 1)
    taps = [sums[t // 9, t // 3 % 3, t % 3] for t in range(27)] + [jnp.zeros((64, 128), F32)]
    for g in range(7):
        four = taps[4 * g : 4 * g + 4]
        turned = [pltpu.roll(x, 32, 1) for x in four]
        out_ref[g, 0] = jnp.where(low, jnp.where(block, four[0], turned[1]), jnp.where(block, four[2], turned[3]))
        out_ref[g, 1] = jnp.where(low, jnp.where(block, turned[0], four[1]), jnp.where(block, turned[2], four[3]))


def weight_two(g, a, sides):
    return call(
        weight_two_kernel,
        [((7, 2, 64, 128), F32, pltpu.VMEM)],
        g, a, sides,
        scratch=[pltpu.VMEM((3, T, 4 * T), BF16), pltpu.VMEM((3, T, 4 * T), BF16)],
    )[0]


def pack_kernel(where_ref, w3_ref, d3_ref, w2_ref, gh_ref, keep_ref, send_ref, pack_ref):
    for t in range(27):
        pack_ref[pl.ds(t, 128, stride=ROWS), :] = w3_ref[t]
    for k in range(4):
        pack_ref[pl.ds(DOWN3 + k, 128, stride=ROWS), :] = d3_ref[k]
    lane = lax.broadcasted_iota(jnp.int32, (64, 128), 1)
    for half in range(2):
        for g in range(6):
            pack_ref[pl.ds(half * ROWS + CONV2 + g, 64, stride=2 * ROWS), :] = w2_ref[g, half]
        heads = pltpu.roll(gh_ref[pl.ds(half, 64, stride=2), :], 96, 1)
        pack_ref[pl.ds(half * ROWS + CONV2 + 6, 64, stride=2 * ROWS), :] = jnp.where(lane < 96, w2_ref[6, half], heads)
    zero = jnp.zeros((128, 128), F32)
    pack_ref[pl.ds(DOWN2, 128, stride=ROWS), :] = zero
    pack_ref[pl.ds(DOWN2 + 1, 128, stride=ROWS), :] = zero
    keep_ref[...] = pack_ref[pl.ds(pl.multiple_of(where_ref[0] * 64 * ROWS, 64 * ROWS), 64 * ROWS), :]
    send_ref[...] = pack_ref[pl.ds(pl.multiple_of((1 - where_ref[0]) * 64 * ROWS, 64 * ROWS), 64 * ROWS), :].astype(BF16)


def packed(*args):
    half = (64 * ROWS, 128)
    return call(
        pack_kernel,
        [(half, F32, pltpu.VMEM), (half, BF16, pltpu.VMEM)],
        *args,
        scratch=[pltpu.VMEM((128 * ROWS, 128), F32)],
    )


def last_own_kernel(g_ref, b2_ref, out_ref, b_ref):
    for n in range(CROPS):
        for d in range(2):
            put_three(b_ref, (2 * n + d) * 3 * T, three_two(g_ref[n, d]))
        own = pl.ds(n * 6 * T, 6 * T)
        out_ref[n, 0] = dot(b2_ref[:, 3 * T :], b_ref[own, :])
        out_ref[n, 1] = dot(b2_ref[:, : 6 * T], b_ref[own, :])


def last_own(g, b2):
    return call(
        last_own_kernel,
        [((CROPS, 2, T, T), F32, pltpu.VMEM)],
        g, b2,
        scratch=[pltpu.VMEM((12 * T, T), BF16)],
    )[0]


def last_kernel(where_ref, one_ref, own_ref, two_ref, b2_ref, a_ref, vp_ref, perm_ref, down_ref, b_ref, t_ref):
    for n in range(CROPS):
        gy = []
        for d, plane in enumerate(sorted_out(where_ref, one_ref[n], two_ref[n])):
            at = (2 * n + d) * 3 * T
            put_three(b_ref, at, three_two(plane))
            rest = dot(b2_ref[:, d * 6 * T : d * 6 * T + 3 * T], b_ref[pl.ds(at, 3 * T), :])
            gy.append(((own_ref[n, d] + rest) * slope(a_ref[n, d])).astype(BF16))
        t = dot_nt(gy[0], vp_ref[n, 0]) + dot_nt(gy[1], vp_ref[n, 1])
        if n == 0:
            t_ref[...] = t
        else:
            t_ref[...] += t
    pairs = []
    lane = lax.broadcasted_iota(jnp.int32, (64, 128), 1)
    for tile in range(8):
        at = pl.ds(tile * 128, 128)
        x = jnp.zeros((64, 128), F32)
        for h in range(4):
            x = jnp.where(lane % 8 // 2 == h, t_ref[pl.ds(h * 64, 64), at], x)
        x = x + pltpu.roll(x, 126, 1)
        x = x + pltpu.roll(x, 124, 1)
        pairs.append(x.astype(BF16))
    down_ref[...] = dot(jnp.concatenate(pairs, axis=1), perm_ref[...])


def last(*args):
    return call(
        last_kernel,
        [((64, 256), F32, pltpu.VMEM)],
        *args,
        scratch=[pltpu.VMEM((12 * T, T), BF16), pltpu.VMEM((T, 1024), F32)],
    )[0]


def join_kernel(where_ref, down_ref, keep_ref, came_ref, out_ref, d_ref):
    for k, sec in enumerate((where_ref[0], 1 - where_ref[0])):
        mine = pl.ds(pl.multiple_of(sec * 32, 32), 32)
        for half in range(2):
            to = pl.ds(half * ROWS + DOWN2 + k, 32, stride=2 * ROWS)
            d_ref[to, :] = down_ref[mine, half * 128 : (half + 1) * 128]
    row = lax.broadcasted_iota(jnp.int32, (ROWS, 128), 0)
    for j in range(64):
        at = pl.ds(j * ROWS, ROWS)
        both = keep_ref[at, :] + came_ref[at, :].astype(F32)
        out_ref[at, :] = jnp.where(row >= DOWN2, d_ref[at, :], both).astype(BF16)


def joined(*args):
    return call(
        join_kernel,
        [((64 * ROWS, 128), BF16, pltpu.VMEM)],
        *args,
        scratch=[pltpu.VMEM((64 * ROWS, 128), F32)],
    )[0]


def swapped(one, two):
    count = lax.axis_size("space")
    near = [(i, i ^ 1) for i in range(count)]
    far = [(i, ((i + 1) ^ 1) - 1) for i in range(1, count - 1)]
    two = lax.ppermute(two, "space", far)
    return lax.ppermute(one, "space", near), two


def swapped_two(x):
    count = lax.axis_size("space")
    near = [(i, i ^ 2) for i in range(count)]
    away = [(i, ((i + 2) ^ 2) - 2) for i in range(2, count - 2)]
    away = lax.ppermute(x, "space", away)
    return lax.ppermute(x, "space", near), away


def partner(x):
    return lax.ppermute(x, "section", [(0, 1), (1, 0)])


def flat(x, step):
    c = lax.broadcasted_iota(jnp.int32, (128, 128), 0) * step
    lane = lax.broadcasted_iota(jnp.int32, (128, 128), 1)
    x = x.T
    pieces = []
    for k in range(16):
        piece = x[8 * k : 8 * k + 8]
        for part in (step // 2, step - step // 2):
            piece = pltpu.roll(piece, 0, 1, stride=part, stride_axis=0)
        pieces.append(pltpu.roll(piece, 8 * k * step % 128, 1) if 8 * k * step % 128 else piece)
    turned = jnp.concatenate(pieces, axis=0)
    row = lax.broadcasted_iota(jnp.int32, (32, 128), 0)
    start = lax.broadcasted_iota(jnp.int32, (32, 128), 1) * step // 128
    exact = functools.partial(jnp.dot, precision=lax.Precision.HIGHEST, preferred_element_type=F32)
    here = lane >= c % 128
    same = exact(jnp.where(row == start, 1.0, 0.0), jnp.where(here, turned, 0.0))
    return same + exact(jnp.where(row == start + 1, 1.0, 0.0), jnp.where(here, 0.0, turned))


def unpack_kernel(sums_ref, two_ref, three_ref, conv_ref, x_ref):
    zero = jnp.zeros((128, 128), F32)
    x_ref[...] = zero
    x_ref[pl.ds(0, DOWN3), :] = sums_ref[pl.ds(0, DOWN3), :]
    conv_ref[...] = flat(x_ref[...], 27)[:27]
    x_ref[...] = zero
    lane = lax.broadcasted_iota(jnp.int32, (7, 128), 1)
    rows = sums_ref[pl.ds(CONV2, 7), :]
    for i in range(4):
        x_ref[pl.ds(i, 7, stride=4), :] = jnp.where(lane < 32, rows if i == 0 else pltpu.roll(rows, 128 - 32 * i, 1), 0.0)
    x_ref[pl.ds(27, 1), :] = jnp.zeros((1, 128), F32)
    two_ref[...] = flat(x_ref[...], 27)[:7]
    x_ref[...] = zero
    lane = lax.broadcasted_iota(jnp.int32, (1, 128), 1)
    for k in range(4):
        row = sums_ref[pl.ds(DOWN3 + k, 1), :]
        at = k // 2 * 4 + k % 2
        x_ref[pl.ds(at, 1), :] = jnp.where(lane < 64, row, 0.0)
        x_ref[pl.ds(at + 2, 1), :] = jnp.where(lane < 64, pltpu.roll(row, 64, 1), 0.0)
    three_ref[...] = flat(x_ref[...], 8)[:4]


def unpack(sums, down):
    two, three, conv = call(
        unpack_kernel,
        [((7, 128), F32, pltpu.VMEM), ((4, 128), F32, pltpu.HBM), ((27, 128), F32, pltpu.HBM)],
        sums,
        scratch=[pltpu.VMEM((128, 128), F32)],
    )
    return (
        down,
        two.reshape(-1)[: 27 * 32],
        three.reshape(-1),
        conv.reshape(-1),
        sums[DOWN2 - 1, 96:100],
    )


def finish(pack):
    terms = lax.all_to_all(pack, "space", 0, 0, tiled=True)
    sums = jnp.sum(terms.astype(F32), axis=0)
    return unpack(sums, sums[DOWN2] + partner(sums[DOWN2 + 1]))


def per_device(volume, labels, down_weight_two, w_conv_two, down_weight_three, w_conv_three, w_head):
    count = lax.axis_size("space")
    voxels = labels.shape[0] * labels.shape[1] * count * labels.shape[2] * labels.shape[3]
    scale = 1.0 / math.sqrt(voxels)
    sec = lax.axis_index("section").astype(jnp.int32)
    space = lax.axis_index("space").astype(jnp.int32)
    where = jnp.stack([sec, space % 2, space % 4 // 2, jnp.minimum(space, 1), jnp.minimum(count - 1 - space, 1)])

    w1 = down_weight_two.transpose(1, 2, 3, 4, 0).reshape(256, 64)
    wd = down_weight_three.transpose(1, 2, 3, 4, 0).reshape(512, 128)
    w2 = w_conv_two.transpose(2, 3, 4, 0, 1).reshape(27, 64, 64)
    w2 = jnp.concatenate([w2, w2], axis=2)
    w3 = w_conv_three.transpose(2, 3, 4, 0, 1).reshape(27, 128, 128)
    marks = lax.dynamic_slice_in_dim(labels[:, 0], CROPS * sec, CROPS, axis=0)
    marks = marks.transpose(1, 0, 2).reshape(2, 256)

    vp, a2, one, two = first(where, volume, w1)
    a2_one, a2_two = swapped(one, two)
    f2, b2, f3, b3, perm, wd, wh = prepare(w2, w3, wd, w_head.T)
    own = second_own(a2, f2)
    a2_one, a2_two, own = lax.optimization_barrier((a2_one, a2_two, own))
    h2, a3, sent, sides = second(where, a2_one, own, a2_two, f2, wd, marks)
    a3_one, a3_two = swapped(sent, sent)
    a3_near, a3_away = swapped_two(a3)
    own, f3, wh = head_own(a3, f3, wh)
    a3_one, a3_two, a3_near, a3_away, own, f3, wh = lax.optimization_barrier(
        (a3_one, a3_two, a3_near, a3_away, own, f3, wh)
    )
    gz4, gh = head(where, a3_one, a3_two, a3_near, a3_away, own, f3, wh, marks, scale)
    gz2, one, two, gd3 = middle(where, gz4, b3, a3, h2, wd)
    gw3 = weight_three(where, gz4, a3_one, a3, a3_two)
    gz2_one, gz2_two = swapped(one, two)
    own = last_own(gz2, b2)
    gw2 = weight_two(gz2, a2, sides)
    keep, send = packed(where, gw3, gd3, gw2, gh)
    gz2_one, gz2_two, send, own = lax.optimization_barrier((gz2_one, gz2_two, send, own))
    came = partner(send)
    down = last(where, gz2_one, own, gz2_two, b2, a2, vp, perm)
    pack = joined(where, down, keep, came)
    return finish(pack.reshape(64, ROWS, 128))


def solution(mesh):
    whole = P(("section", "space"))
    return jax.shard_map(
        per_device,
        mesh=mesh,
        in_specs=(P(None, None, "space", None, None), P(None, "space", None, None), P(), P(), P(), P(), P()),
        out_specs=(whole,) * 5,
        check_vma=False,
    )
```

```python
import functools
import math

import jax
import jax.numpy as jnp
from jax import lax
from jax.experimental import pallas as pl
from jax.experimental.pallas import tpu as pltpu
from jax.sharding import PartitionSpec as P


F32 = jnp.float32
BF16 = jnp.bfloat16
SHIFT = math.log(2.0)
CROPS = 2
T = 256
ROWS = 40
DOWN3, CONV2, DOWN2 = 27, 31, 38


def params(megabytes=12):
    return pltpu.CompilerParams(vmem_limit_bytes=megabytes << 20)


def rectified(v):
    return jnp.maximum(v, 0.0) + jnp.log1p(jnp.exp(-jnp.abs(v))) - SHIFT


def slope(stored):
    return 1.0 - 0.5 * jnp.exp(-stored.astype(F32))


def dot(a, b):
    return jnp.dot(a, b, preferred_element_type=F32)


def dot_tn(a, b):
    return lax.dot_general(a, b, (((0,), (0,)), ((), ())), preferred_element_type=F32)


def dot_nt(a, b):
    return lax.dot_general(a, b, (((1,), (1,)), ((), ())), preferred_element_type=F32)


def moved(x, by):
    x = x.astype(F32)
    lane = lax.broadcasted_iota(jnp.int32, x.shape, 1)
    edge = 0 if by == 1 else 127
    return jnp.where(lane == edge, 0.0, pltpu.roll(x, by % 128, 1)).astype(BF16)


def three_two(x):
    even, odd = x[:, :128], x[:, 128:]
    return ((moved(odd, 1), even), (even, odd), (odd, moved(even, -1)))


def three_three(x):
    first, second = x[:, :128], x[:, 128:]
    return ((moved(first, 1), moved(second, 1)), (first, second), (moved(first, -1), moved(second, -1)))


def put_three(ref, row, shifted):
    for j, (left, right) in enumerate(shifted):
        ref[pl.ds(row + j * T, T), 0:128] = left
        ref[pl.ds(row + j * T, T), 128:256] = right


def call(kernel, outs, *args, scratch=(), far=()):
    spec = pl.BlockSpec(memory_space=pltpu.VMEM)
    scalar = pl.BlockSpec(memory_space=pltpu.SMEM)
    remote = pl.BlockSpec(memory_space=pl.ANY)
    return pl.pallas_call(
        kernel,
        in_specs=[remote if i in far else scalar if a.dtype == jnp.int32 and a.ndim == 1 else spec for i, a in enumerate(args)],
        out_specs=[spec] * len(outs),
        out_shape=[space(s, d) for s, d, space in outs],
        scratch_shapes=list(scratch),
        compiler_params=params(),
    )(*[pltpu.with_memory_space_constraint(a, pltpu.HBM) if i in far else a for i, a in enumerate(args)])


def sorted_out(where_ref, one, two):
    even = where_ref[1] == 0
    return jnp.where(even, two, one), jnp.where(even, one, two)


def first_kernel(
    where_ref, vol_far, w_ref, vp_far, a_ref, one_ref, two_ref, sort_ref, wt_ref, vol_ref, vp_ref, in_sems, out_sems
):
    steps = [(n, d) for n in range(CROPS) for d in range(2)]
    fetches = [
        pltpu.make_async_copy(vol_far.at[CROPS * where_ref[0] + n], vol_ref.at[n], in_sems.at[n]) for n in range(CROPS)
    ]
    stores = [
        pltpu.make_async_copy(vp_ref.at[i], vp_far.at[n, d], out_sems.at[i]) for i, (n, d) in enumerate(steps)
    ]
    for fetch in fetches:
        fetch.start()
    to = lax.broadcasted_iota(jnp.int32, (1, 512), 1)
    source = (to % 128) * 4 + (to // 128) % 2 * 2 + to // 256
    sort_ref[...] = jnp.where(lax.broadcasted_iota(jnp.int32, (512, 512), 0) == source, 1.0, 0.0).astype(BF16)
    to = lax.broadcasted_iota(jnp.int32, (1, 1024), 1)
    height = to % 8
    source = to // 8 % 32 * 8 + to // 512 * 4 + height % 2 * 2 + to // 256 % 2
    pick = jnp.where(lax.broadcasted_iota(jnp.int32, (256, 1024), 0) == source, 1.0, 0.0).astype(BF16)
    w = dot_tn(w_ref[...], pick)
    for h in range(4):
        wt_ref[pl.ds(h * 64, 64), :] = jnp.where(height // 2 == h, w, 0.0).astype(BF16)
    for i, (n, d) in enumerate(steps):
        if d == 0:
            fetches[n].wait()
        for k in range(2):
            v = vol_ref[n, :, 2 * d + k].astype(F32).reshape(256, 512).astype(BF16)
            s = dot(v, sort_ref[...]).astype(BF16)
            vp_ref[i, pl.ds(k * 512, 256), :] = s[:, :256]
            vp_ref[i, pl.ds(k * 512 + 256, 256), :] = s[:, 256:]
        stores[i].start()
        a_ref[n, d] = rectified(dot(wt_ref[...], vp_ref[i])).astype(BF16)
    even = where_ref[1] == 0
    for n in range(CROPS):
        one_ref[n] = jnp.where(even, a_ref[n, 1], a_ref[n, 0])
        two_ref[n] = jnp.where(even, a_ref[n, 0], a_ref[n, 1])
    for store in stores:
        store.wait()


def first(where, volume, w1):
    spec = pl.BlockSpec(memory_space=pltpu.VMEM)
    far = pl.BlockSpec(memory_space=pl.ANY)
    return pl.pallas_call(
        first_kernel,
        in_specs=[pl.BlockSpec(memory_space=pltpu.SMEM), far, spec],
        out_specs=[far, spec, spec, spec],
        out_shape=[
            pltpu.HBM((CROPS, 2, 1024, 256), BF16),
            pltpu.VMEM((CROPS, 2, 256, 256), BF16),
            pltpu.VMEM((CROPS, 256, 256), BF16),
            pltpu.VMEM((CROPS, 256, 256), BF16),
        ],
        scratch_shapes=[
            pltpu.VMEM((512, 512), BF16),
            pltpu.VMEM((256, 1024), BF16),
            pltpu.VMEM((CROPS, 32, 4, 8, 512), BF16),
            pltpu.VMEM((4, 1024, 256), BF16),
            pltpu.SemaphoreType.DMA((CROPS,)),
            pltpu.SemaphoreType.DMA((4,)),
        ],
        compiler_params=params(),
    )(where, pltpu.with_memory_space_constraint(volume, pltpu.HBM), pltpu.with_memory_space_constraint(w1, pltpu.HBM))


def prepare_kernel(
    w2_ref, w3_far, wd_ref, head_ref, f2_ref, b2_ref, f3_ref, b3_ref, perm_ref, d_ref, wh_ref, rows_ref, w3_ref, sem
):
    fetch = pltpu.make_async_copy(w3_far, w3_ref, sem)
    fetch.start()
    low = lax.broadcasted_iota(jnp.int32, (64, 128), 1) < 64
    zero = jnp.zeros((64, 128), F32)
    for d in range(3):
        for j in range(3):
            at = (d * 3 + j) * T
            back = (8 - d * 3 - j) * T
            w = [w2_ref[d * 9 + h * 3 + j].astype(F32) for h in range(3)]
            pairs = {
                (0, 0): jnp.where(low, w[1], w[2]),
                (0, 1): zero,
                (1, 0): jnp.where(low, w[0], w[1]),
                (1, 1): jnp.where(low, w[2], 0.0),
                (2, 0): jnp.where(low, 0.0, w[0]),
                (2, 1): jnp.where(low, w[1], w[2]),
                (3, 0): zero,
                (3, 1): jnp.where(low, w[0], w[1]),
            }
            for (row, col), block in pairs.items():
                f2_ref[pl.ds(row * 64, 64), pl.ds(at + col * 128, 128)] = block.astype(BF16)
            b2_ref[:, pl.ds(back, T)] = f2_ref[:, pl.ds(at, T)].astype(F32).T.astype(BF16)
    rows_ref[...] = wd_ref[...].astype(F32)
    for d in range(2):
        for p in range(2):
            for h in range(4):
                block = rows_ref[pl.ds(d * 4 + h % 2 * 2 + p, 64, stride=8), :].astype(BF16)
                d_ref[2 * d + p, pl.ds(h * 64, 64), pl.ds(h // 2 * 128, 128)] = block
                d_ref[2 * d + p, pl.ds(h * 64, 64), pl.ds(128 - h // 2 * 128, 128)] = jnp.zeros_like(block)
    rows_ref[pl.ds(0, 128), :] = jnp.zeros((128, 128), F32)
    rows_ref[pl.ds(0, 4), :] = head_ref[...].astype(F32)
    wht = rows_ref[pl.ds(0, 128), :]
    wh_ref[pl.ds(0, 128), :] = wht.T.astype(BF16)
    wh_ref[pl.ds(128, 128), :] = wht.astype(BF16)
    to = lax.broadcasted_iota(jnp.int32, (1, 256), 1)
    source = to // 4 % 2 * 512 + to % 2 * 256 + (to // 128 * 16 + to // 8 % 16) * 8 + to // 2 % 2
    perm_ref[...] = jnp.where(lax.broadcasted_iota(jnp.int32, (1024, 256), 0) == source, 1.0, 0.0).astype(BF16)
    fetch.wait()
    for d in range(3):
        for j in range(3):
            at = (d * 3 + j) * T
            back = (8 - d * 3 - j) * T
            for row in range(2):
                for col in range(2):
                    block = w3_ref[d * 9 + (col - row + 1) * 3 + j]
                    f3_ref[pl.ds(row * 128, 128), pl.ds(at + col * 128, 128)] = block
                    b3_ref[pl.ds(col * 128, 128), pl.ds(back + row * 128, 128)] = block.astype(F32).T.astype(BF16)


def prepare(w2, w3, wd, wh):
    def wide(space):
        return ((T, 9 * T), BF16, space)

    return call(
        prepare_kernel,
        [wide(pltpu.VMEM), wide(pltpu.HBM), wide(pltpu.HBM), wide(pltpu.HBM)]
        + [((1024, 256), BF16, pltpu.HBM), ((4, T, T), BF16, pltpu.VMEM), ((256, 128), BF16, pltpu.HBM)],
        w2, w3, wd, wh,
        scratch=[pltpu.VMEM((512, 128), F32), pltpu.VMEM((27, 128, 128), BF16), pltpu.SemaphoreType.DMA],
        far=(1,),
    )


def second_own_kernel(a_ref, f2_ref, out_ref, b_ref):
    for n in range(CROPS):
        for d in range(2):
            put_three(b_ref, (2 * n + d) * 3 * T, three_two(a_ref[n, d]))
        own = pl.ds(n * 6 * T, 6 * T)
        out_ref[n, 0] = dot(f2_ref[:, 3 * T :], b_ref[own, :])
        out_ref[n, 1] = dot(f2_ref[:, : 6 * T], b_ref[own, :])


def second_own(a, f2):
    return call(
        second_own_kernel,
        [((CROPS, 2, T, T), F32, pltpu.VMEM)],
        a, f2,
        scratch=[pltpu.VMEM((12 * T, T), BF16)],
    )[0]


def second_kernel(
    where_ref, one_ref, own_ref, two_ref, f2_ref, wd_ref, marks_ref, h_ref, a3_ref, sent_ref, sides_ref, b_ref, m_ref
):
    for n in range(CROPS):
        for d, plane in enumerate(sorted_out(where_ref, one_ref[n], two_ref[n])):
            at = (2 * n + d) * 3 * T
            sides_ref[n, d] = plane
            put_three(b_ref, at, three_two(plane))
            rest = dot(f2_ref[:, d * 6 * T : d * 6 * T + 3 * T], b_ref[pl.ds(at, 3 * T), :])
            h = rectified(own_ref[n, d] + rest).astype(BF16)
            for p in range(2):
                h_ref[2 * d + p, :, pl.ds(n * 128, 128)] = h[:, p * 128 : (p + 1) * 128]
    total = dot_tn(wd_ref[0], h_ref[0])
    for k in range(1, 4):
        total += dot_tn(wd_ref[k], h_ref[k])
    a3 = rectified(total).astype(BF16)
    a3_ref[...] = a3
    m_ref[...] = jnp.zeros((16, T), F32)
    m_ref[pl.ds(0, 2), :] = marks_ref[...].astype(F32)
    sent_ref[pl.ds(0, T), :] = a3
    sent_ref[pl.ds(T, 16), :] = m_ref[...].astype(BF16)


def second(where, one, own, two, f2, wd, marks):
    return call(
        second_kernel,
        [
            ((4, T, T), BF16, pltpu.HBM),
            ((T, T), BF16, pltpu.VMEM),
            ((T + 16, T), BF16, pltpu.VMEM),
            ((CROPS, 2, T, T), BF16, pltpu.HBM),
        ],
        where, one, own, two, f2, wd, marks,
        scratch=[pltpu.VMEM((12 * T, T), BF16), pltpu.VMEM((16, T), F32)],
    )


def head_own_kernel(a_ref, f3_ref, wh_ref, out_ref, f3_out_ref, wh_out_ref, b_ref):
    put_three(b_ref, 0, three_three(a_ref[...]))
    for k in range(3):
        out_ref[k] = dot(f3_ref[:, (2 - k) * 3 * T : (3 - k) * 3 * T], b_ref[...])
    f3_out_ref[...] = f3_ref[...]
    wh_out_ref[...] = wh_ref[...]


def head_own(a, f3, wh):
    return call(
        head_own_kernel,
        [((3, T, T), F32, pltpu.VMEM), ((T, 9 * T), BF16, pltpu.VMEM), ((256, 128), BF16, pltpu.VMEM)],
        a, f3, wh,
        scratch=[pltpu.VMEM((3 * T, T), BF16)],
    )


def head_kernel(
    scale, where_ref, one_ref, two_ref, near_ref, away_ref, own_ref, f3_ref, wh_ref, marks_ref, gz_ref, gh_ref, b_ref
):
    lo, hi = sorted_out(where_ref, one_ref[...], two_ref[...])
    low_half = where_ref[2] == 0
    lo2 = jnp.where(low_half, away_ref[...], near_ref[...])
    hi2 = jnp.where(low_half, near_ref[...], away_ref[...])
    for k, plane in enumerate((lo2, lo[:T], hi[:T], hi2)):
        put_three(b_ref, k * 3 * T, three_three(plane))
    sums = (
        own_ref[0] + dot(f3_ref[:, : 6 * T], b_ref[: 6 * T, :]),
        own_ref[1] + dot(f3_ref[:, : 3 * T], b_ref[3 * T : 6 * T, :]) + dot(f3_ref[:, 6 * T :], b_ref[6 * T : 9 * T, :]),
        own_ref[2] + dot(f3_ref[:, 3 * T :], b_ref[6 * T :, :]),
    )
    marks = (lo[T:].astype(F32), marks_ref[...].astype(F32), hi[T:].astype(F32))
    row = lax.broadcasted_iota(jnp.int32, (128, T), 0)
    total = jnp.zeros((128, 128), F32)
    for k in range(3):
        top = rectified(sums[k]).astype(BF16)
        for h in range(2):
            mine = top[h * 128 : (h + 1) * 128]
            logits = dot(wh_ref[pl.ds(128, 128), :], mine)
            powers = jnp.where(row < 4, jnp.exp(logits), 0.0)
            share = powers / jnp.sum(powers, axis=0, keepdims=True)
            chosen = jnp.where(row.astype(F32) == marks[k][h : h + 1], 1.0, 0.0)
            g = jnp.where(row < 4, (share - chosen) * scale, 0.0)
            if k != 1:
                g = jnp.where(where_ref[3 + k // 2] == 1, g, 0.0)
            g = g.astype(BF16)
            if k == 1:
                total += dot_nt(mine, g)
            gz_ref[k, pl.ds(h * 128, 128), :] = (dot(wh_ref[pl.ds(0, 128), :], g) * slope(mine)).astype(BF16)
    gh_ref[...] = total


def head(where, one, two, near, away, own, f3, wh, marks, scale):
    return call(
        functools.partial(head_kernel, scale),
        [((3, T, T), BF16, pltpu.VMEM), ((128, 128), F32, pltpu.VMEM)],
        where, one, two, near, away, own, f3, wh, marks,
        scratch=[pltpu.VMEM((12 * T, T), BF16)],
    )


def weight_three_kernel(where_ref, g_ref, one_ref, a_ref, two_ref, out_ref, s_ref):
    put_three(s_ref, 0, three_three(g_ref[1]))
    lo, hi = sorted_out(where_ref, one_ref[:T], two_ref[:T])
    for d, a in enumerate((lo, a_ref[...], hi)):
        for j in range(3):
            t = dot_nt(s_ref[pl.ds((2 - j) * T, T), :], a)
            out_ref[d * 9 + j] = t[128:, :128]
            out_ref[d * 9 + 3 + j] = t[:128, :128] + t[128:, 128:]
            out_ref[d * 9 + 6 + j] = t[:128, 128:]


def weight_three(where, g, one, a, two):
    return call(
        weight_three_kernel,
        [((27, 128, 128), F32, pltpu.VMEM)],
        where, g, one, a, two,
        scratch=[pltpu.VMEM((3 * T, T), BF16)],
    )[0]


def middle_kernel(where_ref, g_ref, b3_ref, a3_ref, h_ref, wd_ref, gz2_ref, gone_ref, gtwo_ref, gd_ref, b_ref):
    for k in range(3):
        put_three(b_ref, k * 3 * T, three_three(g_ref[k]))
    rest = dot(b3_ref[...], b_ref[...])
    gy = (rest * slope(a3_ref[...])).astype(BF16)
    for d in range(2):
        for p in range(2):
            k = 2 * d + p
            q = (dot(wd_ref[k], gy) * slope(h_ref[k])).astype(BF16)
            for n in range(CROPS):
                gz2_ref[n, d, :, pl.ds(p * 128, 128)] = q[:, n * 128 : (n + 1) * 128]
    even = where_ref[1] == 0
    for n in range(CROPS):
        gone_ref[n] = jnp.where(even, gz2_ref[n, 1], gz2_ref[n, 0])
        gtwo_ref[n] = jnp.where(even, gz2_ref[n, 0], gz2_ref[n, 1])
    for k in range(4):
        gd_ref[k] = dot_nt(gy[:128], h_ref[k, :128]) + dot_nt(gy[128:], h_ref[k, 128:])


def middle(where, g, b3, a3, h, wd):
    return call(
        middle_kernel,
        [
            ((CROPS, 2, T, T), BF16, pltpu.VMEM),
            ((CROPS, T, T), BF16, pltpu.VMEM),
            ((CROPS, T, T), BF16, pltpu.VMEM),
            ((4, 128, 128), F32, pltpu.VMEM),
        ],
        where, g, b3, a3, h, wd,
        scratch=[pltpu.VMEM((9 * T, T), BF16)],
    )


def weight_two_kernel(g_ref, a_ref, sides_ref, out_ref, gs_ref, as_ref):
    for n in range(CROPS):
        planes = (sides_ref[n, 0], a_ref[n, 0], a_ref[n, 1], sides_ref[n, 1])
        for d in range(2):
            at = (2 * n + d) * T
            for j, (left, right) in enumerate(three_two(g_ref[n, d])):
                gs_ref[2 - j, :, pl.ds(at, 128)] = left
                gs_ref[2 - j, :, pl.ds(at + 128, 128)] = right
            for k in range(3):
                as_ref[k, :, pl.ds(at, T)] = planes[d + k]
    low = lax.broadcasted_iota(jnp.int32, (64, 128), 1) < 64
    block = (lax.broadcasted_iota(jnp.int32, (64, 128), 1) // 32) % 2 == 0
    sums = {}
    for d in range(3):
        for j in range(3):
            t = dot_nt(gs_ref[j], as_ref[d])
            q = lambda r, c: t[r * 64 : (r + 1) * 64, c * 128 : (c + 1) * 128]
            sums[d, 0, j] = jnp.where(low, q(1, 0) + q(3, 1), q(2, 0))
            sums[d, 1, j] = jnp.where(low, q(0, 0) + q(2, 1), q(1, 0) + q(3, 1))
            sums[d, 2, j] = jnp.where(low, q(1, 1), q(0, 0) + q(2, 1))
        for h in range(3):
            for j in range(3):
                s = sums[d, h, j]
                sums[d, h, j] = s + pltpu.roll(s, 64, 1)
    taps = [sums[t // 9, t // 3 % 3, t % 3] for t in range(27)] + [jnp.zeros((64, 128), F32)]
    for g in range(7):
        four = taps[4 * g : 4 * g + 4]
        turned = [pltpu.roll(x, 32, 1) for x in four]
        out_ref[g, 0] = jnp.where(low, jnp.where(block, four[0], turned[1]), jnp.where(block, four[2], turned[3]))
        out_ref[g, 1] = jnp.where(low, jnp.where(block, turned[0], four[1]), jnp.where(block, turned[2], four[3]))


def weight_two(g, a, sides):
    return call(
        weight_two_kernel,
        [((7, 2, 64, 128), F32, pltpu.VMEM)],
        g, a, sides,
        scratch=[pltpu.VMEM((3, T, 4 * T), BF16), pltpu.VMEM((3, T, 4 * T), BF16)],
    )[0]


def pack_kernel(where_ref, w3_ref, d3_ref, w2_ref, gh_ref, keep_ref, send_ref, pack_ref):
    for t in range(27):
        pack_ref[pl.ds(t, 128, stride=ROWS), :] = w3_ref[t]
    for k in range(4):
        pack_ref[pl.ds(DOWN3 + k, 128, stride=ROWS), :] = d3_ref[k]
    lane = lax.broadcasted_iota(jnp.int32, (64, 128), 1)
    for half in range(2):
        for g in range(6):
            pack_ref[pl.ds(half * ROWS + CONV2 + g, 64, stride=2 * ROWS), :] = w2_ref[g, half]
        heads = pltpu.roll(gh_ref[pl.ds(half, 64, stride=2), :], 96, 1)
        pack_ref[pl.ds(half * ROWS + CONV2 + 6, 64, stride=2 * ROWS), :] = jnp.where(lane < 96, w2_ref[6, half], heads)
    zero = jnp.zeros((128, 128), F32)
    pack_ref[pl.ds(DOWN2, 128, stride=ROWS), :] = zero
    pack_ref[pl.ds(DOWN2 + 1, 128, stride=ROWS), :] = zero
    keep_ref[...] = pack_ref[pl.ds(pl.multiple_of(where_ref[0] * 64 * ROWS, 64 * ROWS), 64 * ROWS), :]
    send_ref[...] = pack_ref[pl.ds(pl.multiple_of((1 - where_ref[0]) * 64 * ROWS, 64 * ROWS), 64 * ROWS), :].astype(BF16)


def packed(*args):
    half = (64 * ROWS, 128)
    return call(
        pack_kernel,
        [(half, F32, pltpu.VMEM), (half, BF16, pltpu.VMEM)],
        *args,
        scratch=[pltpu.VMEM((128 * ROWS, 128), F32)],
    )


def last_own_kernel(g_ref, b2_ref, out_ref, b_ref):
    for n in range(CROPS):
        for d in range(2):
            put_three(b_ref, (2 * n + d) * 3 * T, three_two(g_ref[n, d]))
        own = pl.ds(n * 6 * T, 6 * T)
        out_ref[n, 0] = dot(b2_ref[:, 3 * T :], b_ref[own, :])
        out_ref[n, 1] = dot(b2_ref[:, : 6 * T], b_ref[own, :])


def last_own(g, b2):
    return call(
        last_own_kernel,
        [((CROPS, 2, T, T), F32, pltpu.VMEM)],
        g, b2,
        scratch=[pltpu.VMEM((12 * T, T), BF16)],
    )[0]


def last_kernel(where_ref, one_ref, own_ref, two_ref, b2_ref, a_ref, vp_ref, perm_ref, down_ref, b_ref, t_ref):
    for n in range(CROPS):
        gy = []
        for d, plane in enumerate(sorted_out(where_ref, one_ref[n], two_ref[n])):
            at = (2 * n + d) * 3 * T
            put_three(b_ref, at, three_two(plane))
            rest = dot(b2_ref[:, d * 6 * T : d * 6 * T + 3 * T], b_ref[pl.ds(at, 3 * T), :])
            gy.append(((own_ref[n, d] + rest) * slope(a_ref[n, d])).astype(BF16))
        t = dot_nt(gy[0], vp_ref[n, 0]) + dot_nt(gy[1], vp_ref[n, 1])
        if n == 0:
            t_ref[...] = t
        else:
            t_ref[...] += t
    pairs = []
    lane = lax.broadcasted_iota(jnp.int32, (64, 128), 1)
    for tile in range(8):
        at = pl.ds(tile * 128, 128)
        x = jnp.zeros((64, 128), F32)
        for h in range(4):
            x = jnp.where(lane % 8 // 2 == h, t_ref[pl.ds(h * 64, 64), at], x)
        x = x + pltpu.roll(x, 126, 1)
        x = x + pltpu.roll(x, 124, 1)
        pairs.append(x.astype(BF16))
    down_ref[...] = dot(jnp.concatenate(pairs, axis=1), perm_ref[...])


def last(*args):
    return call(
        last_kernel,
        [((64, 256), F32, pltpu.VMEM)],
        *args,
        scratch=[pltpu.VMEM((12 * T, T), BF16), pltpu.VMEM((T, 1024), F32)],
    )[0]


def join_kernel(where_ref, down_ref, keep_ref, came_ref, out_ref, d_ref):
    for k, sec in enumerate((where_ref[0], 1 - where_ref[0])):
        mine = pl.ds(pl.multiple_of(sec * 32, 32), 32)
        for half in range(2):
            to = pl.ds(half * ROWS + DOWN2 + k, 32, stride=2 * ROWS)
            d_ref[to, :] = down_ref[mine, half * 128 : (half + 1) * 128]
    row = lax.broadcasted_iota(jnp.int32, (ROWS, 128), 0)
    for j in range(64):
        at = pl.ds(j * ROWS, ROWS)
        both = keep_ref[at, :] + came_ref[at, :].astype(F32)
        out_ref[at, :] = jnp.where(row >= DOWN2, d_ref[at, :], both).astype(BF16)


def joined(*args):
    return call(
        join_kernel,
        [((64 * ROWS, 128), BF16, pltpu.VMEM)],
        *args,
        scratch=[pltpu.VMEM((64 * ROWS, 128), F32)],
    )[0]


def swapped(one, two):
    count = lax.axis_size("space")
    near = [(i, i ^ 1) for i in range(count)]
    far = [(i, ((i + 1) ^ 1) - 1) for i in range(1, count - 1)]
    two = lax.ppermute(two, "space", far)
    return lax.ppermute(one, "space", near), two


def swapped_two(x):
    count = lax.axis_size("space")
    near = [(i, i ^ 2) for i in range(count)]
    away = [(i, ((i + 2) ^ 2) - 2) for i in range(2, count - 2)]
    away = lax.ppermute(x, "space", away)
    return lax.ppermute(x, "space", near), away


def partner(x):
    return lax.ppermute(x, "section", [(0, 1), (1, 0)])


def flat(x, step):
    c = lax.broadcasted_iota(jnp.int32, (128, 128), 0) * step
    lane = lax.broadcasted_iota(jnp.int32, (128, 128), 1)
    x = x.T
    pieces = []
    for k in range(16):
        piece = x[8 * k : 8 * k + 8]
        for part in (step // 2, step - step // 2):
            piece = pltpu.roll(piece, 0, 1, stride=part, stride_axis=0)
        pieces.append(pltpu.roll(piece, 8 * k * step % 128, 1) if 8 * k * step % 128 else piece)
    turned = jnp.concatenate(pieces, axis=0)
    row = lax.broadcasted_iota(jnp.int32, (32, 128), 0)
    start = lax.broadcasted_iota(jnp.int32, (32, 128), 1) * step // 128
    exact = functools.partial(jnp.dot, precision=lax.Precision.HIGHEST, preferred_element_type=F32)
    here = lane >= c % 128
    same = exact(jnp.where(row == start, 1.0, 0.0), jnp.where(here, turned, 0.0))
    return same + exact(jnp.where(row == start + 1, 1.0, 0.0), jnp.where(here, 0.0, turned))


def unpack_kernel(sums_ref, came_ref, down_ref, two_ref, three_ref, conv_ref, head_ref, x_ref):
    down_ref[...] = sums_ref[pl.ds(DOWN2, 1), :] + came_ref[...]
    last = sums_ref[pl.ds(DOWN2 - 1, 1), :]
    for k in range(4):
        head_ref[k] = jnp.sum(jnp.where(lax.broadcasted_iota(jnp.int32, (1, 128), 1) == 96 + k, last, 0.0))
    zero = jnp.zeros((128, 128), F32)
    x_ref[...] = zero
    x_ref[pl.ds(0, DOWN3), :] = sums_ref[pl.ds(0, DOWN3), :]
    conv_ref[...] = flat(x_ref[...], 27)[:27]
    x_ref[...] = zero
    lane = lax.broadcasted_iota(jnp.int32, (7, 128), 1)
    rows = sums_ref[pl.ds(CONV2, 7), :]
    for i in range(4):
        x_ref[pl.ds(i, 7, stride=4), :] = jnp.where(lane < 32, rows if i == 0 else pltpu.roll(rows, 128 - 32 * i, 1), 0.0)
    x_ref[pl.ds(27, 1), :] = jnp.zeros((1, 128), F32)
    two_ref[...] = flat(x_ref[...], 27)[:7]
    x_ref[...] = zero
    lane = lax.broadcasted_iota(jnp.int32, (1, 128), 1)
    for k in range(4):
        row = sums_ref[pl.ds(DOWN3 + k, 1), :]
        at = k // 2 * 4 + k % 2
        x_ref[pl.ds(at, 1), :] = jnp.where(lane < 64, row, 0.0)
        x_ref[pl.ds(at + 2, 1), :] = jnp.where(lane < 64, pltpu.roll(row, 64, 1), 0.0)
    three_ref[...] = flat(x_ref[...], 8)[:4]


def unpack(sums, came):
    spec = pl.BlockSpec(memory_space=pltpu.VMEM)
    down, two, three, conv, head = pl.pallas_call(
        unpack_kernel,
        in_specs=[spec] * 2,
        out_specs=[spec] * 4 + [pl.BlockSpec(memory_space=pltpu.SMEM)],
        out_shape=[pltpu.HBM((rows, 128), F32) for rows in (1, 7, 4, 27)] + [jax.ShapeDtypeStruct((4,), F32)],
        scratch_shapes=[pltpu.VMEM((128, 128), F32)],
        compiler_params=params(),
    )(sums, came)
    return down.reshape(-1), two.reshape(-1)[: 27 * 32], three.reshape(-1), conv.reshape(-1), head


def finish(pack):
    terms = lax.all_to_all(pack, "space", 0, 0, tiled=True)
    sums = jnp.sum(terms.astype(F32), axis=0)
    return unpack(sums, partner(sums[DOWN2 + 1 :]))


def per_device(volume, labels, down_weight_two, w_conv_two, down_weight_three, w_conv_three, w_head):
    count = lax.axis_size("space")
    voxels = labels.shape[0] * labels.shape[1] * count * labels.shape[2] * labels.shape[3]
    scale = 1.0 / math.sqrt(voxels)
    sec = lax.axis_index("section").astype(jnp.int32)
    space = lax.axis_index("space").astype(jnp.int32)
    where = jnp.stack([sec, space % 2, space % 4 // 2, jnp.minimum(space, 1), jnp.minimum(count - 1 - space, 1)])

    w1 = down_weight_two.transpose(1, 2, 3, 4, 0).reshape(256, 64)
    wd = down_weight_three.transpose(1, 2, 3, 4, 0).reshape(512, 128)
    w2 = w_conv_two.transpose(2, 3, 4, 0, 1).reshape(27, 64, 64)
    w2 = jnp.concatenate([w2, w2], axis=2)
    w3 = w_conv_three.transpose(2, 3, 4, 0, 1).reshape(27, 128, 128)
    marks = lax.dynamic_slice_in_dim(labels[:, 0], CROPS * sec, CROPS, axis=0)
    marks = marks.transpose(1, 0, 2).reshape(2, 256)

    vp, a2, one, two = first(where, volume, w1)
    a2_one, a2_two = swapped(one, two)
    f2, b2, f3, b3, perm, wd, wh = prepare(w2, w3, wd, w_head.T)
    own = second_own(a2, f2)
    a2_two, a2_one, own = lax.optimization_barrier((a2_two, a2_one, own))
    h2, a3, sent, sides = second(where, a2_one, own, a2_two, f2, wd, marks)
    a3_one, a3_two = swapped(sent, sent)
    a3_near, a3_away = swapped_two(a3)
    own, f3, wh = head_own(a3, f3, wh)
    a3_one, a3_two, a3_near, a3_away, own, f3, wh = lax.optimization_barrier(
        (a3_one, a3_two, a3_near, a3_away, own, f3, wh)
    )
    gz4, gh = head(where, a3_one, a3_two, a3_near, a3_away, own, f3, wh, marks, scale)
    gz2, one, two, gd3 = middle(where, gz4, b3, a3, h2, wd)
    gw3 = weight_three(where, gz4, a3_one, a3, a3_two)
    gz2_one, gz2_two = swapped(one, two)
    own = last_own(gz2, b2)
    gw2 = weight_two(gz2, a2, sides)
    keep, send = packed(where, gw3, gd3, gw2, gh)
    gz2_two, gz2_one, send, own = lax.optimization_barrier((gz2_two, gz2_one, send, own))
    came = partner(send)
    down = last(where, gz2_one, own, gz2_two, b2, a2, vp, perm)
    pack = joined(where, down, keep, came)
    return finish(pack.reshape(64, ROWS, 128))


def solution(mesh):
    whole = P(("section", "space"))
    return jax.shard_map(
        per_device,
        mesh=mesh,
        in_specs=(P(None, None, "space", None, None), P(None, "space", None, None), P(), P(), P(), P(), P()),
        out_specs=(whole,) * 5,
        check_vma=False,
    )
```

```python
import functools
import math

import jax
import jax.numpy as jnp
from jax import lax
from jax.experimental import pallas as pl
from jax.experimental.pallas import tpu as pltpu
from jax.sharding import PartitionSpec as P


F32 = jnp.float32
BF16 = jnp.bfloat16
SHIFT = math.log(2.0)
CROPS = 2
T = 256
ROWS = 40
DOWN3, CONV2, DOWN2 = 27, 31, 38


def params(megabytes=12):
    return pltpu.CompilerParams(vmem_limit_bytes=megabytes << 20)


def rectified(v):
    return jnp.maximum(v, 0.0) + jnp.log1p(jnp.exp(-jnp.abs(v))) - SHIFT


def slope(stored):
    return 1.0 - 0.5 * jnp.exp(-stored.astype(F32))


def dot(a, b):
    return jnp.dot(a, b, preferred_element_type=F32)


def dot_tn(a, b):
    return lax.dot_general(a, b, (((0,), (0,)), ((), ())), preferred_element_type=F32)


def dot_nt(a, b):
    return lax.dot_general(a, b, (((1,), (1,)), ((), ())), preferred_element_type=F32)


def moved(x, by):
    x = x.astype(F32)
    lane = lax.broadcasted_iota(jnp.int32, x.shape, 1)
    edge = 0 if by == 1 else 127
    return jnp.where(lane == edge, 0.0, pltpu.roll(x, by % 128, 1)).astype(BF16)


def three_two(x):
    even, odd = x[:, :128], x[:, 128:]
    return ((moved(odd, 1), even), (even, odd), (odd, moved(even, -1)))


def three_three(x):
    first, second = x[:, :128], x[:, 128:]
    return ((moved(first, 1), moved(second, 1)), (first, second), (moved(first, -1), moved(second, -1)))


def put_three(ref, row, shifted):
    for j, (left, right) in enumerate(shifted):
        ref[pl.ds(row + j * T, T), 0:128] = left
        ref[pl.ds(row + j * T, T), 128:256] = right


def call(kernel, outs, *args, scratch=(), far=()):
    spec = pl.BlockSpec(memory_space=pltpu.VMEM)
    scalar = pl.BlockSpec(memory_space=pltpu.SMEM)
    remote = pl.BlockSpec(memory_space=pl.ANY)
    return pl.pallas_call(
        kernel,
        in_specs=[remote if i in far else scalar if a.dtype == jnp.int32 and a.ndim == 1 else spec for i, a in enumerate(args)],
        out_specs=[spec] * len(outs),
        out_shape=[space(s, d) for s, d, space in outs],
        scratch_shapes=list(scratch),
        compiler_params=params(),
    )(*[pltpu.with_memory_space_constraint(a, pltpu.HBM) if i in far else a for i, a in enumerate(args)])


def sorted_out(where_ref, one, two):
    even = where_ref[1] == 0
    return jnp.where(even, two, one), jnp.where(even, one, two)


def first_kernel(
    where_ref, vol_far, w_ref, vp_far, a_ref, one_ref, two_ref, sort_ref, wt_ref, vol_ref, vp_ref, in_sems, out_sems
):
    steps = [(n, d) for n in range(CROPS) for d in range(2)]
    fetches = [
        pltpu.make_async_copy(vol_far.at[CROPS * where_ref[0] + n], vol_ref.at[n], in_sems.at[n]) for n in range(CROPS)
    ]
    stores = [
        pltpu.make_async_copy(vp_ref.at[i], vp_far.at[n, d], out_sems.at[i]) for i, (n, d) in enumerate(steps)
    ]
    for fetch in fetches:
        fetch.start()
    to = lax.broadcasted_iota(jnp.int32, (1, 512), 1)
    source = (to % 128) * 4 + (to // 128) % 2 * 2 + to // 256
    sort_ref[...] = jnp.where(lax.broadcasted_iota(jnp.int32, (512, 512), 0) == source, 1.0, 0.0).astype(BF16)
    to = lax.broadcasted_iota(jnp.int32, (1, 1024), 1)
    height = to % 8
    source = to // 8 % 32 * 8 + to // 512 * 4 + height % 2 * 2 + to // 256 % 2
    pick = jnp.where(lax.broadcasted_iota(jnp.int32, (256, 1024), 0) == source, 1.0, 0.0).astype(BF16)
    w = dot_tn(w_ref[...], pick)
    for h in range(4):
        wt_ref[pl.ds(h * 64, 64), :] = jnp.where(height // 2 == h, w, 0.0).astype(BF16)
    for i, (n, d) in enumerate(steps):
        if d == 0:
            fetches[n].wait()
        for k in range(2):
            v = vol_ref[n, :, 2 * d + k].astype(F32).reshape(256, 512).astype(BF16)
            s = dot(v, sort_ref[...]).astype(BF16)
            vp_ref[i, pl.ds(k * 512, 256), :] = s[:, :256]
            vp_ref[i, pl.ds(k * 512 + 256, 256), :] = s[:, 256:]
        stores[i].start()
        a_ref[n, d] = rectified(dot(wt_ref[...], vp_ref[i])).astype(BF16)
    even = where_ref[1] == 0
    for n in range(CROPS):
        one_ref[n] = jnp.where(even, a_ref[n, 1], a_ref[n, 0])
        two_ref[n] = jnp.where(even, a_ref[n, 0], a_ref[n, 1])
    for store in stores:
        store.wait()


def first(where, volume, w1):
    spec = pl.BlockSpec(memory_space=pltpu.VMEM)
    far = pl.BlockSpec(memory_space=pl.ANY)
    return pl.pallas_call(
        first_kernel,
        in_specs=[pl.BlockSpec(memory_space=pltpu.SMEM), far, spec],
        out_specs=[far, spec, spec, spec],
        out_shape=[
            pltpu.HBM((CROPS, 2, 1024, 256), BF16),
            pltpu.VMEM((CROPS, 2, 256, 256), BF16),
            pltpu.VMEM((CROPS, 256, 256), BF16),
            pltpu.VMEM((CROPS, 256, 256), BF16),
        ],
        scratch_shapes=[
            pltpu.VMEM((512, 512), BF16),
            pltpu.VMEM((256, 1024), BF16),
            pltpu.VMEM((CROPS, 32, 4, 8, 512), BF16),
            pltpu.VMEM((4, 1024, 256), BF16),
            pltpu.SemaphoreType.DMA((CROPS,)),
            pltpu.SemaphoreType.DMA((4,)),
        ],
        compiler_params=params(),
    )(where, pltpu.with_memory_space_constraint(volume, pltpu.HBM), pltpu.with_memory_space_constraint(w1, pltpu.HBM))


def prepare_kernel(
    w2_ref, w3_far, wd_ref, head_ref, f2_ref, b2_ref, f3_ref, b3_ref, perm_ref, d_ref, wh_ref, rows_ref, w3_ref, sem
):
    fetch = pltpu.make_async_copy(w3_far, w3_ref, sem)
    fetch.start()
    low = lax.broadcasted_iota(jnp.int32, (64, 128), 1) < 64
    zero = jnp.zeros((64, 128), F32)
    for d in range(3):
        for j in range(3):
            at = (d * 3 + j) * T
            back = (8 - d * 3 - j) * T
            w = [w2_ref[d * 9 + h * 3 + j].astype(F32) for h in range(3)]
            pairs = {
                (0, 0): jnp.where(low, w[1], w[2]),
                (0, 1): zero,
                (1, 0): jnp.where(low, w[0], w[1]),
                (1, 1): jnp.where(low, w[2], 0.0),
                (2, 0): jnp.where(low, 0.0, w[0]),
                (2, 1): jnp.where(low, w[1], w[2]),
                (3, 0): zero,
                (3, 1): jnp.where(low, w[0], w[1]),
            }
            for (row, col), block in pairs.items():
                f2_ref[pl.ds(row * 64, 64), pl.ds(at + col * 128, 128)] = block.astype(BF16)
            b2_ref[:, pl.ds(back, T)] = f2_ref[:, pl.ds(at, T)].astype(F32).T.astype(BF16)
    rows_ref[...] = wd_ref[...].astype(F32)
    for d in range(2):
        for p in range(2):
            for h in range(4):
                block = rows_ref[pl.ds(d * 4 + h % 2 * 2 + p, 64, stride=8), :].astype(BF16)
                d_ref[2 * d + p, pl.ds(h * 64, 64), pl.ds(h // 2 * 128, 128)] = block
                d_ref[2 * d + p, pl.ds(h * 64, 64), pl.ds(128 - h // 2 * 128, 128)] = jnp.zeros_like(block)
    rows_ref[pl.ds(0, 128), :] = jnp.zeros((128, 128), F32)
    rows_ref[pl.ds(0, 4), :] = head_ref[...].astype(F32)
    wht = rows_ref[pl.ds(0, 128), :]
    wh_ref[pl.ds(0, 128), :] = wht.T.astype(BF16)
    wh_ref[pl.ds(128, 128), :] = wht.astype(BF16)
    to = lax.broadcasted_iota(jnp.int32, (1, 256), 1)
    source = to // 4 % 2 * 512 + to % 2 * 256 + (to // 128 * 16 + to // 8 % 16) * 8 + to // 2 % 2
    perm_ref[...] = jnp.where(lax.broadcasted_iota(jnp.int32, (1024, 256), 0) == source, 1.0, 0.0).astype(BF16)
    fetch.wait()
    for d in range(3):
        for j in range(3):
            at = (d * 3 + j) * T
            back = (8 - d * 3 - j) * T
            for row in range(2):
                for col in range(2):
                    block = w3_ref[d * 9 + (col - row + 1) * 3 + j]
                    f3_ref[pl.ds(row * 128, 128), pl.ds(at + col * 128, 128)] = block
                    b3_ref[pl.ds(col * 128, 128), pl.ds(back + row * 128, 128)] = block.astype(F32).T.astype(BF16)


def prepare(w2, w3, wd, wh):
    def wide(space):
        return ((T, 9 * T), BF16, space)

    return call(
        prepare_kernel,
        [wide(pltpu.VMEM), wide(pltpu.HBM), wide(pltpu.HBM), wide(pltpu.HBM)]
        + [((1024, 256), BF16, pltpu.HBM), ((4, T, T), BF16, pltpu.VMEM), ((256, 128), BF16, pltpu.HBM)],
        w2, w3, wd, wh,
        scratch=[pltpu.VMEM((512, 128), F32), pltpu.VMEM((27, 128, 128), BF16), pltpu.SemaphoreType.DMA],
        far=(1,),
    )


def second_own_kernel(a_ref, f2_ref, out_ref, b_ref):
    for n in range(CROPS):
        for d in range(2):
            put_three(b_ref, (2 * n + d) * 3 * T, three_two(a_ref[n, d]))
        own = pl.ds(n * 6 * T, 6 * T)
        out_ref[n, 0] = dot(f2_ref[:, 3 * T :], b_ref[own, :])
        out_ref[n, 1] = dot(f2_ref[:, : 6 * T], b_ref[own, :])


def second_own(a, f2):
    return call(
        second_own_kernel,
        [((CROPS, 2, T, T), F32, pltpu.VMEM)],
        a, f2,
        scratch=[pltpu.VMEM((12 * T, T), BF16)],
    )[0]


def second_kernel(
    where_ref, one_ref, own_ref, two_ref, f2_ref, wd_ref, marks_ref, h_ref, a3_ref, sent_ref, sides_ref, b_ref, m_ref
):
    for n in range(CROPS):
        for d, plane in enumerate(sorted_out(where_ref, one_ref[n], two_ref[n])):
            at = (2 * n + d) * 3 * T
            sides_ref[n, d] = plane
            put_three(b_ref, at, three_two(plane))
            rest = dot(f2_ref[:, d * 6 * T : d * 6 * T + 3 * T], b_ref[pl.ds(at, 3 * T), :])
            h = rectified(own_ref[n, d] + rest).astype(BF16)
            for p in range(2):
                h_ref[2 * d + p, :, pl.ds(n * 128, 128)] = h[:, p * 128 : (p + 1) * 128]
    total = dot_tn(wd_ref[0], h_ref[0])
    for k in range(1, 4):
        total += dot_tn(wd_ref[k], h_ref[k])
    a3 = rectified(total).astype(BF16)
    a3_ref[...] = a3
    m_ref[...] = jnp.zeros((16, T), F32)
    m_ref[pl.ds(0, 2), :] = marks_ref[...].astype(F32)
    sent_ref[pl.ds(0, T), :] = a3
    sent_ref[pl.ds(T, 16), :] = m_ref[...].astype(BF16)


def second(where, one, own, two, f2, wd, marks):
    return call(
        second_kernel,
        [
            ((4, T, T), BF16, pltpu.HBM),
            ((T, T), BF16, pltpu.VMEM),
            ((T + 16, T), BF16, pltpu.VMEM),
            ((CROPS, 2, T, T), BF16, pltpu.HBM),
        ],
        where, one, own, two, f2, wd, marks,
        scratch=[pltpu.VMEM((12 * T, T), BF16), pltpu.VMEM((16, T), F32)],
    )


def head_own_kernel(a_ref, f3_ref, wh_ref, out_ref, f3_out_ref, wh_out_ref, b_ref):
    put_three(b_ref, 0, three_three(a_ref[...]))
    for k in range(3):
        out_ref[k] = dot(f3_ref[:, (2 - k) * 3 * T : (3 - k) * 3 * T], b_ref[...])
    f3_out_ref[...] = f3_ref[...]
    wh_out_ref[...] = wh_ref[...]


def head_own(a, f3, wh):
    return call(
        head_own_kernel,
        [((3, T, T), F32, pltpu.VMEM), ((T, 9 * T), BF16, pltpu.VMEM), ((256, 128), BF16, pltpu.VMEM)],
        a, f3, wh,
        scratch=[pltpu.VMEM((3 * T, T), BF16)],
    )


def head_kernel(
    scale, where_ref, one_ref, two_ref, near_ref, away_ref, own_ref, f3_ref, wh_ref, marks_ref, b3_ref, a3_ref, h_ref,
    wd_ref, gz_ref, gh_ref, gz2_ref, gone_ref, gtwo_ref, gy_ref, b_ref
):
    lo, hi = sorted_out(where_ref, one_ref[...], two_ref[...])
    low_half = where_ref[2] == 0
    lo2 = jnp.where(low_half, away_ref[...], near_ref[...])
    hi2 = jnp.where(low_half, near_ref[...], away_ref[...])
    for k, plane in enumerate((lo2, lo[:T], hi[:T], hi2)):
        put_three(b_ref, k * 3 * T, three_three(plane))
    sums = (
        own_ref[0] + dot(f3_ref[:, : 6 * T], b_ref[: 6 * T, :]),
        own_ref[1] + dot(f3_ref[:, : 3 * T], b_ref[3 * T : 6 * T, :]) + dot(f3_ref[:, 6 * T :], b_ref[6 * T : 9 * T, :]),
        own_ref[2] + dot(f3_ref[:, 3 * T :], b_ref[6 * T :, :]),
    )
    marks = (lo[T:].astype(F32), marks_ref[...].astype(F32), hi[T:].astype(F32))
    row = lax.broadcasted_iota(jnp.int32, (128, T), 0)
    total = jnp.zeros((128, 128), F32)
    for k in range(3):
        top = rectified(sums[k]).astype(BF16)
        for h in range(2):
            mine = top[h * 128 : (h + 1) * 128]
            logits = dot(wh_ref[pl.ds(128, 128), :], mine)
            powers = jnp.where(row < 4, jnp.exp(logits), 0.0)
            share = powers / jnp.sum(powers, axis=0, keepdims=True)
            chosen = jnp.where(row.astype(F32) == marks[k][h : h + 1], 1.0, 0.0)
            g = jnp.where(row < 4, (share - chosen) * scale, 0.0)
            if k != 1:
                g = jnp.where(where_ref[3 + k // 2] == 1, g, 0.0)
            g = g.astype(BF16)
            if k == 1:
                total += dot_nt(mine, g)
            gz_ref[k, pl.ds(h * 128, 128), :] = (dot(wh_ref[pl.ds(0, 128), :], g) * slope(mine)).astype(BF16)
    gh_ref[...] = total
    for k in range(3):
        put_three(b_ref, k * 3 * T, three_three(gz_ref[k]))
    gy = (dot(b3_ref[...], b_ref[: 9 * T, :]) * slope(a3_ref[...])).astype(BF16)
    gy_ref[...] = gy
    for d in range(2):
        for p in range(2):
            k = 2 * d + p
            q = (dot(wd_ref[k], gy) * slope(h_ref[k])).astype(BF16)
            for n in range(CROPS):
                gz2_ref[n, d, :, pl.ds(p * 128, 128)] = q[:, n * 128 : (n + 1) * 128]
    even = where_ref[1] == 0
    for n in range(CROPS):
        gone_ref[n] = jnp.where(even, gz2_ref[n, 1], gz2_ref[n, 0])
        gtwo_ref[n] = jnp.where(even, gz2_ref[n, 0], gz2_ref[n, 1])


def head(where, one, two, near, away, own, f3, wh, marks, b3, a3, h, wd, scale):
    return call(
        functools.partial(head_kernel, scale),
        [
            ((3, T, T), BF16, pltpu.VMEM),
            ((128, 128), F32, pltpu.VMEM),
            ((CROPS, 2, T, T), BF16, pltpu.VMEM),
            ((CROPS, T, T), BF16, pltpu.VMEM),
            ((CROPS, T, T), BF16, pltpu.VMEM),
            ((T, T), BF16, pltpu.VMEM),
        ],
        where, one, two, near, away, own, f3, wh, marks, b3, a3, h, wd,
        scratch=[pltpu.VMEM((12 * T, T), BF16)],
    )


def weight_three_kernel(where_ref, g_ref, one_ref, a_ref, two_ref, gy_ref, h_ref, out_ref, gd_ref, s_ref):
    gy = gy_ref[...]
    for k in range(4):
        gd_ref[k] = dot_nt(gy[:128], h_ref[k, :128]) + dot_nt(gy[128:], h_ref[k, 128:])
    put_three(s_ref, 0, three_three(g_ref[1]))
    lo, hi = sorted_out(where_ref, one_ref[:T], two_ref[:T])
    for d, a in enumerate((lo, a_ref[...], hi)):
        for j in range(3):
            t = dot_nt(s_ref[pl.ds((2 - j) * T, T), :], a)
            out_ref[d * 9 + j] = t[128:, :128]
            out_ref[d * 9 + 3 + j] = t[:128, :128] + t[128:, 128:]
            out_ref[d * 9 + 6 + j] = t[:128, 128:]


def weight_three(where, g, one, a, two, gy, h):
    return call(
        weight_three_kernel,
        [((27, 128, 128), F32, pltpu.VMEM), ((4, 128, 128), F32, pltpu.VMEM)],
        where, g, one, a, two, gy, h,
        scratch=[pltpu.VMEM((3 * T, T), BF16)],
    )


def weight_two_kernel(g_ref, a_ref, sides_ref, out_ref, gs_ref, as_ref):
    for n in range(CROPS):
        planes = (sides_ref[n, 0], a_ref[n, 0], a_ref[n, 1], sides_ref[n, 1])
        for d in range(2):
            at = (2 * n + d) * T
            for j, (left, right) in enumerate(three_two(g_ref[n, d])):
                gs_ref[2 - j, :, pl.ds(at, 128)] = left
                gs_ref[2 - j, :, pl.ds(at + 128, 128)] = right
            for k in range(3):
                as_ref[k, :, pl.ds(at, T)] = planes[d + k]
    low = lax.broadcasted_iota(jnp.int32, (64, 128), 1) < 64
    block = (lax.broadcasted_iota(jnp.int32, (64, 128), 1) // 32) % 2 == 0
    sums = {}
    for d in range(3):
        for j in range(3):
            t = dot_nt(gs_ref[j], as_ref[d])
            q = lambda r, c: t[r * 64 : (r + 1) * 64, c * 128 : (c + 1) * 128]
            sums[d, 0, j] = jnp.where(low, q(1, 0) + q(3, 1), q(2, 0))
            sums[d, 1, j] = jnp.where(low, q(0, 0) + q(2, 1), q(1, 0) + q(3, 1))
            sums[d, 2, j] = jnp.where(low, q(1, 1), q(0, 0) + q(2, 1))
        for h in range(3):
            for j in range(3):
                s = sums[d, h, j]
                sums[d, h, j] = s + pltpu.roll(s, 64, 1)
    taps = [sums[t // 9, t // 3 % 3, t % 3] for t in range(27)] + [jnp.zeros((64, 128), F32)]
    for g in range(7):
        four = taps[4 * g : 4 * g + 4]
        turned = [pltpu.roll(x, 32, 1) for x in four]
        out_ref[g, 0] = jnp.where(low, jnp.where(block, four[0], turned[1]), jnp.where(block, four[2], turned[3]))
        out_ref[g, 1] = jnp.where(low, jnp.where(block, turned[0], four[1]), jnp.where(block, turned[2], four[3]))


def weight_two(g, a, sides):
    return call(
        weight_two_kernel,
        [((7, 2, 64, 128), F32, pltpu.VMEM)],
        g, a, sides,
        scratch=[pltpu.VMEM((3, T, 4 * T), BF16), pltpu.VMEM((3, T, 4 * T), BF16)],
    )[0]


def pack_kernel(where_ref, w3_ref, d3_ref, w2_ref, gh_ref, keep_ref, send_ref, pack_ref):
    for t in range(27):
        pack_ref[pl.ds(t, 128, stride=ROWS), :] = w3_ref[t]
    for k in range(4):
        pack_ref[pl.ds(DOWN3 + k, 128, stride=ROWS), :] = d3_ref[k]
    lane = lax.broadcasted_iota(jnp.int32, (64, 128), 1)
    for half in range(2):
        for g in range(6):
            pack_ref[pl.ds(half * ROWS + CONV2 + g, 64, stride=2 * ROWS), :] = w2_ref[g, half]
        heads = pltpu.roll(gh_ref[pl.ds(half, 64, stride=2), :], 96, 1)
        pack_ref[pl.ds(half * ROWS + CONV2 + 6, 64, stride=2 * ROWS), :] = jnp.where(lane < 96, w2_ref[6, half], heads)
    zero = jnp.zeros((128, 128), F32)
    pack_ref[pl.ds(DOWN2, 128, stride=ROWS), :] = zero
    pack_ref[pl.ds(DOWN2 + 1, 128, stride=ROWS), :] = zero
    keep_ref[...] = pack_ref[pl.ds(pl.multiple_of(where_ref[0] * 64 * ROWS, 64 * ROWS), 64 * ROWS), :]
    send_ref[...] = pack_ref[pl.ds(pl.multiple_of((1 - where_ref[0]) * 64 * ROWS, 64 * ROWS), 64 * ROWS), :].astype(BF16)


def packed(*args):
    half = (64 * ROWS, 128)
    return call(
        pack_kernel,
        [(half, F32, pltpu.VMEM), (half, BF16, pltpu.VMEM)],
        *args,
        scratch=[pltpu.VMEM((128 * ROWS, 128), F32)],
    )


def last_own_kernel(g_ref, b2_ref, out_ref, b_ref):
    for n in range(CROPS):
        for d in range(2):
            put_three(b_ref, (2 * n + d) * 3 * T, three_two(g_ref[n, d]))
        own = pl.ds(n * 6 * T, 6 * T)
        out_ref[n, 0] = dot(b2_ref[:, 3 * T :], b_ref[own, :])
        out_ref[n, 1] = dot(b2_ref[:, : 6 * T], b_ref[own, :])


def last_own(g, b2):
    return call(
        last_own_kernel,
        [((CROPS, 2, T, T), F32, pltpu.VMEM)],
        g, b2,
        scratch=[pltpu.VMEM((12 * T, T), BF16)],
    )[0]


def last_kernel(where_ref, one_ref, own_ref, two_ref, b2_ref, a_ref, vp_ref, perm_ref, down_ref, b_ref, t_ref):
    for n in range(CROPS):
        gy = []
        for d, plane in enumerate(sorted_out(where_ref, one_ref[n], two_ref[n])):
            at = (2 * n + d) * 3 * T
            put_three(b_ref, at, three_two(plane))
            rest = dot(b2_ref[:, d * 6 * T : d * 6 * T + 3 * T], b_ref[pl.ds(at, 3 * T), :])
            gy.append(((own_ref[n, d] + rest) * slope(a_ref[n, d])).astype(BF16))
        t = dot_nt(gy[0], vp_ref[n, 0]) + dot_nt(gy[1], vp_ref[n, 1])
        if n == 0:
            t_ref[...] = t
        else:
            t_ref[...] += t
    pairs = []
    lane = lax.broadcasted_iota(jnp.int32, (64, 128), 1)
    for tile in range(8):
        at = pl.ds(tile * 128, 128)
        x = jnp.zeros((64, 128), F32)
        for h in range(4):
            x = jnp.where(lane % 8 // 2 == h, t_ref[pl.ds(h * 64, 64), at], x)
        x = x + pltpu.roll(x, 126, 1)
        x = x + pltpu.roll(x, 124, 1)
        pairs.append(x.astype(BF16))
    down_ref[...] = dot(jnp.concatenate(pairs, axis=1), perm_ref[...])


def last(*args):
    return call(
        last_kernel,
        [((64, 256), F32, pltpu.VMEM)],
        *args,
        scratch=[pltpu.VMEM((12 * T, T), BF16), pltpu.VMEM((T, 1024), F32)],
    )[0]


def join_kernel(where_ref, down_ref, keep_ref, came_ref, out_ref, d_ref):
    for k, sec in enumerate((where_ref[0], 1 - where_ref[0])):
        mine = pl.ds(pl.multiple_of(sec * 32, 32), 32)
        for half in range(2):
            to = pl.ds(half * ROWS + DOWN2 + k, 32, stride=2 * ROWS)
            d_ref[to, :] = down_ref[mine, half * 128 : (half + 1) * 128]
    row = lax.broadcasted_iota(jnp.int32, (ROWS, 128), 0)
    for j in range(64):
        at = pl.ds(j * ROWS, ROWS)
        both = keep_ref[at, :] + came_ref[at, :].astype(F32)
        out_ref[at, :] = jnp.where(row >= DOWN2, d_ref[at, :], both).astype(BF16)


def joined(*args):
    return call(
        join_kernel,
        [((64 * ROWS, 128), BF16, pltpu.VMEM)],
        *args,
        scratch=[pltpu.VMEM((64 * ROWS, 128), F32)],
    )[0]


def swapped(one, two):
    count = lax.axis_size("space")
    near = [(i, i ^ 1) for i in range(count)]
    far = [(i, ((i + 1) ^ 1) - 1) for i in range(1, count - 1)]
    two = lax.ppermute(two, "space", far)
    return lax.ppermute(one, "space", near), two


def swapped_two(x):
    count = lax.axis_size("space")
    near = [(i, i ^ 2) for i in range(count)]
    away = [(i, ((i + 2) ^ 2) - 2) for i in range(2, count - 2)]
    away = lax.ppermute(x, "space", away)
    return lax.ppermute(x, "space", near), away


def partner(x):
    return lax.ppermute(x, "section", [(0, 1), (1, 0)])


def flat(x, step, rows):
    c = lax.broadcasted_iota(jnp.int32, (128, 128), 0) * step
    lane = lax.broadcasted_iota(jnp.int32, (128, 128), 1)
    x = x.T
    pieces = []
    for k in range(16):
        piece = x[8 * k : 8 * k + 8]
        for part in (step // 2, step - step // 2):
            piece = pltpu.roll(piece, 0, 1, stride=part, stride_axis=0)
        pieces.append(pltpu.roll(piece, 8 * k * step % 128, 1) if 8 * k * step % 128 else piece)
    turned = jnp.concatenate(pieces, axis=0)
    row = lax.broadcasted_iota(jnp.int32, (rows, 128), 0)
    start = lax.broadcasted_iota(jnp.int32, (rows, 128), 1) * step // 128
    exact = functools.partial(jnp.dot, precision=lax.Precision.HIGHEST, preferred_element_type=F32)
    here = lane >= c % 128
    same = exact(jnp.where(row == start, 1.0, 0.0), jnp.where(here, turned, 0.0))
    return same + exact(jnp.where(row == start + 1, 1.0, 0.0), jnp.where(here, 0.0, turned))


def unpack_kernel(sums_ref, two_ref, three_ref, conv_ref, head_ref, x_ref, y_ref, z_ref):
    last = sums_ref[pl.ds(DOWN2 - 1, 1), :]
    for k in range(4):
        head_ref[k] = jnp.sum(jnp.where(lax.broadcasted_iota(jnp.int32, (1, 128), 1) == 96 + k, last, 0.0))
    for ref in (x_ref, y_ref, z_ref):
        ref[...] = jnp.zeros((128, 128), F32)
    x_ref[pl.ds(0, DOWN3), :] = sums_ref[pl.ds(0, DOWN3), :]
    lane = lax.broadcasted_iota(jnp.int32, (7, 128), 1)
    rows = sums_ref[pl.ds(CONV2, 7), :]
    for i in range(4):
        y_ref[pl.ds(i, 7, stride=4), :] = jnp.where(lane < 32, rows if i == 0 else pltpu.roll(rows, 128 - 32 * i, 1), 0.0)
    y_ref[pl.ds(27, 1), :] = jnp.zeros((1, 128), F32)
    lane = lax.broadcasted_iota(jnp.int32, (1, 128), 1)
    for k in range(4):
        row = sums_ref[pl.ds(DOWN3 + k, 1), :]
        at = k // 2 * 4 + k % 2
        z_ref[pl.ds(at, 1), :] = jnp.where(lane < 64, row, 0.0)
        z_ref[pl.ds(at + 2, 1), :] = jnp.where(lane < 64, pltpu.roll(row, 64, 1), 0.0)
    conv_ref[...] = flat(x_ref[...], 27, 32)[:27]
    two_ref[...] = flat(y_ref[...], 27, 8)[:7]
    three_ref[...] = flat(z_ref[...], 8, 8)[:4]


def unpack(sums, came):
    spec = pl.BlockSpec(memory_space=pltpu.VMEM)
    two, three, conv, head = pl.pallas_call(
        unpack_kernel,
        in_specs=[spec],
        out_specs=[spec] * 3 + [pl.BlockSpec(memory_space=pltpu.SMEM)],
        out_shape=[pltpu.HBM((rows, 128), F32) for rows in (7, 4, 27)] + [jax.ShapeDtypeStruct((4,), F32)],
        scratch_shapes=[pltpu.VMEM((128, 128), F32)] * 3,
        compiler_params=params(),
    )(sums)
    return sums[DOWN2] + came[0], two.reshape(-1)[: 27 * 32], three.reshape(-1), conv.reshape(-1), head


def finish(pack):
    terms = lax.all_to_all(pack, "space", 0, 0, tiled=True)
    sums = jnp.sum(terms.astype(F32), axis=0)
    return unpack(sums, partner(sums[DOWN2 + 1 :]))


def per_device(volume, labels, down_weight_two, w_conv_two, down_weight_three, w_conv_three, w_head):
    count = lax.axis_size("space")
    voxels = labels.shape[0] * labels.shape[1] * count * labels.shape[2] * labels.shape[3]
    scale = 1.0 / math.sqrt(voxels)
    sec = lax.axis_index("section").astype(jnp.int32)
    space = lax.axis_index("space").astype(jnp.int32)
    where = jnp.stack([sec, space % 2, space % 4 // 2, jnp.minimum(space, 1), jnp.minimum(count - 1 - space, 1)])

    w1 = down_weight_two.transpose(1, 2, 3, 4, 0).reshape(256, 64)
    wd = down_weight_three.transpose(1, 2, 3, 4, 0).reshape(512, 128)
    w2 = w_conv_two.transpose(2, 3, 4, 0, 1).reshape(27, 64, 64)
    w2 = jnp.concatenate([w2, w2], axis=2)
    w3 = w_conv_three.transpose(2, 3, 4, 0, 1).reshape(27, 128, 128)
    marks = lax.dynamic_slice_in_dim(labels[:, 0], CROPS * sec, CROPS, axis=0)
    marks = marks.transpose(1, 0, 2).reshape(2, 256)

    vp, a2, one, two = first(where, volume, w1)
    a2_one, a2_two = swapped(one, two)
    f2, b2, f3, b3, perm, wd, wh = prepare(w2, w3, wd, w_head.T)
    own = second_own(a2, f2)
    a2_two, a2_one, own = lax.optimization_barrier((a2_two, a2_one, own))
    h2, a3, sent, sides = second(where, a2_one, own, a2_two, f2, wd, marks)
    a3_one, a3_two = swapped(sent, sent)
    a3_near, a3_away = swapped_two(a3)
    own, f3, wh = head_own(a3, f3, wh)
    a3_two, a3_away, a3_one, a3_near, own, f3, wh = lax.optimization_barrier(
        (a3_two, a3_away, a3_one, a3_near, own, f3, wh)
    )
    gz4, gh, gz2, one, two, gy3 = head(
        where, a3_one, a3_two, a3_near, a3_away, own, f3, wh, marks, b3, a3, h2, wd, scale
    )
    gw3, gd3 = weight_three(where, gz4, a3_one, a3, a3_two, gy3, h2)
    gz2_one, gz2_two = swapped(one, two)
    own = last_own(gz2, b2)
    gw2 = weight_two(gz2, a2, sides)
    keep, send = packed(where, gw3, gd3, gw2, gh)
    gz2_two, gz2_one, send, own = lax.optimization_barrier((gz2_two, gz2_one, send, own))
    came = partner(send)
    down = last(where, gz2_one, own, gz2_two, b2, a2, vp, perm)
    pack = joined(where, down, keep, came)
    return finish(pack.reshape(64, ROWS, 128))


def solution(mesh):
    whole = P(("section", "space"))
    return jax.shard_map(
        per_device,
        mesh=mesh,
        in_specs=(P(None, None, "space", None, None), P(None, "space", None, None), P(), P(), P(), P(), P()),
        out_specs=(whole,) * 5,
        check_vma=False,
    )
```

```python
import functools
import math

import jax
import jax.numpy as jnp
from jax import lax
from jax.experimental import pallas as pl
from jax.experimental.pallas import tpu as pltpu
from jax.sharding import PartitionSpec as P


F32 = jnp.float32
BF16 = jnp.bfloat16
SHIFT = math.log(2.0)
CROPS = 2
T = 256
ROWS = 40
DOWN3, CONV2, DOWN2 = 27, 31, 38


def params(megabytes=12):
    return pltpu.CompilerParams(vmem_limit_bytes=megabytes << 20)


def rectified(v):
    return jnp.maximum(v, 0.0) + jnp.log1p(jnp.exp(-jnp.abs(v))) - SHIFT


def slope(stored):
    return 1.0 - 0.5 * jnp.exp(-stored.astype(F32))


def dot(a, b):
    return jnp.dot(a, b, preferred_element_type=F32)


def dot_tn(a, b):
    return lax.dot_general(a, b, (((0,), (0,)), ((), ())), preferred_element_type=F32)


def dot_nt(a, b):
    return lax.dot_general(a, b, (((1,), (1,)), ((), ())), preferred_element_type=F32)


def moved(x, by):
    x = x.astype(F32)
    lane = lax.broadcasted_iota(jnp.int32, x.shape, 1)
    edge = 0 if by == 1 else 127
    return jnp.where(lane == edge, 0.0, pltpu.roll(x, by % 128, 1)).astype(BF16)


def three_two(x):
    even, odd = x[:, :128], x[:, 128:]
    return ((moved(odd, 1), even), (even, odd), (odd, moved(even, -1)))


def three_three(x):
    first, second = x[:, :128], x[:, 128:]
    return ((moved(first, 1), moved(second, 1)), (first, second), (moved(first, -1), moved(second, -1)))


def put_three(ref, row, shifted):
    for j, (left, right) in enumerate(shifted):
        ref[pl.ds(row + j * T, T), 0:128] = left
        ref[pl.ds(row + j * T, T), 128:256] = right


def call(kernel, outs, *args, scratch=(), far=()):
    spec = pl.BlockSpec(memory_space=pltpu.VMEM)
    scalar = pl.BlockSpec(memory_space=pltpu.SMEM)
    remote = pl.BlockSpec(memory_space=pl.ANY)
    return pl.pallas_call(
        kernel,
        in_specs=[remote if i in far else scalar if a.dtype == jnp.int32 and a.ndim == 1 else spec for i, a in enumerate(args)],
        out_specs=[spec] * len(outs),
        out_shape=[space(s, d) for s, d, space in outs],
        scratch_shapes=list(scratch),
        compiler_params=params(),
    )(*[pltpu.with_memory_space_constraint(a, pltpu.HBM) if i in far else a for i, a in enumerate(args)])


def sorted_out(where_ref, one, two):
    even = where_ref[1] == 0
    return jnp.where(even, two, one), jnp.where(even, one, two)


def first_kernel(
    where_ref, vol_far, w_ref, vp_far, a_ref, one_ref, two_ref, sort_ref, wt_ref, vol_ref, vp_ref, in_sems, out_sems
):
    steps = [(n, d) for n in range(CROPS) for d in range(2)]
    fetches = [
        pltpu.make_async_copy(vol_far.at[CROPS * where_ref[0] + n], vol_ref.at[n], in_sems.at[n]) for n in range(CROPS)
    ]
    stores = [
        pltpu.make_async_copy(vp_ref.at[i], vp_far.at[n, d], out_sems.at[i]) for i, (n, d) in enumerate(steps)
    ]
    for fetch in fetches:
        fetch.start()
    to = lax.broadcasted_iota(jnp.int32, (1, 512), 1)
    source = (to % 128) * 4 + (to // 128) % 2 * 2 + to // 256
    sort_ref[...] = jnp.where(lax.broadcasted_iota(jnp.int32, (512, 512), 0) == source, 1.0, 0.0).astype(BF16)
    to = lax.broadcasted_iota(jnp.int32, (1, 1024), 1)
    height = to % 8
    source = to // 8 % 32 * 8 + to // 512 * 4 + height % 2 * 2 + to // 256 % 2
    pick = jnp.where(lax.broadcasted_iota(jnp.int32, (256, 1024), 0) == source, 1.0, 0.0).astype(BF16)
    w = dot_tn(w_ref[...], pick)
    for h in range(4):
        wt_ref[pl.ds(h * 64, 64), :] = jnp.where(height // 2 == h, w, 0.0).astype(BF16)
    for i, (n, d) in enumerate(steps):
        if d == 0:
            fetches[n].wait()
        for k in range(2):
            v = vol_ref[n, :, 2 * d + k].astype(F32).reshape(256, 512).astype(BF16)
            s = dot(v, sort_ref[...]).astype(BF16)
            vp_ref[i, pl.ds(k * 512, 256), :] = s[:, :256]
            vp_ref[i, pl.ds(k * 512 + 256, 256), :] = s[:, 256:]
        stores[i].start()
        a_ref[n, d] = rectified(dot(wt_ref[...], vp_ref[i])).astype(BF16)
    even = where_ref[1] == 0
    for n in range(CROPS):
        one_ref[n] = jnp.where(even, a_ref[n, 1], a_ref[n, 0])
        two_ref[n] = jnp.where(even, a_ref[n, 0], a_ref[n, 1])
    for store in stores:
        store.wait()


def first(where, volume, w1):
    spec = pl.BlockSpec(memory_space=pltpu.VMEM)
    far = pl.BlockSpec(memory_space=pl.ANY)
    return pl.pallas_call(
        first_kernel,
        in_specs=[pl.BlockSpec(memory_space=pltpu.SMEM), far, spec],
        out_specs=[far, spec, spec, spec],
        out_shape=[
            pltpu.HBM((CROPS, 2, 1024, 256), BF16),
            pltpu.VMEM((CROPS, 2, 256, 256), BF16),
            pltpu.VMEM((CROPS, 256, 256), BF16),
            pltpu.VMEM((CROPS, 256, 256), BF16),
        ],
        scratch_shapes=[
            pltpu.VMEM((512, 512), BF16),
            pltpu.VMEM((256, 1024), BF16),
            pltpu.VMEM((CROPS, 32, 4, 8, 512), BF16),
            pltpu.VMEM((4, 1024, 256), BF16),
            pltpu.SemaphoreType.DMA((CROPS,)),
            pltpu.SemaphoreType.DMA((4,)),
        ],
        compiler_params=params(),
    )(where, pltpu.with_memory_space_constraint(volume, pltpu.HBM), pltpu.with_memory_space_constraint(w1, pltpu.HBM))


def prepare_kernel(
    w2_ref, w3_far, wd_ref, head_ref, f2_ref, b2_ref, f3_ref, b3_ref, perm_ref, d_ref, wh_ref, rows_ref, w3_ref, sem
):
    fetch = pltpu.make_async_copy(w3_far, w3_ref, sem)
    fetch.start()
    low = lax.broadcasted_iota(jnp.int32, (64, 128), 1) < 64
    zero = jnp.zeros((64, 128), F32)
    for d in range(3):
        for j in range(3):
            at = (d * 3 + j) * T
            back = (8 - d * 3 - j) * T
            w = [w2_ref[d * 9 + h * 3 + j].astype(F32) for h in range(3)]
            pairs = {
                (0, 0): jnp.where(low, w[1], w[2]),
                (0, 1): zero,
                (1, 0): jnp.where(low, w[0], w[1]),
                (1, 1): jnp.where(low, w[2], 0.0),
                (2, 0): jnp.where(low, 0.0, w[0]),
                (2, 1): jnp.where(low, w[1], w[2]),
                (3, 0): zero,
                (3, 1): jnp.where(low, w[0], w[1]),
            }
            for (row, col), block in pairs.items():
                f2_ref[pl.ds(row * 64, 64), pl.ds(at + col * 128, 128)] = block.astype(BF16)
            b2_ref[:, pl.ds(back, T)] = f2_ref[:, pl.ds(at, T)].astype(F32).T.astype(BF16)
    rows_ref[pl.ds(0, 512), :] = wd_ref[...].astype(F32)
    for d in range(2):
        for p in range(2):
            for h in range(4):
                block = rows_ref[pl.ds(d * 4 + h % 2 * 2 + p, 64, stride=8), :].astype(BF16)
                d_ref[2 * d + p, pl.ds(h * 64, 64), pl.ds(h // 2 * 128, 128)] = block
                d_ref[2 * d + p, pl.ds(h * 64, 64), pl.ds(128 - h // 2 * 128, 128)] = jnp.zeros_like(block)
    rows_ref[pl.ds(0, 128), :] = jnp.zeros((128, 128), F32)
    rows_ref[pl.ds(0, 4), :] = head_ref[...].astype(F32)
    wht = rows_ref[pl.ds(0, 128), :]
    wh_ref[pl.ds(0, 128), :] = wht.T.astype(BF16)
    wh_ref[pl.ds(128, 128), :] = wht.astype(BF16)
    to = lax.broadcasted_iota(jnp.int32, (1, 256), 1)
    source = to // 4 % 2 * 512 + to % 2 * 256 + (to // 128 * 16 + to // 8 % 16) * 8 + to // 2 % 2
    perm_ref[...] = jnp.where(lax.broadcasted_iota(jnp.int32, (1024, 256), 0) == source, 1.0, 0.0).astype(BF16)
    fetch.wait()
    for d in range(3):
        for j in range(3):
            at = (d * 3 + j) * T
            back = (8 - d * 3 - j) * T
            for row in range(2):
                for col in range(2):
                    block = w3_ref[d * 9 + (col - row + 1) * 3 + j]
                    f3_ref[pl.ds(row * 128, 128), pl.ds(at + col * 128, 128)] = block
                    b3_ref[pl.ds(col * 128, 128), pl.ds(back + row * 128, 128)] = block.astype(F32).T.astype(BF16)


def prepare(w2, w3, wd, wh):
    def wide(space):
        return ((T, 9 * T), BF16, space)

    return call(
        prepare_kernel,
        [wide(pltpu.VMEM), wide(pltpu.HBM), wide(pltpu.HBM), wide(pltpu.HBM)]
        + [((1024, 256), BF16, pltpu.HBM), ((4, T, T), BF16, pltpu.VMEM), ((256, 128), BF16, pltpu.HBM)],
        w2, w3, wd, wh,
        scratch=[pltpu.VMEM((520, 128), F32), pltpu.VMEM((27, 128, 128), BF16), pltpu.SemaphoreType.DMA],
        far=(1,),
    )


def second_own_kernel(a_ref, f2_ref, out_ref, b_ref):
    for n in range(CROPS):
        for d in range(2):
            put_three(b_ref, (2 * n + d) * 3 * T, three_two(a_ref[n, d]))
        own = pl.ds(n * 6 * T, 6 * T)
        out_ref[n, 0] = dot(f2_ref[:, 3 * T :], b_ref[own, :])
        out_ref[n, 1] = dot(f2_ref[:, : 6 * T], b_ref[own, :])


def second_own(a, f2):
    return call(
        second_own_kernel,
        [((CROPS, 2, T, T), F32, pltpu.VMEM)],
        a, f2,
        scratch=[pltpu.VMEM((12 * T, T), BF16)],
    )[0]


def second_kernel(
    where_ref, one_ref, own_ref, two_ref, f2_ref, wd_ref, marks_ref, h_ref, a3_ref, sent_ref, sides_ref, b_ref, m_ref
):
    for n in range(CROPS):
        for d, plane in enumerate(sorted_out(where_ref, one_ref[n], two_ref[n])):
            at = (2 * n + d) * 3 * T
            sides_ref[n, d] = plane
            put_three(b_ref, at, three_two(plane))
            rest = dot(f2_ref[:, d * 6 * T : d * 6 * T + 3 * T], b_ref[pl.ds(at, 3 * T), :])
            h = rectified(own_ref[n, d] + rest).astype(BF16)
            for p in range(2):
                h_ref[2 * d + p, :, pl.ds(n * 128, 128)] = h[:, p * 128 : (p + 1) * 128]
    total = dot_tn(wd_ref[0], h_ref[0])
    for k in range(1, 4):
        total += dot_tn(wd_ref[k], h_ref[k])
    a3 = rectified(total).astype(BF16)
    a3_ref[...] = a3
    m_ref[...] = jnp.zeros((16, T), F32)
    m_ref[pl.ds(0, 2), :] = marks_ref[...].astype(F32)
    sent_ref[pl.ds(0, T), :] = a3
    sent_ref[pl.ds(T, 16), :] = m_ref[...].astype(BF16)


def second(where, one, own, two, f2, wd, marks):
    return call(
        second_kernel,
        [
            ((4, T, T), BF16, pltpu.HBM),
            ((T, T), BF16, pltpu.VMEM),
            ((T + 16, T), BF16, pltpu.VMEM),
            ((CROPS, 2, T, T), BF16, pltpu.HBM),
        ],
        where, one, own, two, f2, wd, marks,
        scratch=[pltpu.VMEM((12 * T, T), BF16), pltpu.VMEM((16, T), F32)],
    )


def head_own_kernel(a_ref, f3_ref, wh_ref, out_ref, f3_out_ref, wh_out_ref, b_ref):
    put_three(b_ref, 0, three_three(a_ref[...]))
    for k in range(3):
        out_ref[k] = dot(f3_ref[:, (2 - k) * 3 * T : (3 - k) * 3 * T], b_ref[...])
    f3_out_ref[...] = f3_ref[...]
    wh_out_ref[...] = wh_ref[...]


def head_own(a, f3, wh):
    return call(
        head_own_kernel,
        [((3, T, T), F32, pltpu.VMEM), ((T, 9 * T), BF16, pltpu.VMEM), ((256, 128), BF16, pltpu.VMEM)],
        a, f3, wh,
        scratch=[pltpu.VMEM((3 * T, T), BF16)],
    )


def head_kernel(
    scale, where_ref, one_ref, two_ref, near_ref, away_ref, own_ref, f3_ref, wh_ref, marks_ref, b3_ref, a3_ref, h_ref,
    wd_ref, gz_ref, gh_ref, gz2_ref, gone_ref, gtwo_ref, gy_ref, b_ref
):
    lo, hi = sorted_out(where_ref, one_ref[...], two_ref[...])
    low_half = where_ref[2] == 0
    lo2 = jnp.where(low_half, away_ref[...], near_ref[...])
    hi2 = jnp.where(low_half, near_ref[...], away_ref[...])
    for k, plane in enumerate((lo2, lo[:T], hi[:T], hi2)):
        put_three(b_ref, k * 3 * T, three_three(plane))
    sums = (
        own_ref[0] + dot(f3_ref[:, : 6 * T], b_ref[: 6 * T, :]),
        own_ref[1] + dot(f3_ref[:, : 3 * T], b_ref[3 * T : 6 * T, :]) + dot(f3_ref[:, 6 * T :], b_ref[6 * T : 9 * T, :]),
        own_ref[2] + dot(f3_ref[:, 3 * T :], b_ref[6 * T :, :]),
    )
    marks = (lo[T:].astype(F32), marks_ref[...].astype(F32), hi[T:].astype(F32))
    row = lax.broadcasted_iota(jnp.int32, (128, T), 0)
    total = jnp.zeros((128, 128), F32)
    for k in range(3):
        top = rectified(sums[k]).astype(BF16)
        for h in range(2):
            mine = top[h * 128 : (h + 1) * 128]
            logits = dot(wh_ref[pl.ds(128, 128), :], mine)
            powers = jnp.where(row < 4, jnp.exp(logits), 0.0)
            share = powers / jnp.sum(powers, axis=0, keepdims=True)
            chosen = jnp.where(row.astype(F32) == marks[k][h : h + 1], 1.0, 0.0)
            g = jnp.where(row < 4, (share - chosen) * scale, 0.0)
            if k != 1:
                g = jnp.where(where_ref[3 + k // 2] == 1, g, 0.0)
            g = g.astype(BF16)
            if k == 1:
                total += dot_nt(mine, g)
            gz_ref[k, pl.ds(h * 128, 128), :] = (dot(wh_ref[pl.ds(0, 128), :], g) * slope(mine)).astype(BF16)
    gh_ref[...] = total
    for k in range(3):
        put_three(b_ref, k * 3 * T, three_three(gz_ref[k]))
    gy = (dot(b3_ref[...], b_ref[: 9 * T, :]) * slope(a3_ref[...])).astype(BF16)
    gy_ref[...] = gy
    for d in range(2):
        for p in range(2):
            k = 2 * d + p
            q = (dot(wd_ref[k], gy) * slope(h_ref[k])).astype(BF16)
            for n in range(CROPS):
                gz2_ref[n, d, :, pl.ds(p * 128, 128)] = q[:, n * 128 : (n + 1) * 128]
    even = where_ref[1] == 0
    for n in range(CROPS):
        gone_ref[n] = jnp.where(even, gz2_ref[n, 1], gz2_ref[n, 0])
        gtwo_ref[n] = jnp.where(even, gz2_ref[n, 0], gz2_ref[n, 1])


def head(where, one, two, near, away, own, f3, wh, marks, b3, a3, h, wd, scale):
    return call(
        functools.partial(head_kernel, scale),
        [
            ((3, T, T), BF16, pltpu.VMEM),
            ((128, 128), F32, pltpu.VMEM),
            ((CROPS, 2, T, T), BF16, pltpu.VMEM),
            ((CROPS, T, T), BF16, pltpu.VMEM),
            ((CROPS, T, T), BF16, pltpu.VMEM),
            ((T, T), BF16, pltpu.VMEM),
        ],
        where, one, two, near, away, own, f3, wh, marks, b3, a3, h, wd,
        scratch=[pltpu.VMEM((12 * T, T), BF16)],
    )


def weight_three_kernel(where_ref, g_ref, one_ref, a_ref, two_ref, gy_ref, h_ref, out_ref, gd_ref, s_ref):
    gy = gy_ref[...]
    for k in range(4):
        gd_ref[k] = dot_nt(gy[:128], h_ref[k, :128]) + dot_nt(gy[128:], h_ref[k, 128:])
    put_three(s_ref, 0, three_three(g_ref[1]))
    lo, hi = sorted_out(where_ref, one_ref[:T], two_ref[:T])
    for d, a in enumerate((lo, a_ref[...], hi)):
        for j in range(3):
            t = dot_nt(s_ref[pl.ds((2 - j) * T, T), :], a)
            out_ref[d * 9 + j] = t[128:, :128]
            out_ref[d * 9 + 3 + j] = t[:128, :128] + t[128:, 128:]
            out_ref[d * 9 + 6 + j] = t[:128, 128:]


def weight_three(where, g, one, a, two, gy, h):
    return call(
        weight_three_kernel,
        [((27, 128, 128), F32, pltpu.VMEM), ((4, 128, 128), F32, pltpu.VMEM)],
        where, g, one, a, two, gy, h,
        scratch=[pltpu.VMEM((3 * T, T), BF16)],
    )


def weight_two_kernel(g_ref, a_ref, sides_ref, out_ref, gs_ref, as_ref):
    for n in range(CROPS):
        planes = (sides_ref[n, 0], a_ref[n, 0], a_ref[n, 1], sides_ref[n, 1])
        for d in range(2):
            at = (2 * n + d) * T
            for j, (left, right) in enumerate(three_two(g_ref[n, d])):
                gs_ref[2 - j, :, pl.ds(at, 128)] = left
                gs_ref[2 - j, :, pl.ds(at + 128, 128)] = right
            for k in range(3):
                as_ref[k, :, pl.ds(at, T)] = planes[d + k]
    low = lax.broadcasted_iota(jnp.int32, (64, 128), 1) < 64
    block = (lax.broadcasted_iota(jnp.int32, (64, 128), 1) // 32) % 2 == 0
    sums = {}
    for d in range(3):
        for j in range(3):
            t = dot_nt(gs_ref[j], as_ref[d])
            q = lambda r, c: t[r * 64 : (r + 1) * 64, c * 128 : (c + 1) * 128]
            sums[d, 0, j] = jnp.where(low, q(1, 0) + q(3, 1), q(2, 0))
            sums[d, 1, j] = jnp.where(low, q(0, 0) + q(2, 1), q(1, 0) + q(3, 1))
            sums[d, 2, j] = jnp.where(low, q(1, 1), q(0, 0) + q(2, 1))
        for h in range(3):
            for j in range(3):
                s = sums[d, h, j]
                sums[d, h, j] = s + pltpu.roll(s, 64, 1)
    taps = [sums[t // 9, t // 3 % 3, t % 3] for t in range(27)] + [jnp.zeros((64, 128), F32)]
    for g in range(7):
        four = taps[4 * g : 4 * g + 4]
        turned = [pltpu.roll(x, 32, 1) for x in four]
        out_ref[g, 0] = jnp.where(low, jnp.where(block, four[0], turned[1]), jnp.where(block, four[2], turned[3]))
        out_ref[g, 1] = jnp.where(low, jnp.where(block, turned[0], four[1]), jnp.where(block, turned[2], four[3]))


def weight_two(g, a, sides):
    return call(
        weight_two_kernel,
        [((7, 2, 64, 128), F32, pltpu.VMEM)],
        g, a, sides,
        scratch=[pltpu.VMEM((3, T, 4 * T), BF16), pltpu.VMEM((3, T, 4 * T), BF16)],
    )[0]


def pack_kernel(where_ref, w3_ref, d3_ref, w2_ref, gh_ref, keep_ref, send_ref, pack_ref, head_ref):
    for t in range(27):
        pack_ref[pl.ds(t, 128, stride=ROWS), :] = w3_ref[t]
    for k in range(4):
        pack_ref[pl.ds(DOWN3 + k, 128, stride=ROWS), :] = d3_ref[k]
    head_ref[pl.ds(0, 128), :] = gh_ref[...]
    lane = lax.broadcasted_iota(jnp.int32, (64, 128), 1)
    for half in range(2):
        for g in range(6):
            pack_ref[pl.ds(half * ROWS + CONV2 + g, 64, stride=2 * ROWS), :] = w2_ref[g, half]
        heads = pltpu.roll(head_ref[pl.ds(half, 64, stride=2), :], 96, 1)
        pack_ref[pl.ds(half * ROWS + CONV2 + 6, 64, stride=2 * ROWS), :] = jnp.where(lane < 96, w2_ref[6, half], heads)
    zero = jnp.zeros((128, 128), F32)
    pack_ref[pl.ds(DOWN2, 128, stride=ROWS), :] = zero
    pack_ref[pl.ds(DOWN2 + 1, 128, stride=ROWS), :] = zero
    keep_ref[...] = pack_ref[pl.ds(pl.multiple_of(where_ref[0] * 64 * ROWS, 64 * ROWS), 64 * ROWS), :]
    send_ref[...] = pack_ref[pl.ds(pl.multiple_of((1 - where_ref[0]) * 64 * ROWS, 64 * ROWS), 64 * ROWS), :].astype(BF16)


def packed(*args):
    half = (64 * ROWS, 128)
    return call(
        pack_kernel,
        [(half, F32, pltpu.VMEM), (half, BF16, pltpu.VMEM)],
        *args,
        scratch=[pltpu.VMEM((129 * ROWS, 128), F32), pltpu.VMEM((136, 128), F32)],
    )


def last_own_kernel(g_ref, b2_ref, out_ref, b_ref):
    for n in range(CROPS):
        for d in range(2):
            put_three(b_ref, (2 * n + d) * 3 * T, three_two(g_ref[n, d]))
        own = pl.ds(n * 6 * T, 6 * T)
        out_ref[n, 0] = dot(b2_ref[:, 3 * T :], b_ref[own, :])
        out_ref[n, 1] = dot(b2_ref[:, : 6 * T], b_ref[own, :])


def last_own(g, b2):
    return call(
        last_own_kernel,
        [((CROPS, 2, T, T), F32, pltpu.VMEM)],
        g, b2,
        scratch=[pltpu.VMEM((12 * T, T), BF16)],
    )[0]


def last_kernel(where_ref, one_ref, own_ref, two_ref, b2_ref, a_ref, vp_ref, perm_ref, down_ref, b_ref, t_ref):
    for n in range(CROPS):
        gy = []
        for d, plane in enumerate(sorted_out(where_ref, one_ref[n], two_ref[n])):
            at = (2 * n + d) * 3 * T
            put_three(b_ref, at, three_two(plane))
            rest = dot(b2_ref[:, d * 6 * T : d * 6 * T + 3 * T], b_ref[pl.ds(at, 3 * T), :])
            gy.append(((own_ref[n, d] + rest) * slope(a_ref[n, d])).astype(BF16))
        t = dot_nt(gy[0], vp_ref[n, 0]) + dot_nt(gy[1], vp_ref[n, 1])
        if n == 0:
            t_ref[...] = t
        else:
            t_ref[...] += t
    pairs = []
    lane = lax.broadcasted_iota(jnp.int32, (64, 128), 1)
    for tile in range(8):
        at = pl.ds(tile * 128, 128)
        x = jnp.zeros((64, 128), F32)
        for h in range(4):
            x = jnp.where(lane % 8 // 2 == h, t_ref[pl.ds(h * 64, 64), at], x)
        x = x + pltpu.roll(x, 126, 1)
        x = x + pltpu.roll(x, 124, 1)
        pairs.append(x.astype(BF16))
    down_ref[...] = dot(jnp.concatenate(pairs, axis=1), perm_ref[...])


def last(*args):
    return call(
        last_kernel,
        [((64, 256), F32, pltpu.VMEM)],
        *args,
        scratch=[pltpu.VMEM((12 * T, T), BF16), pltpu.VMEM((T, 1024), F32)],
    )[0]


def join_kernel(where_ref, down_ref, keep_ref, came_ref, out_ref, d_ref):
    for k, sec in enumerate((where_ref[0], 1 - where_ref[0])):
        mine = pl.ds(pl.multiple_of(sec * 32, 32), 32)
        for half in range(2):
            to = pl.ds(half * ROWS + DOWN2 + k, 32, stride=2 * ROWS)
            d_ref[to, :] = down_ref[mine, half * 128 : (half + 1) * 128]
    row = lax.broadcasted_iota(jnp.int32, (ROWS, 128), 0)
    for j in range(64):
        at = pl.ds(j * ROWS, ROWS)
        both = keep_ref[at, :] + came_ref[at, :].astype(F32)
        out_ref[at, :] = jnp.where(row >= DOWN2, d_ref[at, :], both).astype(BF16)


def joined(*args):
    return call(
        join_kernel,
        [((64 * ROWS, 128), BF16, pltpu.VMEM)],
        *args,
        scratch=[pltpu.VMEM((66 * ROWS, 128), F32)],
    )[0]


def swapped(one, two):
    count = lax.axis_size("space")
    near = [(i, i ^ 1) for i in range(count)]
    far = [(i, ((i + 1) ^ 1) - 1) for i in range(1, count - 1)]
    two = lax.ppermute(two, "space", far)
    return lax.ppermute(one, "space", near), two


def swapped_two(x, later):
    count = lax.axis_size("space")
    near = [(i, i ^ 2) for i in range(count)]
    away = [(i, ((i + 2) ^ 2) - 2) for i in range(2, count - 2)]
    away = lax.ppermute(x, "space", away)
    return lax.ppermute(later, "space", near), away


def partner(x):
    return lax.ppermute(x, "section", [(0, 1), (1, 0)])


def flat(x, step, rows):
    c = lax.broadcasted_iota(jnp.int32, (128, 128), 0) * step
    lane = lax.broadcasted_iota(jnp.int32, (128, 128), 1)
    x = x.T
    pieces = []
    for k in range(16):
        piece = x[8 * k : 8 * k + 8]
        for part in (step // 2, step - step // 2):
            piece = pltpu.roll(piece, 0, 1, stride=part, stride_axis=0)
        pieces.append(pltpu.roll(piece, 8 * k * step % 128, 1) if 8 * k * step % 128 else piece)
    turned = jnp.concatenate(pieces, axis=0)
    row = lax.broadcasted_iota(jnp.int32, (rows, 128), 0)
    start = lax.broadcasted_iota(jnp.int32, (rows, 128), 1) * step // 128
    exact = functools.partial(jnp.dot, precision=lax.Precision.HIGHEST, preferred_element_type=F32)
    here = lane >= c % 128
    same = exact(jnp.where(row == start, 1.0, 0.0), jnp.where(here, turned, 0.0))
    return same + exact(jnp.where(row == start + 1, 1.0, 0.0), jnp.where(here, 0.0, turned))


def unpack_kernel(sums_ref, two_ref, three_ref, conv_ref, head_ref, x_ref, y_ref, z_ref):
    last = sums_ref[pl.ds(DOWN2 - 1, 1), :]
    for k in range(4):
        head_ref[k] = jnp.sum(jnp.where(lax.broadcasted_iota(jnp.int32, (1, 128), 1) == 96 + k, last, 0.0))
    for ref in (x_ref, y_ref, z_ref):
        ref[...] = jnp.zeros((128, 128), F32)
    x_ref[pl.ds(0, DOWN3), :] = sums_ref[pl.ds(0, DOWN3), :]
    lane = lax.broadcasted_iota(jnp.int32, (7, 128), 1)
    rows = sums_ref[pl.ds(CONV2, 7), :]
    for i in range(4):
        y_ref[pl.ds(i, 7, stride=4), :] = jnp.where(lane < 32, rows if i == 0 else pltpu.roll(rows, 128 - 32 * i, 1), 0.0)
    y_ref[pl.ds(27, 1), :] = jnp.zeros((1, 128), F32)
    lane = lax.broadcasted_iota(jnp.int32, (1, 128), 1)
    for k in range(4):
        row = sums_ref[pl.ds(DOWN3 + k, 1), :]
        at = k // 2 * 4 + k % 2
        z_ref[pl.ds(at, 1), :] = jnp.where(lane < 64, row, 0.0)
        z_ref[pl.ds(at + 2, 1), :] = jnp.where(lane < 64, pltpu.roll(row, 64, 1), 0.0)
    conv_ref[...] = flat(x_ref[...], 27, 32)[:27]
    two_ref[...] = flat(y_ref[...], 27, 8)[:7]
    three_ref[...] = flat(z_ref[...], 8, 8)[:4]


def unpack(sums, came):
    spec = pl.BlockSpec(memory_space=pltpu.VMEM)
    two, three, conv, head = pl.pallas_call(
        unpack_kernel,
        in_specs=[spec],
        out_specs=[spec] * 3 + [pl.BlockSpec(memory_space=pltpu.SMEM)],
        out_shape=[pltpu.HBM((rows, 128), F32) for rows in (7, 4, 27)] + [jax.ShapeDtypeStruct((4,), F32)],
        scratch_shapes=[pltpu.VMEM((128, 128), F32)] * 3,
        compiler_params=params(),
    )(sums)
    return sums[DOWN2] + came[0], two.reshape(-1)[: 27 * 32], three.reshape(-1), conv.reshape(-1), head


def finish(pack):
    terms = lax.all_to_all(pack, "space", 0, 0, tiled=True)
    sums = jnp.sum(terms.astype(F32), axis=0)
    return unpack(sums, partner(sums[DOWN2 + 1 :]))


def per_device(volume, labels, down_weight_two, w_conv_two, down_weight_three, w_conv_three, w_head):
    count = lax.axis_size("space")
    voxels = labels.shape[0] * labels.shape[1] * count * labels.shape[2] * labels.shape[3]
    scale = 1.0 / math.sqrt(voxels)
    sec = lax.axis_index("section").astype(jnp.int32)
    space = lax.axis_index("space").astype(jnp.int32)
    where = jnp.stack([sec, space % 2, space % 4 // 2, jnp.minimum(space, 1), jnp.minimum(count - 1 - space, 1)])

    w1 = down_weight_two.transpose(1, 2, 3, 4, 0).reshape(256, 64)
    wd = down_weight_three.transpose(1, 2, 3, 4, 0).reshape(512, 128)
    w2 = w_conv_two.transpose(2, 3, 4, 0, 1).reshape(27, 64, 64)
    w2 = jnp.concatenate([w2, w2], axis=2)
    w3 = w_conv_three.transpose(2, 3, 4, 0, 1).reshape(27, 128, 128)
    marks = lax.dynamic_slice_in_dim(labels[:, 0], CROPS * sec, CROPS, axis=0)
    marks = marks.transpose(1, 0, 2).reshape(2, 256)

    vp, a2, one, two = first(where, volume, w1)
    a2_one, a2_two = swapped(one, two)
    f2, b2, f3, b3, perm, wd, wh = prepare(w2, w3, wd, w_head.T)
    own = second_own(a2, f2)
    a2_two, a2_one, own = lax.optimization_barrier((a2_two, a2_one, own))
    h2, a3, sent, sides = second(where, a2_one, own, a2_two, f2, wd, marks)
    a3_one, a3_two = swapped(sent, sent)
    a3_one, later = lax.optimization_barrier((a3_one, a3))
    a3_near, a3_away = swapped_two(a3, later)
    own, f3, wh = head_own(a3, f3, wh)
    a3_two, a3_away, a3_one, a3_near, own, f3, wh = lax.optimization_barrier(
        (a3_two, a3_away, a3_one, a3_near, own, f3, wh)
    )
    gz4, gh, gz2, one, two, gy3 = head(
        where, a3_one, a3_two, a3_near, a3_away, own, f3, wh, marks, b3, a3, h2, wd, scale
    )
    gw3, gd3 = weight_three(where, gz4, a3_one, a3, a3_two, gy3, h2)
    gz2_one, gz2_two = swapped(one, two)
    own = last_own(gz2, b2)
    gw2 = weight_two(gz2, a2, sides)
    keep, send = packed(where, gw3, gd3, gw2, gh)
    gz2_two, gz2_one, send, own = lax.optimization_barrier((gz2_two, gz2_one, send, own))
    came = partner(send)
    down = last(where, gz2_one, own, gz2_two, b2, a2, vp, perm)
    pack = joined(where, down, keep, came)
    return finish(pack.reshape(64, ROWS, 128))


def solution(mesh):
    whole = P(("section", "space"))
    return jax.shard_map(
        per_device,
        mesh=mesh,
        in_specs=(P(None, None, "space", None, None), P(None, "space", None, None), P(), P(), P(), P(), P()),
        out_specs=(whole,) * 5,
        check_vma=False,
    )
```

```python
import functools
import math

import jax
import jax.numpy as jnp
from jax import lax
from jax.experimental import pallas as pl
from jax.experimental.pallas import tpu as pltpu
from jax.sharding import PartitionSpec as P


F32 = jnp.float32
BF16 = jnp.bfloat16
SHIFT = math.log(2.0)
CROPS = 2
T = 256
ROWS = 40
DOWN3, CONV2, DOWN2 = 27, 31, 38


def params(megabytes=12):
    return pltpu.CompilerParams(vmem_limit_bytes=megabytes << 20)


def rectified(v):
    return jnp.maximum(v, 0.0) + jnp.log1p(jnp.exp(-jnp.abs(v))) - SHIFT


def slope(stored):
    return 1.0 - 0.5 * jnp.exp(-stored.astype(F32))


def dot(a, b):
    return jnp.dot(a, b, preferred_element_type=F32)


def dot_tn(a, b):
    return lax.dot_general(a, b, (((0,), (0,)), ((), ())), preferred_element_type=F32)


def dot_nt(a, b):
    return lax.dot_general(a, b, (((1,), (1,)), ((), ())), preferred_element_type=F32)


def moved(x, by):
    x = x.astype(F32)
    lane = lax.broadcasted_iota(jnp.int32, x.shape, 1)
    edge = 0 if by == 1 else 127
    return jnp.where(lane == edge, 0.0, pltpu.roll(x, by % 128, 1)).astype(BF16)


def three_two(x):
    even, odd = x[:, :128], x[:, 128:]
    return ((moved(odd, 1), even), (even, odd), (odd, moved(even, -1)))


def three_three(x):
    first, second = x[:, :128], x[:, 128:]
    return ((moved(first, 1), moved(second, 1)), (first, second), (moved(first, -1), moved(second, -1)))


def put_three(ref, row, shifted):
    for j, (left, right) in enumerate(shifted):
        ref[pl.ds(row + j * T, T), 0:128] = left
        ref[pl.ds(row + j * T, T), 128:256] = right


def call(kernel, outs, *args, scratch=(), far=()):
    spec = pl.BlockSpec(memory_space=pltpu.VMEM)
    scalar = pl.BlockSpec(memory_space=pltpu.SMEM)
    remote = pl.BlockSpec(memory_space=pl.ANY)
    return pl.pallas_call(
        kernel,
        in_specs=[remote if i in far else scalar if a.dtype == jnp.int32 and a.ndim == 1 else spec for i, a in enumerate(args)],
        out_specs=[spec] * len(outs),
        out_shape=[space(s, d) for s, d, space in outs],
        scratch_shapes=list(scratch),
        compiler_params=params(),
    )(*[pltpu.with_memory_space_constraint(a, pltpu.HBM) if i in far else a for i, a in enumerate(args)])


def sorted_out(where_ref, one, two):
    even = where_ref[1] == 0
    return jnp.where(even, two, one), jnp.where(even, one, two)


def first_kernel(
    where_ref, vol_far, w_ref, vp_far, a_ref, one_ref, two_ref, sort_ref, wt_ref, vol_ref, vp_ref, in_sems, out_sems
):
    steps = [(n, d) for n in range(CROPS) for d in range(2)]
    fetches = [
        pltpu.make_async_copy(vol_far.at[CROPS * where_ref[0] + n], vol_ref.at[n], in_sems.at[n]) for n in range(CROPS)
    ]
    stores = [
        pltpu.make_async_copy(vp_ref.at[i], vp_far.at[n, d], out_sems.at[i]) for i, (n, d) in enumerate(steps)
    ]
    for fetch in fetches:
        fetch.start()
    to = lax.broadcasted_iota(jnp.int32, (1, 512), 1)
    source = (to % 128) * 4 + (to // 128) % 2 * 2 + to // 256
    sort_ref[...] = jnp.where(lax.broadcasted_iota(jnp.int32, (512, 512), 0) == source, 1.0, 0.0).astype(BF16)
    to = lax.broadcasted_iota(jnp.int32, (1, 1024), 1)
    height = to % 8
    source = to // 8 % 32 * 8 + to // 512 * 4 + height % 2 * 2 + to // 256 % 2
    pick = jnp.where(lax.broadcasted_iota(jnp.int32, (256, 1024), 0) == source, 1.0, 0.0).astype(BF16)
    w = dot_tn(w_ref[...], pick)
    for h in range(4):
        wt_ref[pl.ds(h * 64, 64), :] = jnp.where(height // 2 == h, w, 0.0).astype(BF16)
    for i, (n, d) in enumerate(steps):
        if d == 0:
            fetches[n].wait()
        for k in range(2):
            v = vol_ref[n, :, 2 * d + k].astype(F32).reshape(256, 512).astype(BF16)
            s = dot(v, sort_ref[...]).astype(BF16)
            vp_ref[i, pl.ds(k * 512, 256), :] = s[:, :256]
            vp_ref[i, pl.ds(k * 512 + 256, 256), :] = s[:, 256:]
        stores[i].start()
        a_ref[n, d] = rectified(dot(wt_ref[...], vp_ref[i])).astype(BF16)
    even = where_ref[1] == 0
    for n in range(CROPS):
        one_ref[n] = jnp.where(even, a_ref[n, 1], a_ref[n, 0])
        two_ref[n] = jnp.where(even, a_ref[n, 0], a_ref[n, 1])
    for store in stores:
        store.wait()


def first(where, volume, w1):
    spec = pl.BlockSpec(memory_space=pltpu.VMEM)
    far = pl.BlockSpec(memory_space=pl.ANY)
    return pl.pallas_call(
        first_kernel,
        in_specs=[pl.BlockSpec(memory_space=pltpu.SMEM), far, spec],
        out_specs=[far, spec, spec, spec],
        out_shape=[
            pltpu.HBM((CROPS, 2, 1024, 256), BF16),
            pltpu.VMEM((CROPS, 2, 256, 256), BF16),
            pltpu.VMEM((CROPS, 256, 256), BF16),
            pltpu.VMEM((CROPS, 256, 256), BF16),
        ],
        scratch_shapes=[
            pltpu.VMEM((512, 512), BF16),
            pltpu.VMEM((256, 1024), BF16),
            pltpu.VMEM((CROPS, 32, 4, 8, 512), BF16),
            pltpu.VMEM((4, 1024, 256), BF16),
            pltpu.SemaphoreType.DMA((CROPS,)),
            pltpu.SemaphoreType.DMA((4,)),
        ],
        compiler_params=params(),
    )(where, pltpu.with_memory_space_constraint(volume, pltpu.HBM), pltpu.with_memory_space_constraint(w1, pltpu.HBM))


def prepare_kernel(
    w2_ref, w3_far, wd_ref, head_ref, f2_ref, b2_ref, f3_ref, b3_ref, perm_ref, d_ref, wh_ref, rows_ref, w3_ref, sem
):
    fetch = pltpu.make_async_copy(w3_far, w3_ref, sem)
    fetch.start()
    low = lax.broadcasted_iota(jnp.int32, (64, 128), 1) < 64
    zero = jnp.zeros((64, 128), F32)
    for d in range(3):
        for j in range(3):
            at = (d * 3 + j) * T
            back = (8 - d * 3 - j) * T
            w = [w2_ref[d * 9 + h * 3 + j].astype(F32) for h in range(3)]
            pairs = {
                (0, 0): jnp.where(low, w[1], w[2]),
                (0, 1): zero,
                (1, 0): jnp.where(low, w[0], w[1]),
                (1, 1): jnp.where(low, w[2], 0.0),
                (2, 0): jnp.where(low, 0.0, w[0]),
                (2, 1): jnp.where(low, w[1], w[2]),
                (3, 0): zero,
                (3, 1): jnp.where(low, w[0], w[1]),
            }
            for (row, col), block in pairs.items():
                f2_ref[pl.ds(row * 64, 64), pl.ds(at + col * 128, 128)] = block.astype(BF16)
            b2_ref[:, pl.ds(back, T)] = f2_ref[:, pl.ds(at, T)].astype(F32).T.astype(BF16)
    rows_ref[pl.ds(0, 512), :] = wd_ref[...].astype(F32)
    for d in range(2):
        for p in range(2):
            for h in range(4):
                block = rows_ref[pl.ds(d * 4 + h % 2 * 2 + p, 64, stride=8), :].astype(BF16)
                d_ref[2 * d + p, pl.ds(h * 64, 64), pl.ds(h // 2 * 128, 128)] = block
                d_ref[2 * d + p, pl.ds(h * 64, 64), pl.ds(128 - h // 2 * 128, 128)] = jnp.zeros_like(block)
    rows_ref[pl.ds(0, 128), :] = jnp.zeros((128, 128), F32)
    rows_ref[pl.ds(0, 4), :] = head_ref[...].astype(F32)
    wht = rows_ref[pl.ds(0, 128), :]
    wh_ref[pl.ds(0, 128), :] = wht.T.astype(BF16)
    wh_ref[pl.ds(128, 128), :] = wht.astype(BF16)
    to = lax.broadcasted_iota(jnp.int32, (1, 256), 1)
    source = to // 4 % 2 * 512 + to % 2 * 256 + (to // 128 * 16 + to // 8 % 16) * 8 + to // 2 % 2
    perm_ref[...] = jnp.where(lax.broadcasted_iota(jnp.int32, (1024, 256), 0) == source, 1.0, 0.0).astype(BF16)
    fetch.wait()
    for d in range(3):
        for j in range(3):
            at = (d * 3 + j) * T
            back = (8 - d * 3 - j) * T
            for row in range(2):
                for col in range(2):
                    block = w3_ref[d * 9 + (col - row + 1) * 3 + j]
                    f3_ref[pl.ds(row * 128, 128), pl.ds(at + col * 128, 128)] = block
                    b3_ref[pl.ds(col * 128, 128), pl.ds(back + row * 128, 128)] = block.astype(F32).T.astype(BF16)


def prepare(w2, w3, wd, wh):
    def wide(space):
        return ((T, 9 * T), BF16, space)

    return call(
        prepare_kernel,
        [wide(pltpu.VMEM), wide(pltpu.HBM), wide(pltpu.HBM), wide(pltpu.HBM)]
        + [((1024, 256), BF16, pltpu.HBM), ((4, T, T), BF16, pltpu.VMEM), ((256, 128), BF16, pltpu.HBM)],
        w2, w3, wd, wh,
        scratch=[pltpu.VMEM((520, 128), F32), pltpu.VMEM((27, 128, 128), BF16), pltpu.SemaphoreType.DMA],
        far=(1,),
    )


def second_own_kernel(a_ref, f2_ref, out_ref, b_ref):
    for n in range(CROPS):
        for d in range(2):
            put_three(b_ref, (2 * n + d) * 3 * T, three_two(a_ref[n, d]))
        own = pl.ds(n * 6 * T, 6 * T)
        out_ref[n, 0] = dot(f2_ref[:, 3 * T :], b_ref[own, :])
        out_ref[n, 1] = dot(f2_ref[:, : 6 * T], b_ref[own, :])


def second_own(a, f2):
    return call(
        second_own_kernel,
        [((CROPS, 2, T, T), F32, pltpu.VMEM)],
        a, f2,
        scratch=[pltpu.VMEM((12 * T, T), BF16)],
    )[0]


def second_kernel(
    where_ref, one_ref, own_ref, two_ref, f2_ref, wd_ref, marks_ref, h_ref, a3_ref, sent_ref, sides_ref, b_ref, m_ref
):
    for n in range(CROPS):
        for d, plane in enumerate(sorted_out(where_ref, one_ref[n], two_ref[n])):
            at = (2 * n + d) * 3 * T
            sides_ref[n, d] = plane
            put_three(b_ref, at, three_two(plane))
            rest = dot(f2_ref[:, d * 6 * T : d * 6 * T + 3 * T], b_ref[pl.ds(at, 3 * T), :])
            h = rectified(own_ref[n, d] + rest).astype(BF16)
            for p in range(2):
                h_ref[2 * d + p, :, pl.ds(n * 128, 128)] = h[:, p * 128 : (p + 1) * 128]
    total = dot_tn(wd_ref[0], h_ref[0])
    for k in range(1, 4):
        total += dot_tn(wd_ref[k], h_ref[k])
    a3 = rectified(total).astype(BF16)
    a3_ref[...] = a3
    m_ref[...] = jnp.zeros((16, T), F32)
    m_ref[pl.ds(0, 2), :] = marks_ref[...].astype(F32)
    sent_ref[pl.ds(0, T), :] = a3
    sent_ref[pl.ds(T, 16), :] = m_ref[...].astype(BF16)


def second(where, one, own, two, f2, wd, marks):
    return call(
        second_kernel,
        [
            ((4, T, T), BF16, pltpu.HBM),
            ((T, T), BF16, pltpu.VMEM),
            ((T + 16, T), BF16, pltpu.VMEM),
            ((CROPS, 2, T, T), BF16, pltpu.HBM),
        ],
        where, one, own, two, f2, wd, marks,
        scratch=[pltpu.VMEM((12 * T, T), BF16), pltpu.VMEM((16, T), F32)],
    )


def head_own_kernel(a_ref, f3_ref, wh_ref, out_ref, f3_out_ref, wh_out_ref, b_ref):
    put_three(b_ref, 0, three_three(a_ref[...]))
    for k in range(3):
        out_ref[k] = dot(f3_ref[:, (2 - k) * 3 * T : (3 - k) * 3 * T], b_ref[...])
    f3_out_ref[...] = f3_ref[...]
    wh_out_ref[...] = wh_ref[...]


def head_own(a, f3, wh):
    return call(
        head_own_kernel,
        [((3, T, T), F32, pltpu.VMEM), ((T, 9 * T), BF16, pltpu.VMEM), ((256, 128), BF16, pltpu.VMEM)],
        a, f3, wh,
        scratch=[pltpu.VMEM((3 * T, T), BF16)],
    )


def head_kernel(
    scale, where_ref, one_ref, two_ref, near_ref, away_ref, own_ref, f3_ref, wh_ref, marks_ref, b3_ref, a3_ref, h_ref,
    wd_ref, gz_ref, gh_ref, gz2_ref, gone_ref, gtwo_ref, gy_ref, b_ref
):
    lo, hi = sorted_out(where_ref, one_ref[...], two_ref[...])
    low_half = where_ref[2] == 0
    lo2 = jnp.where(low_half, away_ref[...], near_ref[...])
    hi2 = jnp.where(low_half, near_ref[...], away_ref[...])
    for k, plane in enumerate((lo2, lo[:T], hi[:T], hi2)):
        put_three(b_ref, k * 3 * T, three_three(plane))
    sums = (
        own_ref[0] + dot(f3_ref[:, : 6 * T], b_ref[: 6 * T, :]),
        own_ref[1] + dot(f3_ref[:, : 3 * T], b_ref[3 * T : 6 * T, :]) + dot(f3_ref[:, 6 * T :], b_ref[6 * T : 9 * T, :]),
        own_ref[2] + dot(f3_ref[:, 3 * T :], b_ref[6 * T :, :]),
    )
    marks = (lo[T:].astype(F32), marks_ref[...].astype(F32), hi[T:].astype(F32))
    row = lax.broadcasted_iota(jnp.int32, (128, T), 0)
    total = jnp.zeros((128, 128), F32)
    for k in range(3):
        top = rectified(sums[k]).astype(BF16)
        for h in range(2):
            mine = top[h * 128 : (h + 1) * 128]
            logits = dot(wh_ref[pl.ds(128, 128), :], mine)
            powers = jnp.where(row < 4, jnp.exp(logits), 0.0)
            share = powers / jnp.sum(powers, axis=0, keepdims=True)
            chosen = jnp.where(row.astype(F32) == marks[k][h : h + 1], 1.0, 0.0)
            g = jnp.where(row < 4, (share - chosen) * scale, 0.0)
            if k != 1:
                g = jnp.where(where_ref[3 + k // 2] == 1, g, 0.0)
            g = g.astype(BF16)
            if k == 1:
                total += dot_nt(mine, g)
            gz_ref[k, pl.ds(h * 128, 128), :] = (dot(wh_ref[pl.ds(0, 128), :], g) * slope(mine)).astype(BF16)
    gh_ref[...] = total
    for k in range(3):
        put_three(b_ref, k * 3 * T, three_three(gz_ref[k]))
    gy = (dot(b3_ref[...], b_ref[: 9 * T, :]) * slope(a3_ref[...])).astype(BF16)
    gy_ref[...] = gy
    for d in range(2):
        for p in range(2):
            k = 2 * d + p
            q = (dot(wd_ref[k], gy) * slope(h_ref[k])).astype(BF16)
            for n in range(CROPS):
                gz2_ref[n, d, :, pl.ds(p * 128, 128)] = q[:, n * 128 : (n + 1) * 128]
    even = where_ref[1] == 0
    for n in range(CROPS):
        gone_ref[n] = jnp.where(even, gz2_ref[n, 1], gz2_ref[n, 0])
        gtwo_ref[n] = jnp.where(even, gz2_ref[n, 0], gz2_ref[n, 1])


def head(where, one, two, near, away, own, f3, wh, marks, b3, a3, h, wd, scale):
    return call(
        functools.partial(head_kernel, scale),
        [
            ((3, T, T), BF16, pltpu.VMEM),
            ((128, 128), F32, pltpu.VMEM),
            ((CROPS, 2, T, T), BF16, pltpu.VMEM),
            ((CROPS, T, T), BF16, pltpu.VMEM),
            ((CROPS, T, T), BF16, pltpu.VMEM),
            ((T, T), BF16, pltpu.VMEM),
        ],
        where, one, two, near, away, own, f3, wh, marks, b3, a3, h, wd,
        scratch=[pltpu.VMEM((12 * T, T), BF16)],
    )


def weight_three_kernel(where_ref, g_ref, one_ref, a_ref, two_ref, gy_ref, h_ref, out_ref, gd_ref, s_ref):
    gy = gy_ref[...]
    for k in range(4):
        gd_ref[k] = dot_nt(gy[:128], h_ref[k, :128]) + dot_nt(gy[128:], h_ref[k, 128:])
    put_three(s_ref, 0, three_three(g_ref[1]))
    lo, hi = sorted_out(where_ref, one_ref[:T], two_ref[:T])
    for d, a in enumerate((lo, a_ref[...], hi)):
        for j in range(3):
            t = dot_nt(s_ref[pl.ds((2 - j) * T, T), :], a)
            out_ref[d * 9 + j] = t[128:, :128]
            out_ref[d * 9 + 3 + j] = t[:128, :128] + t[128:, 128:]
            out_ref[d * 9 + 6 + j] = t[:128, 128:]


def weight_three(where, g, one, a, two, gy, h):
    return call(
        weight_three_kernel,
        [((27, 128, 128), F32, pltpu.VMEM), ((4, 128, 128), F32, pltpu.VMEM)],
        where, g, one, a, two, gy, h,
        scratch=[pltpu.VMEM((3 * T, T), BF16)],
    )


def weight_two_kernel(g_ref, a_ref, sides_ref, out_ref, gs_ref, as_ref):
    for n in range(CROPS):
        planes = (sides_ref[n, 0], a_ref[n, 0], a_ref[n, 1], sides_ref[n, 1])
        for d in range(2):
            at = (2 * n + d) * T
            for j, (left, right) in enumerate(three_two(g_ref[n, d])):
                gs_ref[2 - j, :, pl.ds(at, 128)] = left
                gs_ref[2 - j, :, pl.ds(at + 128, 128)] = right
            for k in range(3):
                as_ref[k, :, pl.ds(at, T)] = planes[d + k]
    low = lax.broadcasted_iota(jnp.int32, (64, 128), 1) < 64
    block = (lax.broadcasted_iota(jnp.int32, (64, 128), 1) // 32) % 2 == 0
    sums = {}
    for d in range(3):
        for j in range(3):
            t = dot_nt(gs_ref[j], as_ref[d])
            q = lambda r, c: t[r * 64 : (r + 1) * 64, c * 128 : (c + 1) * 128]
            sums[d, 0, j] = jnp.where(low, q(1, 0) + q(3, 1), q(2, 0))
            sums[d, 1, j] = jnp.where(low, q(0, 0) + q(2, 1), q(1, 0) + q(3, 1))
            sums[d, 2, j] = jnp.where(low, q(1, 1), q(0, 0) + q(2, 1))
        for h in range(3):
            for j in range(3):
                s = sums[d, h, j]
                sums[d, h, j] = s + pltpu.roll(s, 64, 1)
    taps = [sums[t // 9, t // 3 % 3, t % 3] for t in range(27)] + [jnp.zeros((64, 128), F32)]
    for g in range(7):
        four = taps[4 * g : 4 * g + 4]
        turned = [pltpu.roll(x, 32, 1) for x in four]
        out_ref[g, 0] = jnp.where(low, jnp.where(block, four[0], turned[1]), jnp.where(block, four[2], turned[3]))
        out_ref[g, 1] = jnp.where(low, jnp.where(block, turned[0], four[1]), jnp.where(block, turned[2], four[3]))


def weight_two(g, a, sides):
    return call(
        weight_two_kernel,
        [((7, 2, 64, 128), F32, pltpu.VMEM)],
        g, a, sides,
        scratch=[pltpu.VMEM((3, T, 4 * T), BF16), pltpu.VMEM((3, T, 4 * T), BF16)],
    )[0]


def pack_kernel(where_ref, w3_ref, d3_ref, w2_ref, gh_ref, keep_ref, send_ref, pack_ref, head_ref):
    for t in range(27):
        pack_ref[pl.ds(t, 128, stride=ROWS), :] = w3_ref[t]
    for k in range(4):
        pack_ref[pl.ds(DOWN3 + k, 128, stride=ROWS), :] = d3_ref[k]
    head_ref[pl.ds(0, 128), :] = gh_ref[...]
    lane = lax.broadcasted_iota(jnp.int32, (64, 128), 1)
    for half in range(2):
        for g in range(6):
            pack_ref[pl.ds(half * ROWS + CONV2 + g, 64, stride=2 * ROWS), :] = w2_ref[g, half]
        heads = pltpu.roll(head_ref[pl.ds(half, 64, stride=2), :], 96, 1)
        pack_ref[pl.ds(half * ROWS + CONV2 + 6, 64, stride=2 * ROWS), :] = jnp.where(lane < 96, w2_ref[6, half], heads)
    zero = jnp.zeros((128, 128), F32)
    pack_ref[pl.ds(DOWN2, 128, stride=ROWS), :] = zero
    pack_ref[pl.ds(DOWN2 + 1, 128, stride=ROWS), :] = zero
    keep_ref[...] = pack_ref[pl.ds(pl.multiple_of(where_ref[0] * 64 * ROWS, 64 * ROWS), 64 * ROWS), :]
    send_ref[...] = pack_ref[pl.ds(pl.multiple_of((1 - where_ref[0]) * 64 * ROWS, 64 * ROWS), 64 * ROWS), :].astype(BF16)


def packed(*args):
    half = (64 * ROWS, 128)
    return call(
        pack_kernel,
        [(half, F32, pltpu.VMEM), (half, BF16, pltpu.VMEM)],
        *args,
        scratch=[pltpu.VMEM((129 * ROWS, 128), F32), pltpu.VMEM((136, 128), F32)],
    )


def last_own_kernel(g_ref, b2_ref, a_ref, out_ref, slope_ref, b_ref):
    slope_ref[...] = slope(a_ref[...])
    for n in range(CROPS):
        for d in range(2):
            put_three(b_ref, (2 * n + d) * 3 * T, three_two(g_ref[n, d]))
        own = pl.ds(n * 6 * T, 6 * T)
        out_ref[n, 0] = dot(b2_ref[:, 3 * T :], b_ref[own, :])
        out_ref[n, 1] = dot(b2_ref[:, : 6 * T], b_ref[own, :])


def last_own(g, b2, a):
    return call(
        last_own_kernel,
        [((CROPS, 2, T, T), F32, pltpu.VMEM)] * 2,
        g, b2, a,
        scratch=[pltpu.VMEM((12 * T, T), BF16)],
    )


def last_kernel(where_ref, one_ref, own_ref, two_ref, b2_ref, a_ref, vp_ref, perm_ref, down_ref, b_ref, t_ref):
    for n in range(CROPS):
        gy = []
        for d, plane in enumerate(sorted_out(where_ref, one_ref[n], two_ref[n])):
            at = (2 * n + d) * 3 * T
            put_three(b_ref, at, three_two(plane))
            rest = dot(b2_ref[:, d * 6 * T : d * 6 * T + 3 * T], b_ref[pl.ds(at, 3 * T), :])
            gy.append(((own_ref[n, d] + rest) * a_ref[n, d]).astype(BF16))
        t = dot_nt(gy[0], vp_ref[n, 0]) + dot_nt(gy[1], vp_ref[n, 1])
        if n == 0:
            t_ref[...] = t
        else:
            t_ref[...] += t
    pairs = []
    lane = lax.broadcasted_iota(jnp.int32, (64, 128), 1)
    for tile in range(8):
        at = pl.ds(tile * 128, 128)
        x = jnp.zeros((64, 128), F32)
        for h in range(4):
            x = jnp.where(lane % 8 // 2 == h, t_ref[pl.ds(h * 64, 64), at], x)
        x = x + pltpu.roll(x, 126, 1)
        x = x + pltpu.roll(x, 124, 1)
        pairs.append(x.astype(BF16))
    down_ref[...] = dot(jnp.concatenate(pairs, axis=1), perm_ref[...])


def last(*args):
    return call(
        last_kernel,
        [((64, 256), F32, pltpu.VMEM)],
        *args,
        scratch=[pltpu.VMEM((12 * T, T), BF16), pltpu.VMEM((T, 1024), F32)],
    )[0]


def join_kernel(where_ref, down_ref, keep_ref, came_ref, out_ref, d_ref):
    for k, sec in enumerate((where_ref[0], 1 - where_ref[0])):
        mine = pl.ds(pl.multiple_of(sec * 32, 32), 32)
        for half in range(2):
            to = pl.ds(half * ROWS + DOWN2 + k, 32, stride=2 * ROWS)
            d_ref[to, :] = down_ref[mine, half * 128 : (half + 1) * 128]
    row = lax.broadcasted_iota(jnp.int32, (ROWS, 128), 0)
    for j in range(64):
        at = pl.ds(j * ROWS, ROWS)
        both = keep_ref[at, :] + came_ref[at, :].astype(F32)
        out_ref[at, :] = jnp.where(row >= DOWN2, d_ref[at, :], both).astype(BF16)


def joined(*args):
    return call(
        join_kernel,
        [((64 * ROWS, 128), BF16, pltpu.VMEM)],
        *args,
        scratch=[pltpu.VMEM((66 * ROWS, 128), F32)],
    )[0]


def swapped(one, two):
    count = lax.axis_size("space")
    near = [(i, i ^ 1) for i in range(count)]
    far = [(i, ((i + 1) ^ 1) - 1) for i in range(1, count - 1)]
    two = lax.ppermute(two, "space", far)
    return lax.ppermute(one, "space", near), two


def swapped_two(x, later):
    count = lax.axis_size("space")
    near = [(i, i ^ 2) for i in range(count)]
    away = [(i, ((i + 2) ^ 2) - 2) for i in range(2, count - 2)]
    away = lax.ppermute(x, "space", away)
    return lax.ppermute(later, "space", near), away


def partner(x):
    return lax.ppermute(x, "section", [(0, 1), (1, 0)])


def flat(x, step, rows):
    c = lax.broadcasted_iota(jnp.int32, (128, 128), 0) * step
    lane = lax.broadcasted_iota(jnp.int32, (128, 128), 1)
    x = x.T
    pieces = []
    for k in range(16):
        piece = x[8 * k : 8 * k + 8]
        for part in (step // 2, step - step // 2):
            piece = pltpu.roll(piece, 0, 1, stride=part, stride_axis=0)
        pieces.append(pltpu.roll(piece, 8 * k * step % 128, 1) if 8 * k * step % 128 else piece)
    turned = jnp.concatenate(pieces, axis=0)
    row = lax.broadcasted_iota(jnp.int32, (rows, 128), 0)
    start = lax.broadcasted_iota(jnp.int32, (rows, 128), 1) * step // 128
    exact = functools.partial(jnp.dot, precision=lax.Precision.HIGHEST, preferred_element_type=F32)
    here = lane >= c % 128
    same = exact(jnp.where(row == start, 1.0, 0.0), jnp.where(here, turned, 0.0))
    return same + exact(jnp.where(row == start + 1, 1.0, 0.0), jnp.where(here, 0.0, turned))


def unpack_kernel(sums_ref, two_ref, three_ref, conv_ref, head_ref, x_ref, y_ref, z_ref):
    last = sums_ref[pl.ds(DOWN2 - 1, 1), :]
    for k in range(4):
        head_ref[k] = jnp.sum(jnp.where(lax.broadcasted_iota(jnp.int32, (1, 128), 1) == 96 + k, last, 0.0))
    for ref in (x_ref, y_ref, z_ref):
        ref[...] = jnp.zeros((128, 128), F32)
    x_ref[pl.ds(0, DOWN3), :] = sums_ref[pl.ds(0, DOWN3), :]
    lane = lax.broadcasted_iota(jnp.int32, (7, 128), 1)
    rows = sums_ref[pl.ds(CONV2, 7), :]
    for i in range(4):
        y_ref[pl.ds(i, 7, stride=4), :] = jnp.where(lane < 32, rows if i == 0 else pltpu.roll(rows, 128 - 32 * i, 1), 0.0)
    y_ref[pl.ds(27, 1), :] = jnp.zeros((1, 128), F32)
    lane = lax.broadcasted_iota(jnp.int32, (1, 128), 1)
    for k in range(4):
        row = sums_ref[pl.ds(DOWN3 + k, 1), :]
        at = k // 2 * 4 + k % 2
        z_ref[pl.ds(at, 1), :] = jnp.where(lane < 64, row, 0.0)
        z_ref[pl.ds(at + 2, 1), :] = jnp.where(lane < 64, pltpu.roll(row, 64, 1), 0.0)
    conv_ref[...] = flat(x_ref[...], 27, 32)[:27]
    two_ref[...] = flat(y_ref[...], 27, 8)[:7]
    three_ref[...] = flat(z_ref[...], 8, 8)[:4]


def unpack(sums, came):
    spec = pl.BlockSpec(memory_space=pltpu.VMEM)
    two, three, conv, head = pl.pallas_call(
        unpack_kernel,
        in_specs=[spec],
        out_specs=[spec] * 3 + [pl.BlockSpec(memory_space=pltpu.SMEM)],
        out_shape=[pltpu.HBM((rows, 128), F32) for rows in (7, 4, 27)] + [jax.ShapeDtypeStruct((4,), F32)],
        scratch_shapes=[pltpu.VMEM((128, 128), F32)] * 3,
        compiler_params=params(),
    )(sums)
    return sums[DOWN2] + came[0], two.reshape(-1)[: 27 * 32], three.reshape(-1), conv.reshape(-1), head


def finish(pack):
    terms = lax.all_to_all(pack, "space", 0, 0, tiled=True)
    sums = jnp.sum(terms.astype(F32), axis=0)
    return unpack(sums, partner(sums[DOWN2 + 1 :]))


def per_device(volume, labels, down_weight_two, w_conv_two, down_weight_three, w_conv_three, w_head):
    count = lax.axis_size("space")
    voxels = labels.shape[0] * labels.shape[1] * count * labels.shape[2] * labels.shape[3]
    scale = 1.0 / math.sqrt(voxels)
    sec = lax.axis_index("section").astype(jnp.int32)
    space = lax.axis_index("space").astype(jnp.int32)
    where = jnp.stack([sec, space % 2, space % 4 // 2, jnp.minimum(space, 1), jnp.minimum(count - 1 - space, 1)])

    w1 = down_weight_two.transpose(1, 2, 3, 4, 0).reshape(256, 64)
    wd = down_weight_three.transpose(1, 2, 3, 4, 0).reshape(512, 128)
    w2 = w_conv_two.transpose(2, 3, 4, 0, 1).reshape(27, 64, 64)
    w2 = jnp.concatenate([w2, w2], axis=2)
    w3 = w_conv_three.transpose(2, 3, 4, 0, 1).reshape(27, 128, 128)
    marks = lax.dynamic_slice_in_dim(labels[:, 0], CROPS * sec, CROPS, axis=0)
    marks = marks.transpose(1, 0, 2).reshape(2, 256)

    vp, a2, one, two = first(where, volume, w1)
    a2_one, a2_two = swapped(one, two)
    f2, b2, f3, b3, perm, wd, wh = prepare(w2, w3, wd, w_head.T)
    own = second_own(a2, f2)
    a2_two, a2_one, own = lax.optimization_barrier((a2_two, a2_one, own))
    h2, a3, sent, sides = second(where, a2_one, own, a2_two, f2, wd, marks)
    a3_one, a3_two = swapped(sent, sent)
    a3_one, later = lax.optimization_barrier((a3_one, a3))
    a3_near, a3_away = swapped_two(a3, later)
    own, f3, wh = head_own(a3, f3, wh)
    a3_two, a3_away, a3_one, a3_near, own, f3, wh = lax.optimization_barrier(
        (a3_two, a3_away, a3_one, a3_near, own, f3, wh)
    )
    gz4, gh, gz2, one, two, gy3 = head(
        where, a3_one, a3_two, a3_near, a3_away, own, f3, wh, marks, b3, a3, h2, wd, scale
    )
    gw3, gd3 = weight_three(where, gz4, a3_one, a3, a3_two, gy3, h2)
    gz2_one, gz2_two = swapped(one, two)
    own, slopes = last_own(gz2, b2, a2)
    gw2 = weight_two(gz2, a2, sides)
    keep, send = packed(where, gw3, gd3, gw2, gh)
    gz2_two, gz2_one, send, own, slopes = lax.optimization_barrier((gz2_two, gz2_one, send, own, slopes))
    came = partner(send)
    down = last(where, gz2_one, own, gz2_two, b2, slopes, vp, perm)
    pack = joined(where, down, keep, came)
    return finish(pack.reshape(64, ROWS, 128))


def solution(mesh):
    whole = P(("section", "space"))
    return jax.shard_map(
        per_device,
        mesh=mesh,
        in_specs=(P(None, None, "space", None, None), P(None, "space", None, None), P(), P(), P(), P(), P()),
        out_specs=(whole,) * 5,
        check_vma=False,
    )
```
